256 devices in a mesh: mx: 8 (over z), my: 32 (over x, y, core).
Axes of the slice: x: 4, y: 4, z: 8, core: 2. Of those that a mesh axis runs over, the one named last changes fastest.
Arguments:
- friction: float32 [2048, 4096], P('mx', 'my'), may hold values from 0.5 to 2
- taps_row: float32 [17], replicated, may hold values from 0.03 to 0.09
- taps_col: float32 [17], replicated, may hold values from 0.03 to 0.09
- probe: float32 [2048, 4096], P('mx', 'my'), may hold values from -6 to 6
- win_row: int32 [8, 32, 16], P('mx', 'my'), may hold values from 0 to 223
- win_col: int32 [8, 32, 16], P('mx', 'my'), may hold values from 0 to 95
- live_count: int32 [8, 32], P('mx', 'my'), may hold values from 1 to 16, as said below
Outputs:
- hessian_apply: float32 [2048, 4096], P('mx', 'my')
The draws below stay inside these ranges and needn't reach their ends.
Inputs may be any that keep to these rules, and one draw needn't show every extreme that they name: `live_count`: every tile has at least one live slot; some tile has all 16 live in every draw.
All inputs are finite; a program needn't handle non-finite values.
Results may differ from the reference program's by a relative error of at most 0.0001.
Values sent between devices are 32-bit elements; how exact they have to be, the bound alone decides.
No kernel may reach another device: no remote copies, remote signals or barrier semaphores. Data moves between devices by JAX's collectives and lax.ppermute only.
A program may use at most 64 MiB of HBM per device.

```python
import math
import jax
import jax.numpy as jnp
from jax import lax

TILE_R = 256
TILE_C = 128
SLOTS = 16
PATCH = 64
RADIUS = 8
SWEEPS = 4
GRID_TR = 8
GRID_TC = 32
NR = 2048
NC = 4096
N_MX = 8
N_MY = 32


def draw_live_count(key, part):
    key = jax.random.fold_in(key, 11)
    key_counts, key_full = jax.random.split(key)
    counts = jax.random.randint(key_counts, (GRID_TR * GRID_TC,), 1, SLOTS + 1).astype(jnp.int32)
    chosen = jax.random.randint(key_full, (), 0, GRID_TR * GRID_TC)
    counts = counts.at[chosen].set(SLOTS)
    return counts.reshape(GRID_TR, GRID_TC)


def set_ends(values, own_key, smallest, largest):
    dims = values.shape
    index_at = [jax.random.randint(jax.random.fold_in(own_key, axis), (), 0, dims[axis]) for axis in range(len(dims))]
    values = values.at[tuple(index_at)].set(smallest)
    longest = dims.index(max(dims))
    index_at[longest] = (index_at[longest] + 1) % dims[longest]
    return values.at[tuple(index_at)].set(largest)


def block_levels(own_key, extent, cuts, least, top_value):
    gain = 1.0
    for position, shards_of in cuts:
        heights = jax.random.uniform(jax.random.fold_in(jax.random.fold_in(own_key, 6), position), (shards_of,), jnp.float32, least / len(cuts), top_value / len(cuts))
        gain = gain * jnp.repeat(jnp.exp(heights), extent[position] // shards_of).reshape((-1,) + (1,) * (len(extent) - 1 - position))
    return gain


def centred(own_key, dims, scale, reach, cuts=(), kind=jnp.bfloat16):
    factor_of = block_levels(own_key, dims, cuts, -0.22, 0.18) if cuts else 1.0
    array = jax.random.normal(own_key, dims, jnp.float32) * scale * factor_of
    return jnp.minimum(jnp.maximum(array, -reach), reach).astype(kind)


def setup_inputs(seed: int = 0) -> dict:
    arg_keys = jax.random.split(jax.random.key(seed), 8)
    return {
        "friction": jnp.clip(jnp.exp(math.log(2.0) - 1.3862944 * jax.random.uniform(arg_keys[0], (NR, NC), jnp.float32) ** block_levels(arg_keys[0], (NR, NC), ((0, 8), (1, 32)), -0.2, 0.2)), 0.5, 2.0),
        "taps_row": jnp.clip(jax.random.uniform(arg_keys[1], (2 * RADIUS + 1,), jnp.float32, 0.03, 0.09), 0.03, 0.09),
        "taps_col": jnp.clip(jax.random.uniform(arg_keys[2], (2 * RADIUS + 1,), jnp.float32, 0.03, 0.09), 0.03, 0.09),
        "probe": centred(arg_keys[3], (NR, NC), 1.0, 6.0, ((0, 8), (1, 32)), jnp.float32),
        "win_row": set_ends(jax.random.randint(arg_keys[4], (GRID_TR, GRID_TC, SLOTS), 0, TILE_R - PATCH // 2), jax.random.fold_in(arg_keys[4], 1), 0, (TILE_R - PATCH // 2) - 1).astype(jnp.int32),
        "win_col": set_ends(jax.random.randint(arg_keys[5], (GRID_TR, GRID_TC, SLOTS), 0, TILE_C - PATCH // 2), jax.random.fold_in(arg_keys[5], 1), 0, (TILE_C - PATCH // 2) - 1).astype(jnp.int32),
        "live_count": draw_live_count(jax.random.fold_in(arg_keys[7], 71), 0),
    }


impulse_height = 64.0


def smooth(padded, taps_row, taps_col, out_rows, out_cols):
    width = taps_row.shape[0]
    row_pass = taps_row[0] * padded[:, 0:out_rows, :]
    for offset in range(1, width):
        row_pass = row_pass + taps_row[offset] * padded[:, offset:offset + out_rows, :]
    col_pass = taps_col[0] * row_pass[:, :, 0:out_cols]
    for offset in range(1, width):
        col_pass = col_pass + taps_col[offset] * row_pass[:, :, offset:offset + out_cols]
    return col_pass


def reference(friction, taps_row, taps_col, probe, win_row, win_col, live_count):
    half_patch = PATCH // 2
    size_fft = 2 * PATCH
    rows_total, cols_total = friction.shape
    slot_ids = jnp.arange(SLOTS, dtype=jnp.int32)
    comb_ids = slot_ids % 4
    live_slots = (slot_ids[None, None, :] < live_count[:, :, None]).astype(jnp.float32)
    global_row = (jnp.arange(N_MX, dtype=jnp.int32)[:, None, None] * TILE_R + win_row).astype(jnp.int32)
    global_col = (jnp.arange(N_MY, dtype=jnp.int32)[None, :, None] * TILE_C + win_col).astype(jnp.int32)
    comb_index = jnp.broadcast_to(comb_ids[None, None, :], win_row.shape).astype(jnp.int32)
    response = jnp.zeros((4, rows_total, cols_total), jnp.float32).at[
        comb_index, global_row + half_patch, global_col + half_patch].add(live_slots * impulse_height)
    for sweep_idx in range(SWEEPS):
        padded = jnp.pad(response, ((0, 0), (RADIUS, RADIUS), (RADIUS, RADIUS)))
        response = friction[None] * smooth(padded, taps_row, taps_col, rows_total, cols_total)
    fields = jnp.concatenate([response, probe[None]], 0)
    extended = jnp.pad(fields, ((0, 0), (0, PATCH), (0, PATCH)))
    flat_row = global_row.reshape(N_MX * N_MY, SLOTS)
    flat_col = global_col.reshape(N_MX * N_MY, SLOTS)
    flat_live = live_slots.reshape(N_MX * N_MY, SLOTS)
    span = jnp.arange(size_fft, dtype=jnp.int32)
    probe_ids = jnp.full((SLOTS,), 4, jnp.int32)

    def take_window(layer, top, left):
        return lax.dynamic_slice(extended, (layer, top, left), (1, PATCH, PATCH))[0]

    def add_tile(total, tile_items):
        tops, lefts, lives = tile_items
        kernels = jax.vmap(take_window)(comb_ids, tops, lefts)
        windows = jax.vmap(take_window)(probe_ids, tops, lefts)
        spectra = jnp.fft.rfft2(kernels, s=(size_fft, size_fft)) * jnp.fft.rfft2(windows, s=(size_fft, size_fft))
        patches = jnp.fft.irfft2(spectra, s=(size_fft, size_fft)) * lives[:, None, None]
        row_index = tops[:, None, None] + span[None, :, None]
        col_index = lefts[:, None, None] + span[None, None, :]
        return total.at[row_index, col_index].add(patches.astype(total.dtype)), None

    total = jnp.zeros((rows_total + size_fft, cols_total + size_fft), jnp.float32)
    total, _ = lax.scan(add_tile, total, (flat_row, flat_col, flat_live))
    return total[:rows_total, :cols_total]
```

```python
import ml_dtypes
import numpy as np

import jax
import jax.numpy as jnp
from jax import lax
from jax.experimental import pallas as pl
from jax.experimental.pallas import tpu as pltpu
from jax.sharding import PartitionSpec as P

SLOTS = 16
PATCH = 64
TILE_R = 256
LANES = 128
UP = 32
DOWN = 64
EXT_F = UP + TILE_R + DOWN
EXT_P = TILE_R + 32
OUT_R = TILE_R + 96
DEAD = -1.0e6
BF = jnp.bfloat16
F32 = jnp.float32
VMEM = pl.BlockSpec(memory_space=pltpu.VMEM)
SMEM = pl.BlockSpec(memory_space=pltpu.SMEM)


def split(x):
    hi = x.astype(BF)
    return hi, (x - hi.astype(F32)).astype(BF)


def dot(a, b):
    return jnp.dot(a, b, preferred_element_type=F32)


def halves(x, axis):
    n = x.shape[axis] // 2
    return lax.slice_in_dim(x, 0, n, axis=axis) + lax.slice_in_dim(x, n, 2 * n, axis=axis)


def np_split(x):
    hi = x.astype(ml_dtypes.bfloat16)
    return hi, (x - hi.astype(np.float64)).astype(ml_dtypes.bfloat16)


def transform_tables():
    theta = np.pi * (2 * np.arange(64) + 1) / 128
    short = np.outer(np.arange(64), theta)
    forward = np.concatenate([np.cos(short), np.sin(short)], 1)
    wide = np.zeros((128, 128))
    wide[32:96] = forward
    full = np.outer(theta, np.arange(128))
    inverse = np.concatenate([np.cos(full), np.sin(full)], 0) / 64
    hi, lo = np_split(wide)
    lane_fwd = np.block([[hi, lo], [hi, lo]])
    hi, lo = np_split(forward.T)
    row_fwd = np.block([[hi, hi], [lo, lo]])
    hi, lo = np_split(inverse)
    lane_inv = np.block([[hi, lo], [hi, lo]])
    hi, lo = np_split(inverse.T)
    row_inv = np.block([[hi, hi], [lo, lo]])
    return lane_fwd, row_fwd, lane_inv, row_inv


def bands_kernel(taps_row, taps_col, row_out, col_out):
    gap = lax.broadcasted_iota(jnp.int32, (112, 128), 1) - lax.broadcasted_iota(jnp.int32, (112, 128), 0)
    band = jnp.zeros((112, 128), F32)
    for t in range(17):
        band = jnp.where(gap == t, taps_row[t], band)
    hi, lo = split(band)
    row_out[0:112, :] = hi
    row_out[112:224, :] = lo
    gap = lax.broadcasted_iota(jnp.int32, (128, 128), 0) - lax.broadcasted_iota(jnp.int32, (128, 128), 1) + 8
    band = jnp.zeros((128, 128), F32)
    for t in range(17):
        band = jnp.where(gap == t, taps_col[t], band)
    hi, lo = split(band)
    pair = jnp.concatenate([hi, lo], 1)
    col_out[...] = jnp.concatenate([pair, pair], 0)


def info_block(win_row, win_col, live_count):
    sub = lax.broadcasted_iota(jnp.int32, (8, LANES), 0)
    lane = lax.broadcasted_iota(jnp.int32, (8, LANES), 1)
    block = jnp.full((8, LANES), DEAD, F32)
    live = live_count[0, 0]
    for k in range(SLOTS):
        half, m = (k % 4) // 2, 2 * (k // 4) + k % 2
        row = jnp.where(k < live, win_row[0, 0, k].astype(F32), DEAD)
        block = jnp.where((sub == half) & (lane == m), row, block)
        block = jnp.where((sub == half + 2) & (lane == m), win_col[0, 0, k].astype(F32), block)
    return block


def pack_rows_kernel(win_row, win_col, live_count, friction, probe, down, up):
    info = info_block(win_row, win_col, live_count)
    down[0:UP, :] = friction[TILE_R - UP : TILE_R, :]
    down[UP : UP + 8, :] = info
    up[0:DOWN, :] = friction[0:DOWN, :]
    up[DOWN : DOWN + 32, :] = probe[0:32, :]
    up[DOWN + 32 : DOWN + 40, :] = info


def pack_cols_kernel(edges, win_row, win_col, live_count, friction, probe, above, below, fa, pa, right, left):
    top, bottom = edges[0] == 0, edges[0] == edges[2] - 1
    info = info_block(win_row, win_col, live_count)
    fa[0:UP, :] = jnp.where(top, 0.0, above[0:UP, :])
    fa[UP : UP + TILE_R, :] = friction[...]
    fa[UP + TILE_R : EXT_F, :] = jnp.where(bottom, 0.0, below[0:DOWN, :])
    pa[0:TILE_R, :] = probe[...]
    pa[TILE_R:EXT_P, :] = jnp.where(bottom, 0.0, below[DOWN : DOWN + 32, :])
    infos = (
        info,
        jnp.where(top, DEAD, above[UP : UP + 8, :]),
        jnp.where(bottom, DEAD, below[DOWN + 32 : DOWN + 40, :]),
    )

    def packed(ref, rows, width, start):
        count = LANES // width
        part = rows // count
        lane = lax.broadcasted_iota(jnp.int32, (part, LANES), 1) // width
        total = jnp.zeros((part, LANES), F32)
        for i in range(count):
            piece = pltpu.roll(ref[i * part : (i + 1) * part, :], (width * i - start) % LANES, 1)
            total = jnp.where(lane == i, piece, total)
        return total

    right[0:88, :] = packed(fa, EXT_F, 32, 96)
    left[0:176, :] = packed(fa, EXT_F, 64, 0)
    left[176:248, :] = packed(pa, EXT_P, 32, 0)
    for n, block in enumerate(infos):
        right[88 + 8 * n : 96 + 8 * n, :] = block
        left[248 + 8 * n : 256 + 8 * n, :] = block


def window(a, b, start):
    turn = lax.rem(256 - start, 128)
    lane = lax.broadcasted_iota(jnp.int32, a.shape, 1) + start
    return jnp.where((lane >= 0) & (lane < LANES), pltpu.roll(a, turn, 1), pltpu.roll(b, turn, 1))


def core_kernel(
    edges, win_row, win_col, live_count, fa, pa, above, below, from_left, from_right, bands, col_band,
    lane_fwd, row_fwd, lane_inv, row_inv, oa, ob, fb, pb, fw, y2, z,
):
    top, bottom = edges[0] == 0, edges[0] == edges[2] - 1
    leftmost, rightmost = edges[1] == 0, edges[1] == edges[3] - 1
    lane = lax.broadcasted_iota(jnp.int32, (8, LANES), 1)
    for i in range(4):
        rows = slice(88 * i, 88 * i + 88)
        rim = pltpu.roll(from_left[0:88, :], 96 - 32 * i, 1)
        lane88 = lax.broadcasted_iota(jnp.int32, (88, LANES), 1)
        near = from_right[88 * (i % 2) : 88 * (i % 2) + 88, :]
        if i >= 2:
            near = pltpu.roll(near, 64, 1)
        keep_l = (lane88 >= 96) & jnp.logical_not(leftmost)
        keep_r = (lane88 < 64) & jnp.logical_not(rightmost)
        fb[rows, :] = jnp.where(keep_l, rim, jnp.where(keep_r, near, 0.0))
        lane72 = lax.broadcasted_iota(jnp.int32, (72, LANES), 1)
        near = pltpu.roll(from_right[176:248, :], (128 - 32 * i) % 128, 1)
        pb[72 * i : 72 * i + 72, :] = jnp.where((lane72 < 32) & jnp.logical_not(rightmost), near, 0.0)
    sub = lax.broadcasted_iota(jnp.int32, (8, LANES), 0)
    is_row = sub < 2
    cand = jnp.full((8, LANES), DEAD, F32)
    tile = 0
    for dc, mine in ((0, None), (-1, from_left), (1, from_right)):
        for n, dr in enumerate((0, -1, 1)):
            if dc == 0:
                if dr == 0:
                    block = info_block(win_row, win_col, live_count)
                elif dr == -1:
                    block = jnp.where(top, DEAD, above[UP : UP + 8, :])
                else:
                    block = jnp.where(bottom, DEAD, below[DOWN + 32 : DOWN + 40, :])
            elif dc == -1:
                block = jnp.where(leftmost, DEAD, from_left[88 + 8 * n : 96 + 8 * n, :])
            else:
                block = jnp.where(rightmost, DEAD, from_right[248 + 8 * n : 256 + 8 * n, :])
            block = block + jnp.where(is_row, float(TILE_R * dr), float(LANES * dc))
            cand = jnp.where(lane // 8 == tile, pltpu.roll(block, 8 * tile, 1), cand)
            tile += 1
    for k in range(SLOTS):
        rows = pl.ds(win_row[0, 0, k], 128)
        fw[k] = window(fa[rows, :], fb[rows, :], win_col[0, 0, k] - 32)
    sub_f = lax.broadcasted_iota(jnp.int32, (128, 128), 0).astype(F32)
    lane1 = lax.broadcasted_iota(jnp.int32, (1, LANES), 1)
    for k in range(0, SLOTS, 2):
        combs = []
        for kk in (k, k + 1):
            half = (kk % 4) // 2
            mine = lax.rem(lane1, 2) == kk % 2
            p = jnp.where(mine, cand[half : half + 1] - (win_row[0, 0, kk] - 64).astype(F32), -1.0)
            q = jnp.where(mine, cand[half + 2 : half + 3] - (win_col[0, 0, kk] - 64).astype(F32), -1.0)
            at_row = (sub_f == p).astype(F32).astype(BF)
            at_col = jnp.where(sub_f == q, 64.0, 0.0).astype(BF)
            comb = lax.dot_general(at_row, at_col, (((1,), (1,)), ((), ())), preferred_element_type=F32)
            combs.append(comb.astype(BF))
        t = halves(dot(bands[...], jnp.concatenate(combs, 1)), 0)
        for m in range(2):
            hi, lo = split(t[:, 128 * m : 128 * m + 128])
            y2[pl.ds((k + m) * 112, 112), :] = jnp.concatenate([hi, lo], 1)
    first, n = 8, 112
    while True:
        o = halves(dot(y2[0 : SLOTS * n, :], col_band[...]), 1)
        o = o.reshape(SLOTS, n, 128) * fw[:, first : first + n, :]
        if n == PATCH:
            break
        hi, lo = split(o)
        both = jnp.concatenate([hi, lo], 1)
        m = n - 16
        band_hi, band_lo = bands[0:m, 0:n], bands[112 : 112 + m, 0:n]
        lhs = jnp.concatenate(
            [jnp.concatenate([band_hi, band_hi], 1), jnp.concatenate([band_lo, band_lo], 1)], 0
        )
        for k in range(0, SLOTS, 2):
            t = halves(dot(lhs, jnp.concatenate([both[k], both[k + 1]], 1)), 0)
            for i in range(2):
                hi, lo = split(t[:, 128 * i : 128 * i + 128])
                y2[pl.ds((k + i) * m, m), :] = jnp.concatenate([hi, lo], 1)
        first, n = first + 8, m

    def lane_transform(x):
        hi, lo = split(x)
        return split(halves(dot(jnp.concatenate([hi, lo], 1), lane_fwd[...]), 1))

    ker_hi, ker_lo = lane_transform(o.reshape(SLOTS * PATCH, 128))
    for k in range(SLOTS):
        rows = pl.ds(win_row[0, 0, k], PATCH)
        z[pl.ds(k * PATCH, PATCH), :] = window(pa[rows, :], pb[rows, :], win_col[0, 0, k] - 32)
    win_hi, win_lo = lane_transform(z[...])
    left_half = lax.broadcasted_iota(jnp.int32, (PATCH, 128), 1) < 64
    sign = jnp.where(left_half, -1.0, 1.0)

    def pair(t):
        a, b = t[:64], pltpu.roll(t[64:], 64, 1) * sign
        return a + b, a - b

    def times(a, b):
        ar, br = pltpu.roll(a, 64, 1), pltpu.roll(b, 64, 1)
        return jnp.where(left_half, a, ar) * b + jnp.where(left_half, -ar, a) * br

    def spectrum(k):
        s = slice(PATCH * k, PATCH * k + PATCH)
        w = jnp.concatenate(
            [jnp.concatenate([ker_hi[s], win_hi[s]], 1), jnp.concatenate([ker_lo[s], win_lo[s]], 1)], 0
        )
        t = halves(dot(row_fwd[...], w), 0)
        k1, k2 = pair(t[:, :128])
        w1, w2 = pair(t[:, 128:])
        p1, p2 = times(k1, w1), times(k2, w2)
        return jnp.concatenate([(p1 + p2) * 0.5, pltpu.roll((p1 - p2) * (0.5 * sign), 64, 1)], 0)

    oa[...] = jnp.zeros_like(oa)
    ob[...] = jnp.zeros_like(ob)
    lane128 = lax.broadcasted_iota(jnp.int32, (128, 128), 1)
    for k in range(0, SLOTS, 2):
        hi, lo = split(jnp.concatenate([spectrum(k), spectrum(k + 1)], 0))
        e = halves(dot(jnp.concatenate([hi, lo], 1), lane_inv[...]), 1)
        hi, lo = split(e)
        w = jnp.concatenate(
            [jnp.concatenate([hi[:128], lo[:128]], 0), jnp.concatenate([hi[128:], lo[128:]], 0)], 1
        )
        t = halves(dot(row_inv[...], w), 0)
        for m in range(2):
            kk = k + m
            col = win_col[0, 0, kk]
            live = jnp.where(kk < live_count[0, 0], 1.0, 0.0)
            patch = pltpu.roll(t[:, 128 * m : 128 * m + 128] * live, col, 1)
            rows = pl.ds(win_row[0, 0, kk], 128)
            oa[rows, :] += jnp.where(lane128 >= col, patch, 0.0)
            ob[rows, :] += jnp.where(lane128 < col, patch, 0.0)


def shape(rows, dtype=F32, cols=LANES):
    return jax.ShapeDtypeStruct((rows, cols), dtype)


def ring(x, axis, by):
    count = lax.axis_size(axis)
    return lax.ppermute(x, axis, [(i, (i + by) % count) for i in range(count)])


def per_device(friction, taps_row, taps_col, probe, win_row, win_col, live_count):
    params = pltpu.CompilerParams(vmem_limit_bytes=40 * 2**20)
    edges = jnp.stack(
        [lax.axis_index("mx"), lax.axis_index("my"), lax.axis_size("mx"), lax.axis_size("my")]
    ).astype(jnp.int32)
    down, up = pl.pallas_call(
        pack_rows_kernel,
        out_shape=[shape(UP + 8), shape(DOWN + 40)],
        in_specs=[SMEM] * 3 + [VMEM] * 2,
        out_specs=[VMEM] * 2,
        compiler_params=params,
    )(win_row, win_col, live_count, friction, probe)
    above = ring(down, "mx", 1)
    below = ring(up, "mx", -1)
    bands, col_band = pl.pallas_call(
        bands_kernel,
        out_shape=[shape(224, BF), shape(256, BF, 256)],
        in_specs=[SMEM] * 2,
        out_specs=[VMEM] * 2,
        compiler_params=params,
    )(taps_row, taps_col)
    fa, pa, right, left = pl.pallas_call(
        pack_cols_kernel,
        out_shape=[shape(EXT_F), shape(EXT_P), shape(112), shape(272)],
        in_specs=[SMEM] * 4 + [VMEM] * 4,
        out_specs=[VMEM] * 4,
        compiler_params=params,
    )(edges, win_row, win_col, live_count, friction, probe, above, below)
    from_left = ring(right, "my", 1)
    from_right = ring(left, "my", -1)
    tables = [jnp.asarray(t) for t in transform_tables()]
    oa, ob = pl.pallas_call(
        core_kernel,
        out_shape=[shape(OUT_R)] * 2,
        in_specs=[SMEM] * 4 + [VMEM] * 12,
        out_specs=[VMEM] * 2,
        scratch_shapes=[
            pltpu.VMEM((EXT_F, LANES), F32),
            pltpu.VMEM((EXT_P, LANES), F32),
            pltpu.VMEM((SLOTS, 128, LANES), F32),
            pltpu.VMEM((SLOTS * 112, 256), BF),
            pltpu.VMEM((SLOTS * PATCH, LANES), F32),
        ],
        compiler_params=params,
    )(
        edges, win_row, win_col, live_count, fa, pa, above, below, from_left, from_right, bands, col_band, *tables
    )
    spill = ring(ob, "my", 1)
    total = oa + jnp.where(lax.axis_index("my") > 0, spill, 0.0)
    lower = ring(total[TILE_R:], "mx", 1)
    lower = jnp.where(lax.axis_index("mx") > 0, lower, 0.0)
    return total[:TILE_R] + jnp.pad(lower, ((0, TILE_R - lower.shape[0]), (0, 0)))


def solution(mesh):
    placed = (
        P("mx", "my"),
        P(),
        P(),
        P("mx", "my"),
        P("mx", "my", None),
        P("mx", "my", None),
        P("mx", "my"),
    )
    return jax.shard_map(
        per_device, mesh=mesh, in_specs=placed, out_specs=P("mx", "my"), check_vma=False
    )
```

```python
import ml_dtypes
import numpy as np

import jax
import jax.numpy as jnp
from jax import lax
from jax.experimental import pallas as pl
from jax.experimental.pallas import tpu as pltpu
from jax.sharding import PartitionSpec as P

SLOTS = 16
PATCH = 64
TILE_R = 256
LANES = 128
UP = 32
DOWN = 64
EXT_F = UP + TILE_R + DOWN
EXT_P = TILE_R + 32
OUT_R = TILE_R + 96
DEAD = -1.0e6
BF = jnp.bfloat16
F32 = jnp.float32
VMEM = pl.BlockSpec(memory_space=pltpu.VMEM)
SMEM = pl.BlockSpec(memory_space=pltpu.SMEM)
ANY = pl.BlockSpec(memory_space=pltpu.HBM)


def split(x):
    hi = x.astype(BF)
    return hi, (x - hi.astype(F32)).astype(BF)


def dot(a, b):
    return jnp.dot(a, b, preferred_element_type=F32)


def halves(x, axis):
    n = x.shape[axis] // 2
    return lax.slice_in_dim(x, 0, n, axis=axis) + lax.slice_in_dim(x, n, 2 * n, axis=axis)


def np_split(x):
    hi = x.astype(ml_dtypes.bfloat16)
    return hi, (x - hi.astype(np.float64)).astype(ml_dtypes.bfloat16)


def transform_tables():
    theta = np.pi * (2 * np.arange(64) + 1) / 128
    short = np.outer(np.arange(64), theta)
    forward = np.concatenate([np.cos(short), np.sin(short)], 1)
    wide = np.zeros((128, 128))
    wide[32:96] = forward
    full = np.outer(theta, np.arange(128))
    inverse = np.concatenate([np.cos(full), np.sin(full)], 0) / 64
    hi, lo = np_split(wide)
    lane_fwd = np.block([[hi, lo], [hi, lo]])
    hi, lo = np_split(forward.T)
    row_fwd = np.block([[hi, hi], [lo, lo]])
    hi, lo = np_split(inverse)
    lane_inv = np.block([[hi, lo], [hi, lo]])
    hi, lo = np_split(inverse.T)
    row_inv = np.block([[hi, hi], [lo, lo]])
    return np.concatenate([lane_fwd, lane_inv, row_inv, row_fwd], 1)


def bands_kernel(taps_row, taps_col, tables_in, row_out, col_out, tables, sem):
    table_copy = pltpu.make_async_copy(tables_in, tables, sem)
    table_copy.start()
    gap = lax.broadcasted_iota(jnp.int32, (112, 128), 1) - lax.broadcasted_iota(jnp.int32, (112, 128), 0)
    band = jnp.zeros((112, 128), F32)
    for t in range(17):
        band = jnp.where(gap == t, taps_row[t], band)
    hi, lo = split(band)
    row_out[0:112, :] = hi
    row_out[112:224, :] = lo
    gap = lax.broadcasted_iota(jnp.int32, (128, 128), 0) - lax.broadcasted_iota(jnp.int32, (128, 128), 1) + 8
    band = jnp.zeros((128, 128), F32)
    for t in range(17):
        band = jnp.where(gap == t, taps_col[t], band)
    hi, lo = split(band)
    pair = jnp.concatenate([hi, lo], 1)
    col_out[...] = jnp.concatenate([pair, pair], 0)
    table_copy.wait()


def own_index(axis):
    return lax.axis_index(axis), lax.axis_size(axis)


def pack_rows_kernel(win_row, win_col, live_count, friction, probe, even_out, odd_out, rows, cols, count, sems):
    def fetch(down, up):
        return [
            pltpu.make_async_copy(friction.at[pl.ds(TILE_R - UP, UP)], down.at[pl.ds(0, UP)], sems.at[3]),
            pltpu.make_async_copy(friction.at[pl.ds(0, DOWN)], up.at[pl.ds(0, DOWN)], sems.at[4]),
            pltpu.make_async_copy(probe.at[pl.ds(0, 32)], up.at[pl.ds(DOWN, 32)], sems.at[5]),
        ]

    is_even = lax.rem(lax.axis_index("mx"), 2) == 0

    @pl.when(is_even)
    def _():
        for copy in fetch(even_out, odd_out):
            copy.start()

    @pl.when(jnp.logical_not(is_even))
    def _():
        for copy in fetch(odd_out, even_out):
            copy.start()

    copies = [
        pltpu.make_async_copy(win_row.at[0], rows, sems.at[0]),
        pltpu.make_async_copy(win_col.at[0], cols, sems.at[1]),
        pltpu.make_async_copy(live_count, count, sems.at[2]),
    ]
    for copy in copies:
        copy.start()
    for copy in copies:
        copy.wait()
    lane = lax.broadcasted_iota(jnp.int32, (1, SLOTS), 1)
    live = lane < count[...]
    row = jnp.where(live, rows[...].astype(F32), DEAD)
    col = cols[...].astype(F32)
    wide = jnp.concatenate([jnp.concatenate([x, jnp.zeros((1, LANES - SLOTS), F32)], 1) for x in (row, col)], 0)
    turned = pltpu.roll(wide, LANES - 2, 1)
    info = jnp.concatenate([wide[0:1], turned[0:1], wide[1:2], turned[1:2], jnp.zeros((4, LANES), F32)], 0)
    even_out[96:104, :] = info
    odd_out[96:104, :] = info
    for copy in fetch(even_out, odd_out):
        copy.wait()


def pack_cols_kernel(friction, probe, mine, row_even, row_odd, fa, pa, infos, even_out, odd_out):
    at, count = own_index("mx")
    top, bottom = at == 0, at == count - 1
    is_even = lax.rem(at, 2) == 0
    above = jnp.where(is_even, row_odd[...], row_even[...])
    below = jnp.where(is_even, row_even[...], row_odd[...])
    fa[0:UP, :] = jnp.where(top, 0.0, above[0:UP])
    fa[UP : UP + TILE_R, :] = friction[...]
    fa[UP + TILE_R : EXT_F, :] = jnp.where(bottom, 0.0, below[0:DOWN])
    pa[0:TILE_R, :] = probe[...]
    pa[TILE_R:EXT_P, :] = jnp.where(bottom, 0.0, below[DOWN : DOWN + 32])
    infos[0:8, :] = mine[96:104, :]
    infos[8:16, :] = jnp.where(top, DEAD, above[96:104])
    infos[16:24, :] = jnp.where(bottom, DEAD, below[96:104])

    def packed(ref, rows, width, start):
        count = LANES // width
        part = rows // count
        lane = lax.broadcasted_iota(jnp.int32, (part, LANES), 1) // width
        total = jnp.zeros((part, LANES), F32)
        for i in range(count):
            piece = pltpu.roll(ref[i * part : (i + 1) * part, :], (width * i - start) % LANES, 1)
            total = jnp.where(lane == i, piece, total)
        return total

    def fill(right, left):
        right[0:88, :] = packed(fa, EXT_F, 32, 96)
        left[0:176, :] = packed(fa, EXT_F, 64, 0)
        left[176:248, :] = packed(pa, EXT_P, 32, 0)
        right[248:272, :] = infos[...]
        left[248:272, :] = infos[...]

    is_even = lax.rem(lax.axis_index("my"), 2) == 0

    @pl.when(is_even)
    def _():
        fill(even_out, odd_out)

    @pl.when(jnp.logical_not(is_even))
    def _():
        fill(odd_out, even_out)


def window(a, b, start):
    turn = lax.rem(256 - start, 128)
    lane = lax.broadcasted_iota(jnp.int32, a.shape, 1) + start
    return jnp.where((lane >= 0) & (lane < LANES), pltpu.roll(a, turn, 1), pltpu.roll(b, turn, 1))


def core_kernel(
    win_row_in, win_col_in, live_in, fa, pa, infos, even_in, odd_in, bands, col_band, tables,
    oa, ob, fb, pb, fw, y2, z, win_row, win_col, live_count, from_left, from_right, sems,
):
    scalar_copies = [
        pltpu.make_async_copy(win_row_in, win_row, sems.at[1]),
        pltpu.make_async_copy(win_col_in, win_col, sems.at[2]),
        pltpu.make_async_copy(live_in, live_count, sems.at[3]),
    ]
    for copy in scalar_copies:
        copy.start()
    at_col, col_count = own_index("my")
    leftmost, rightmost = at_col == 0, at_col == col_count - 1
    is_even = lax.rem(at_col, 2) == 0
    from_left[...] = jnp.where(is_even, odd_in[...], even_in[...])
    from_right[...] = jnp.where(is_even, even_in[...], odd_in[...])
    lane = lax.broadcasted_iota(jnp.int32, (8, LANES), 1)
    for i in range(4):
        rows = slice(88 * i, 88 * i + 88)
        rim = pltpu.roll(from_left[0:88, :], 96 - 32 * i, 1)
        lane88 = lax.broadcasted_iota(jnp.int32, (88, LANES), 1)
        near = from_right[88 * (i % 2) : 88 * (i % 2) + 88, :]
        if i >= 2:
            near = pltpu.roll(near, 64, 1)
        keep_l = (lane88 >= 96) & jnp.logical_not(leftmost)
        keep_r = (lane88 < 64) & jnp.logical_not(rightmost)
        fb[rows, :] = jnp.where(keep_l, rim, jnp.where(keep_r, near, 0.0))
        lane72 = lax.broadcasted_iota(jnp.int32, (72, LANES), 1)
        near = pltpu.roll(from_right[176:248, :], (128 - 32 * i) % 128, 1)
        pb[72 * i : 72 * i + 72, :] = jnp.where((lane72 < 32) & jnp.logical_not(rightmost), near, 0.0)
    is_row = lax.broadcasted_iota(jnp.int32, (8, LANES), 0) < 2
    cand = jnp.full((8, LANES), DEAD, F32)
    tile = 0
    for dc in (0, -1, 1):
        for n, dr in enumerate((0, -1, 1)):
            if dc == 0:
                block = infos[8 * n : 8 * n + 8, :]
            elif dc == -1:
                block = jnp.where(leftmost, DEAD, from_left[248 + 8 * n : 256 + 8 * n, :])
            else:
                block = jnp.where(rightmost, DEAD, from_right[248 + 8 * n : 256 + 8 * n, :])
            block = block + jnp.where(is_row, float(TILE_R * dr), float(LANES * dc))
            here = (lane // 16 == tile // 2) & (lax.rem(lane, 4) // 2 == tile % 2)
            cand = jnp.where(here, pltpu.roll(block, 16 * (tile // 2) + 2 * (tile % 2), 1), cand)
            tile += 1
    for copy in scalar_copies:
        copy.wait()
    for k in range(SLOTS):
        rows = pl.ds(win_row[0, 0, k], 128)
        fw[k] = window(fa[rows, :], fb[rows, :], win_col[0, 0, k] - 32)
    sub_f = lax.broadcasted_iota(jnp.int32, (128, 128), 0).astype(F32)
    lane1 = lax.broadcasted_iota(jnp.int32, (1, LANES), 1)
    for k in range(0, SLOTS, 2):
        combs = []
        for kk in (k, k + 1):
            half = (kk % 4) // 2
            mine = lax.rem(lane1, 2) == kk % 2
            p = jnp.where(mine, cand[half : half + 1] - (win_row[0, 0, kk] - 64).astype(F32), -1.0)
            q = jnp.where(mine, cand[half + 2 : half + 3] - (win_col[0, 0, kk] - 64).astype(F32), -1.0)
            at_row = (sub_f == p).astype(F32).astype(BF)
            at_col = jnp.where(sub_f == q, 64.0, 0.0).astype(BF)
            comb = lax.dot_general(at_row, at_col, (((1,), (1,)), ((), ())), preferred_element_type=F32)
            combs.append(comb.astype(BF))
        t = halves(dot(bands[...], jnp.concatenate(combs, 1)), 0)
        for m in range(2):
            hi, lo = split(t[:, 128 * m : 128 * m + 128])
            y2[pl.ds((k + m) * 112, 112), :] = jnp.concatenate([hi, lo], 1)
    first, n = 8, 112
    while True:
        o = halves(dot(y2[0 : SLOTS * n, :], col_band[...]), 1)
        o = o.reshape(SLOTS, n, 128) * fw[:, first : first + n, :]
        if n == PATCH:
            break
        hi, lo = split(o)
        both = jnp.concatenate([hi, lo], 1)
        m = n - 16
        band_hi, band_lo = bands[0:m, 0:n], bands[112 : 112 + m, 0:n]
        lhs = jnp.concatenate(
            [jnp.concatenate([band_hi, band_hi], 1), jnp.concatenate([band_lo, band_lo], 1)], 0
        )
        for k in range(0, SLOTS, 2):
            t = halves(dot(lhs, jnp.concatenate([both[k], both[k + 1]], 1)), 0)
            for i in range(2):
                hi, lo = split(t[:, 128 * i : 128 * i + 128])
                y2[pl.ds((k + i) * m, m), :] = jnp.concatenate([hi, lo], 1)
        first, n = first + 8, m

    def lane_transform(x):
        hi, lo = split(x)
        return split(halves(dot(jnp.concatenate([hi, lo], 1), tables[:, 0:256]), 1))

    ker_hi, ker_lo = lane_transform(o.reshape(SLOTS * PATCH, 128))
    for k in range(SLOTS):
        rows = pl.ds(win_row[0, 0, k], PATCH)
        z[pl.ds(k * PATCH, PATCH), :] = window(pa[rows, :], pb[rows, :], win_col[0, 0, k] - 32)
    win_hi, win_lo = lane_transform(z[...])
    left_half = lax.broadcasted_iota(jnp.int32, (PATCH, 128), 1) < 64
    sign = jnp.where(left_half, -1.0, 1.0)

    def pair(t):
        a, b = t[:64], pltpu.roll(t[64:], 64, 1) * sign
        return a + b, a - b

    def times(a, b):
        ar, br = pltpu.roll(a, 64, 1), pltpu.roll(b, 64, 1)
        return jnp.where(left_half, a, ar) * b + jnp.where(left_half, -ar, a) * br

    def spectrum(k):
        s = slice(PATCH * k, PATCH * k + PATCH)
        w = jnp.concatenate(
            [jnp.concatenate([ker_hi[s], win_hi[s]], 1), jnp.concatenate([ker_lo[s], win_lo[s]], 1)], 0
        )
        t = halves(dot(tables[:, 768:896], w), 0)
        k1, k2 = pair(t[:, :128])
        w1, w2 = pair(t[:, 128:])
        p1, p2 = times(k1, w1), times(k2, w2)
        return jnp.concatenate([(p1 + p2) * 0.5, pltpu.roll((p1 - p2) * (0.5 * sign), 64, 1)], 0)

    oa[...] = jnp.zeros_like(oa)
    ob[...] = jnp.zeros_like(ob)
    lane128 = lax.broadcasted_iota(jnp.int32, (128, 128), 1)
    for k in range(0, SLOTS, 2):
        hi, lo = split(jnp.concatenate([spectrum(k), spectrum(k + 1)], 0))
        e = halves(dot(jnp.concatenate([hi, lo], 1), tables[:, 256:512]), 1)
        hi, lo = split(e)
        w = jnp.concatenate(
            [jnp.concatenate([hi[:128], lo[:128]], 0), jnp.concatenate([hi[128:], lo[128:]], 0)], 1
        )
        t = halves(dot(tables[:, 512:768], w), 0)
        for m in range(2):
            kk = k + m
            col = win_col[0, 0, kk]
            live = jnp.where(kk < live_count[0, 0], 1.0, 0.0)
            patch = pltpu.roll(t[:, 128 * m : 128 * m + 128] * live, col, 1)
            rows = pl.ds(win_row[0, 0, kk], 128)
            oa[rows, :] += jnp.where(lane128 >= col, patch, 0.0)
            ob[rows, :] += jnp.where(lane128 < col, patch, 0.0)


def shape(rows, dtype=F32, cols=LANES):
    return jax.ShapeDtypeStruct((rows, cols), dtype)


def ring(x, axis, by):
    count = lax.axis_size(axis)
    return lax.ppermute(x, axis, [(i, (i + by) % count) for i in range(count)])


def swap(x, axis, odd):
    rows, cols = lax.axis_size("mx"), lax.axis_size("my")
    pairs = []
    for i in range(rows):
        for j in range(cols):
            if axis == "my":
                k = ((j + 1) ^ 1) - 1 if odd else j ^ 1
                to = (i, k) if 0 <= k < cols else (i ^ 1, j)
            else:
                k = ((i + 1) ^ 1) - 1 if odd else i ^ 1
                to = (k, j) if 0 <= k < rows else (i, j ^ 1)
            pairs.append((i * cols + j, to[0] * cols + to[1]))
    return lax.ppermute(x, ("mx", "my"), pairs)


def diagonal(x):
    rows, cols = lax.axis_size("mx"), lax.axis_size("my")
    pairs = [(i * cols + j, (i + 1) % rows * cols + (j + 1) % cols) for i in range(rows) for j in range(cols)]
    return lax.ppermute(x, ("mx", "my"), pairs)


def core_call(win_row, win_col, live_count, fa, pa, infos, even_in, odd_in, bands, col_band, tables):
    return pl.pallas_call(
        core_kernel,
        out_shape=[shape(OUT_R)] * 2,
        in_specs=[ANY] * 3 + [VMEM] * 8,
        out_specs=[VMEM] * 2,
        scratch_shapes=[
            pltpu.VMEM((EXT_F, LANES), F32),
            pltpu.VMEM((EXT_P, LANES), F32),
            pltpu.VMEM((SLOTS, 128, LANES), F32),
            pltpu.VMEM((SLOTS * 112, 256), BF),
            pltpu.VMEM((SLOTS * PATCH, LANES), F32),
            pltpu.SMEM((1, 1, SLOTS), jnp.int32),
            pltpu.SMEM((1, 1, SLOTS), jnp.int32),
            pltpu.SMEM((1, 1), jnp.int32),
            pltpu.VMEM((272, LANES), F32),
            pltpu.VMEM((272, LANES), F32),
            pltpu.SemaphoreType.DMA((4,)),
        ],
        compiler_params=pltpu.CompilerParams(vmem_limit_bytes=40 * 2**20),
    )(
        win_row, win_col, live_count, fa, pa, infos, even_in, odd_in, bands, col_band, tables,
    )


def per_device(friction, taps_row, taps_col, probe, win_row, win_col, live_count):
    params = pltpu.CompilerParams(vmem_limit_bytes=40 * 2**20)
    row_even_out, row_odd_out = pl.pallas_call(
        pack_rows_kernel,
        out_shape=[shape(104), shape(104)],
        in_specs=[ANY] * 5,
        out_specs=[VMEM] * 2,
        scratch_shapes=[
            pltpu.VMEM((1, SLOTS), jnp.int32),
            pltpu.VMEM((1, SLOTS), jnp.int32),
            pltpu.VMEM((1, 1), jnp.int32),
            pltpu.SemaphoreType.DMA((6,)),
        ],
        compiler_params=pltpu.CompilerParams(vmem_limit_bytes=40 * 2**20),
    )(win_row, win_col, live_count, friction, probe)
    row_odd = swap(row_odd_out, "mx", True)
    row_even = swap(row_even_out, "mx", False)
    bands, col_band, tables = pl.pallas_call(
        bands_kernel,
        out_shape=[shape(224, BF), shape(256, BF, 256), shape(256, BF, 896)],
        in_specs=[SMEM] * 2 + [ANY],
        out_specs=[VMEM] * 3,
        scratch_shapes=[pltpu.SemaphoreType.DMA],
        compiler_params=params,
    )(taps_row, taps_col, jnp.asarray(transform_tables()))
    fa, pa, infos, even_out, odd_out = pl.pallas_call(
        pack_cols_kernel,
        out_shape=[shape(EXT_F), shape(EXT_P), shape(24), shape(272), shape(272)],
        in_specs=[VMEM] * 5,
        out_specs=[VMEM] * 5,
        compiler_params=params,
    )(friction, probe, row_even_out, row_even, row_odd)
    odd_in = swap(odd_out, "my", True)
    even_in = swap(even_out, "my", False)
    oa, ob = core_call(
        win_row, win_col, live_count, fa, pa, infos, even_in, odd_in, bands, col_band, tables
    )
    side, side_low, own, own_low = ob[:TILE_R], ob[TILE_R:], oa[:TILE_R], oa[TILE_R:]
    corner = diagonal(side_low)
    spill = ring(side, "my", 1)
    lower = ring(own_low, "mx", 1)
    inner_row, inner_col = lax.axis_index("mx") > 0, lax.axis_index("my") > 0
    result = own + jnp.where(inner_col, spill, 0.0)
    low = jnp.where(inner_row, lower, 0.0) + jnp.where(inner_row & inner_col, corner, 0.0)
    return result + jnp.pad(low, ((0, TILE_R - low.shape[0]), (0, 0)))


def solution(mesh):
    placed = (
        P("mx", "my"),
        P(),
        P(),
        P("mx", "my"),
        P("mx", "my", None),
        P("mx", "my", None),
        P("mx", "my"),
    )
    return jax.shard_map(
        per_device, mesh=mesh, in_specs=placed, out_specs=P("mx", "my"), check_vma=False
    )
```

```python
import ml_dtypes
import numpy as np

import jax
import jax.numpy as jnp
from jax import lax
from jax.experimental import pallas as pl
from jax.experimental.pallas import tpu as pltpu
from jax.sharding import PartitionSpec as P

SLOTS = 16
PATCH = 64
TILE_R = 256
LANES = 128
UP = 32
DOWN = 64
EXT_F = UP + TILE_R + DOWN
EXT_P = TILE_R + 32
OUT_R = TILE_R + 96
DEAD = -1.0e6
BF = jnp.bfloat16
F32 = jnp.float32
VMEM = pl.BlockSpec(memory_space=pltpu.VMEM)
SMEM = pl.BlockSpec(memory_space=pltpu.SMEM)
ANY = pl.BlockSpec(memory_space=pltpu.HBM)


def split(x):
    hi = x.astype(BF)
    return hi, (x - hi.astype(F32)).astype(BF)


def dot(a, b):
    return jnp.dot(a, b, preferred_element_type=F32)


def halves(x, axis):
    n = x.shape[axis] // 2
    return lax.slice_in_dim(x, 0, n, axis=axis) + lax.slice_in_dim(x, n, 2 * n, axis=axis)


def np_split(x):
    hi = x.astype(ml_dtypes.bfloat16)
    return hi, (x - hi.astype(np.float64)).astype(ml_dtypes.bfloat16)


def transform_tables():
    theta = np.pi * (2 * np.arange(64) + 1) / 128
    short = np.outer(np.arange(64), theta)
    forward = np.concatenate([np.cos(short), np.sin(short)], 1)
    wide = np.zeros((128, 128))
    wide[32:96] = forward
    full = np.outer(theta, np.arange(128))
    inverse = np.concatenate([np.cos(full), np.sin(full)], 0) / 64
    lane_half = inverse / 2
    hi, lo = np_split(wide)
    lane_fwd = np.block([[hi, lo], [hi, lo]])
    hi, lo = np_split(forward.T)
    row_fwd = np.block([[hi, hi], [lo, lo]])
    hi, lo = np_split(lane_half)
    lane_inv = np.block([[hi, lo], [hi, lo]])
    hi, lo = np_split(inverse.T)
    row_inv = np.block([[hi, hi], [lo, lo]])
    return np.concatenate([lane_fwd, lane_inv, row_inv, row_fwd], 1)


def bands_kernel(taps_row, taps_col, tables_in, row_out, col_out, tables, sem):
    table_copy = pltpu.make_async_copy(tables_in, tables, sem)
    table_copy.start()
    gap = lax.broadcasted_iota(jnp.int32, (112, 128), 1) - lax.broadcasted_iota(jnp.int32, (112, 128), 0)
    band = jnp.zeros((112, 128), F32)
    for t in range(17):
        band = jnp.where(gap == t, taps_row[t], band)
    hi, lo = split(band)
    row_out[0:112, :] = hi
    row_out[112:224, :] = lo
    gap = lax.broadcasted_iota(jnp.int32, (128, 128), 0) - lax.broadcasted_iota(jnp.int32, (128, 128), 1) + 8
    band = jnp.zeros((128, 128), F32)
    for t in range(17):
        band = jnp.where(gap == t, taps_col[t], band)
    hi, lo = split(band)
    pair = jnp.concatenate([hi, lo], 1)
    col_out[...] = jnp.concatenate([pair, pair], 0)
    table_copy.wait()


def own_index(axis):
    return lax.axis_index(axis), lax.axis_size(axis)


def pack_rows_kernel(win_row, win_col, live_count, friction, probe, even_out, odd_out, rows, cols, count, sems):
    def fetch(down, up):
        return [
            pltpu.make_async_copy(friction.at[pl.ds(TILE_R - UP, UP)], down.at[pl.ds(0, UP)], sems.at[3]),
            pltpu.make_async_copy(friction.at[pl.ds(0, DOWN)], up.at[pl.ds(0, DOWN)], sems.at[4]),
            pltpu.make_async_copy(probe.at[pl.ds(0, 32)], up.at[pl.ds(DOWN, 32)], sems.at[5]),
        ]

    is_even = lax.rem(lax.axis_index("mx"), 2) == 0

    @pl.when(is_even)
    def _():
        for copy in fetch(even_out, odd_out):
            copy.start()

    @pl.when(jnp.logical_not(is_even))
    def _():
        for copy in fetch(odd_out, even_out):
            copy.start()

    copies = [
        pltpu.make_async_copy(win_row.at[0], rows, sems.at[0]),
        pltpu.make_async_copy(win_col.at[0], cols, sems.at[1]),
        pltpu.make_async_copy(live_count, count, sems.at[2]),
    ]
    for copy in copies:
        copy.start()
    for copy in copies:
        copy.wait()
    lane = lax.broadcasted_iota(jnp.int32, (1, SLOTS), 1)
    live = lane < count[...]
    row = jnp.where(live, rows[...].astype(F32), DEAD)
    col = cols[...].astype(F32)
    wide = jnp.concatenate([jnp.concatenate([x, jnp.zeros((1, LANES - SLOTS), F32)], 1) for x in (row, col)], 0)
    turned = pltpu.roll(wide, LANES - 2, 1)
    info = jnp.concatenate([wide[0:1], turned[0:1], wide[1:2], turned[1:2], jnp.zeros((4, LANES), F32)], 0)
    even_out[96:104, :] = info
    odd_out[96:104, :] = info
    for copy in fetch(even_out, odd_out):
        copy.wait()


def pack_cols_kernel(friction, probe, mine, row_even, row_odd, fa, pa, infos, even_out, odd_out):
    at, count = own_index("mx")
    top, bottom = at == 0, at == count - 1
    is_even = lax.rem(at, 2) == 0
    above = jnp.where(is_even, row_odd[...], row_even[...])
    below = jnp.where(is_even, row_even[...], row_odd[...])
    fa[0:UP, :] = jnp.where(top, 0.0, above[0:UP])
    fa[UP : UP + TILE_R, :] = friction[...]
    fa[UP + TILE_R : EXT_F, :] = jnp.where(bottom, 0.0, below[0:DOWN])
    pa[0:TILE_R, :] = probe[...]
    pa[TILE_R:EXT_P, :] = jnp.where(bottom, 0.0, below[DOWN : DOWN + 32])
    infos[0:8, :] = mine[96:104, :]
    infos[8:16, :] = jnp.where(top, DEAD, above[96:104])
    infos[16:24, :] = jnp.where(bottom, DEAD, below[96:104])

    def packed(ref, rows, width, start):
        count = LANES // width
        part = rows // count
        lane = lax.broadcasted_iota(jnp.int32, (part, LANES), 1) // width
        total = jnp.zeros((part, LANES), F32)
        for i in range(count):
            piece = pltpu.roll(ref[i * part : (i + 1) * part, :], (width * i - start) % LANES, 1)
            total = jnp.where(lane == i, piece, total)
        return total

    def fill(right, left):
        right[0:88, :] = packed(fa, EXT_F, 32, 96)
        left[0:176, :] = packed(fa, EXT_F, 64, 0)
        left[176:248, :] = packed(pa, EXT_P, 32, 0)
        right[248:272, :] = infos[...]
        left[248:272, :] = infos[...]

    is_even = lax.rem(lax.axis_index("my"), 2) == 0

    @pl.when(is_even)
    def _():
        fill(even_out, odd_out)

    @pl.when(jnp.logical_not(is_even))
    def _():
        fill(odd_out, even_out)


def window(a, b, start):
    turn = lax.rem(256 - start, 128)
    lane = lax.broadcasted_iota(jnp.int32, a.shape, 1) + start
    return jnp.where((lane >= 0) & (lane < LANES), pltpu.roll(a, turn, 1), pltpu.roll(b, turn, 1))


def core_kernel(
    win_row_in, win_col_in, live_in, fa, pa, infos, even_in, odd_in, bands, col_band, tables,
    oa, ob, fb, pb, fw, y2, z, comb, spec, wide, win_row, win_col, live_count, from_left, from_right, sems,
):
    scalar_copies = [
        pltpu.make_async_copy(win_row_in, win_row, sems.at[1]),
        pltpu.make_async_copy(win_col_in, win_col, sems.at[2]),
        pltpu.make_async_copy(live_in, live_count, sems.at[3]),
    ]
    for copy in scalar_copies:
        copy.start()
    at_col, col_count = own_index("my")
    leftmost, rightmost = at_col == 0, at_col == col_count - 1
    is_even = lax.rem(at_col, 2) == 0
    from_left[...] = jnp.where(is_even, odd_in[...], even_in[...])
    from_right[...] = jnp.where(is_even, even_in[...], odd_in[...])
    lane = lax.broadcasted_iota(jnp.int32, (8, LANES), 1)
    for i in range(4):
        rows = slice(88 * i, 88 * i + 88)
        rim = pltpu.roll(from_left[0:88, :], 96 - 32 * i, 1)
        lane88 = lax.broadcasted_iota(jnp.int32, (88, LANES), 1)
        near = from_right[88 * (i % 2) : 88 * (i % 2) + 88, :]
        if i >= 2:
            near = pltpu.roll(near, 64, 1)
        keep_l = (lane88 >= 96) & jnp.logical_not(leftmost)
        keep_r = (lane88 < 64) & jnp.logical_not(rightmost)
        fb[rows, :] = jnp.where(keep_l, rim, jnp.where(keep_r, near, 0.0))
        lane72 = lax.broadcasted_iota(jnp.int32, (72, LANES), 1)
        near = pltpu.roll(from_right[176:248, :], (128 - 32 * i) % 128, 1)
        pb[72 * i : 72 * i + 72, :] = jnp.where((lane72 < 32) & jnp.logical_not(rightmost), near, 0.0)
    is_row = lax.broadcasted_iota(jnp.int32, (8, LANES), 0) < 2
    cand = jnp.full((8, LANES), DEAD, F32)
    tile = 0
    for dc in (0, -1, 1):
        for n, dr in enumerate((0, -1, 1)):
            if dc == 0:
                block = infos[8 * n : 8 * n + 8, :]
            elif dc == -1:
                block = jnp.where(leftmost, DEAD, from_left[248 + 8 * n : 256 + 8 * n, :])
            else:
                block = jnp.where(rightmost, DEAD, from_right[248 + 8 * n : 256 + 8 * n, :])
            block = block + jnp.where(is_row, float(TILE_R * dr), float(LANES * dc))
            here = (lane // 16 == tile // 2) & (lax.rem(lane, 4) // 2 == tile % 2)
            cand = jnp.where(here, pltpu.roll(block, 16 * (tile // 2) + 2 * (tile % 2), 1), cand)
            tile += 1
    sub_f = lax.broadcasted_iota(jnp.int32, (128, LANES), 0).astype(F32)
    lane_f = lax.broadcasted_iota(jnp.int32, (128, LANES), 1).astype(F32)
    lane1 = lax.broadcasted_iota(jnp.int32, (1, LANES), 1)
    upright = cand.T
    columns = [jnp.broadcast_to(upright[:, 2 + h : 3 + h], (128, LANES)) for h in range(2)]
    for k in range(SLOTS):
        half = (k % 4) // 2
        row0, col0 = infos[0:1, k : k + 1] - 64.0, infos[2:3, k : k + 1] - 64.0
        p = jnp.where(lax.rem(lane1, 2) == k % 2, cand[half : half + 1] - row0, -1.0)
        at_row = (sub_f == p).astype(F32).astype(BF)
        at_col = jnp.where(lane_f + col0 == columns[half], 64.0, 0.0).astype(BF)
        comb[k // 2, :, 128 * (k % 2) : 128 * (k % 2) + 128] = dot(at_row, at_col).astype(BF)
    for k in range(0, SLOTS, 2):
        t = halves(dot(bands[...], comb[k // 2]), 0)
        for m in range(2):
            hi, lo = split(t[:, 128 * m : 128 * m + 128])
            y2[pl.ds((k + m) * 112, 112), :] = jnp.concatenate([hi, lo], 1)
    for copy in scalar_copies:
        copy.wait()
    for k in range(SLOTS):
        rows = pl.ds(win_row[0, 0, k], 128)
        fw[k] = window(fa[rows, :], fb[rows, :], win_col[0, 0, k] - 32)
    first, n = 8, 112
    while True:
        o = halves(dot(y2[0 : SLOTS * n, :], col_band[...]), 1)
        o = o.reshape(SLOTS, n, 128) * fw[:, first : first + n, :]
        if n == PATCH:
            break
        hi, lo = split(o)
        both = jnp.concatenate([hi, lo], 1)
        m = n - 16
        band_hi, band_lo = bands[0:m, 0:n], bands[112 : 112 + m, 0:n]
        lhs = jnp.concatenate(
            [jnp.concatenate([band_hi, band_hi], 1), jnp.concatenate([band_lo, band_lo], 1)], 0
        )
        for k in range(0, SLOTS, 2):
            t = halves(dot(lhs, jnp.concatenate([both[k], both[k + 1]], 1)), 0)
            for i in range(2):
                hi, lo = split(t[:, 128 * i : 128 * i + 128])
                y2[pl.ds((k + i) * m, m), :] = jnp.concatenate([hi, lo], 1)
        first, n = first + 8, m

    def lane_transform(x):
        hi, lo = split(x)
        return split(halves(dot(jnp.concatenate([hi, lo], 1), tables[:, 0:256]), 1))

    ker_hi, ker_lo = lane_transform(o.reshape(SLOTS * PATCH, 128))
    for k in range(SLOTS):
        rows = pl.ds(win_row[0, 0, k], PATCH)
        z[pl.ds(k * PATCH, PATCH), :] = window(pa[rows, :], pb[rows, :], win_col[0, 0, k] - 32)
    win_hi, win_lo = lane_transform(z[...])
    left_half = lax.broadcasted_iota(jnp.int32, (PATCH, 128), 1) < 64
    sign = jnp.where(left_half, -1.0, 1.0)

    def pair(t):
        a, b = t[:64], pltpu.roll(t[64:], 64, 1) * sign
        return a + b, a - b

    def times(a, b):
        ar, br = pltpu.roll(a, 64, 1), pltpu.roll(b, 64, 1)
        return jnp.where(left_half, a, ar) * b + jnp.where(left_half, -ar, a) * br

    def spectrum(k):
        s = slice(PATCH * k, PATCH * k + PATCH)
        w = jnp.concatenate(
            [jnp.concatenate([ker_hi[s], win_hi[s]], 1), jnp.concatenate([ker_lo[s], win_lo[s]], 1)], 0
        )
        t = halves(dot(tables[:, 768:896], w), 0)
        k1, k2 = pair(t[:, :128])
        w1, w2 = pair(t[:, 128:])
        p1, p2 = times(k1, w1), times(k2, w2)
        return jnp.concatenate([p1 + p2, pltpu.roll((p1 - p2) * sign, 64, 1)], 0)

    for k in range(SLOTS):
        hi, lo = split(spectrum(k))
        spec[pl.ds(k * 128, 128), :] = jnp.concatenate([hi, lo], 1)
    for k in range(SLOTS):
        hi, lo = split(halves(dot(spec[k * 128 : k * 128 + 128, :], tables[:, 256:512]), 1))
        wide[k // 2, :, 128 * (k % 2) : 128 * (k % 2) + 128] = jnp.concatenate([hi, lo], 0)
    oa[...] = jnp.zeros_like(oa)
    ob[...] = jnp.zeros_like(ob)
    lane128 = lax.broadcasted_iota(jnp.int32, (128, LANES), 1)
    for k in range(0, SLOTS, 2):
        t = halves(dot(tables[:, 512:768], wide[k // 2]), 0)
        for m in range(2):
            kk = k + m
            col = win_col[0, 0, kk]
            live = jnp.where(kk < live_count[0, 0], 1.0, 0.0)
            patch = pltpu.roll(t[:, 128 * m : 128 * m + 128] * live, col, 1)
            rows = pl.ds(win_row[0, 0, kk], 128)
            oa[rows, :] += jnp.where(lane128 >= col, patch, 0.0)
            ob[rows, :] += jnp.where(lane128 < col, patch, 0.0)


def shape(rows, dtype=F32, cols=LANES):
    return jax.ShapeDtypeStruct((rows, cols), dtype)


def ring(x, axis, by):
    count = lax.axis_size(axis)
    return lax.ppermute(x, axis, [(i, (i + by) % count) for i in range(count)])


def swap(x, axis, odd):
    rows, cols = lax.axis_size("mx"), lax.axis_size("my")
    pairs = []
    for i in range(rows):
        for j in range(cols):
            if axis == "my":
                k = ((j + 1) ^ 1) - 1 if odd else j ^ 1
                to = (i, k) if 0 <= k < cols else (i ^ 1, j)
            else:
                k = ((i + 1) ^ 1) - 1 if odd else i ^ 1
                to = (k, j) if 0 <= k < rows else (i, j ^ 1)
            pairs.append((i * cols + j, to[0] * cols + to[1]))
    return lax.ppermute(x, ("mx", "my"), pairs)


def diagonal(x):
    rows, cols = lax.axis_size("mx"), lax.axis_size("my")
    pairs = [(i * cols + j, (i + 1) % rows * cols + (j + 1) % cols) for i in range(rows) for j in range(cols)]
    return lax.ppermute(x, ("mx", "my"), pairs)


def core_call(win_row, win_col, live_count, fa, pa, infos, even_in, odd_in, bands, col_band, tables):
    return pl.pallas_call(
        core_kernel,
        out_shape=[shape(OUT_R)] * 2,
        in_specs=[ANY] * 3 + [VMEM] * 8,
        out_specs=[VMEM] * 2,
        scratch_shapes=[
            pltpu.VMEM((EXT_F, LANES), F32),
            pltpu.VMEM((EXT_P, LANES), F32),
            pltpu.VMEM((SLOTS, 128, LANES), F32),
            pltpu.VMEM((SLOTS * 112, 256), BF),
            pltpu.VMEM((SLOTS * PATCH, LANES), F32),
            pltpu.VMEM((SLOTS // 2, 128, 256), BF),
            pltpu.VMEM((SLOTS * 128, 256), BF),
            pltpu.VMEM((SLOTS // 2, 256, 256), BF),
            pltpu.SMEM((1, 1, SLOTS), jnp.int32),
            pltpu.SMEM((1, 1, SLOTS), jnp.int32),
            pltpu.SMEM((1, 1), jnp.int32),
            pltpu.VMEM((272, LANES), F32),
            pltpu.VMEM((272, LANES), F32),
            pltpu.SemaphoreType.DMA((4,)),
        ],
        compiler_params=pltpu.CompilerParams(vmem_limit_bytes=40 * 2**20),
    )(
        win_row, win_col, live_count, fa, pa, infos, even_in, odd_in, bands, col_band, tables,
    )


def per_device(friction, taps_row, taps_col, probe, win_row, win_col, live_count):
    params = pltpu.CompilerParams(vmem_limit_bytes=40 * 2**20)
    row_even_out, row_odd_out = pl.pallas_call(
        pack_rows_kernel,
        out_shape=[shape(104), shape(104)],
        in_specs=[ANY] * 5,
        out_specs=[VMEM] * 2,
        scratch_shapes=[
            pltpu.VMEM((1, SLOTS), jnp.int32),
            pltpu.VMEM((1, SLOTS), jnp.int32),
            pltpu.VMEM((1, 1), jnp.int32),
            pltpu.SemaphoreType.DMA((6,)),
        ],
        compiler_params=pltpu.CompilerParams(vmem_limit_bytes=40 * 2**20),
    )(win_row, win_col, live_count, friction, probe)
    row_odd = swap(row_odd_out, "mx", True)
    row_even = swap(row_even_out, "mx", False)
    bands, col_band, tables = pl.pallas_call(
        bands_kernel,
        out_shape=[shape(224, BF), shape(256, BF, 256), shape(256, BF, 896)],
        in_specs=[SMEM] * 2 + [ANY],
        out_specs=[VMEM] * 3,
        scratch_shapes=[pltpu.SemaphoreType.DMA],
        compiler_params=params,
    )(taps_row, taps_col, jnp.asarray(transform_tables()))
    fa, pa, infos, even_out, odd_out = pl.pallas_call(
        pack_cols_kernel,
        out_shape=[shape(EXT_F), shape(EXT_P), shape(24), shape(272), shape(272)],
        in_specs=[VMEM] * 5,
        out_specs=[VMEM] * 5,
        compiler_params=params,
    )(friction, probe, row_even_out, row_even, row_odd)
    odd_in = swap(odd_out, "my", True)
    even_in = swap(even_out, "my", False)
    oa, ob = core_call(
        win_row, win_col, live_count, fa, pa, infos, even_in, odd_in, bands, col_band, tables
    )
    side, side_low, own, own_low = ob[:TILE_R], ob[TILE_R:], oa[:TILE_R], oa[TILE_R:]
    corner = diagonal(side_low)
    spill = ring(side, "my", 1)
    lower = ring(own_low, "mx", 1)
    inner_row, inner_col = lax.axis_index("mx") > 0, lax.axis_index("my") > 0
    result = own + jnp.where(inner_col, spill, 0.0)
    low = jnp.where(inner_row, lower, 0.0) + jnp.where(inner_row & inner_col, corner, 0.0)
    return result + jnp.pad(low, ((0, TILE_R - low.shape[0]), (0, 0)))


def solution(mesh):
    placed = (
        P("mx", "my"),
        P(),
        P(),
        P("mx", "my"),
        P("mx", "my", None),
        P("mx", "my", None),
        P("mx", "my"),
    )
    return jax.shard_map(
        per_device, mesh=mesh, in_specs=placed, out_specs=P("mx", "my"), check_vma=False
    )
```

```python
import ml_dtypes
import numpy as np

import jax
import jax.numpy as jnp
from jax import lax
from jax.experimental import pallas as pl
from jax.experimental.pallas import tpu as pltpu
from jax.sharding import PartitionSpec as P

SLOTS = 16
PATCH = 64
TILE_R = 256
LANES = 128
UP = 32
DOWN = 64
EXT_F = UP + TILE_R + DOWN
EXT_P = TILE_R + 32
OUT_R = TILE_R + 96
DEAD = -1.0e6
BF = jnp.bfloat16
F32 = jnp.float32
VMEM = pl.BlockSpec(memory_space=pltpu.VMEM)
SMEM = pl.BlockSpec(memory_space=pltpu.SMEM)
ANY = pl.BlockSpec(memory_space=pltpu.HBM)


def split(x):
    hi = x.astype(BF)
    return hi, (x - hi.astype(F32)).astype(BF)


def dot(a, b):
    return jnp.dot(a, b, preferred_element_type=F32)


def halves(x, axis):
    n = x.shape[axis] // 2
    return lax.slice_in_dim(x, 0, n, axis=axis) + lax.slice_in_dim(x, n, 2 * n, axis=axis)


def np_split(x):
    hi = x.astype(ml_dtypes.bfloat16)
    return hi, (x - hi.astype(np.float64)).astype(ml_dtypes.bfloat16)


def transform_tables():
    theta = np.pi * (2 * np.arange(64) + 1) / 128
    short = np.outer(np.arange(64), theta)
    forward = np.concatenate([np.cos(short), np.sin(short)], 1)
    wide = np.zeros((128, 128))
    wide[32:96] = forward
    full = np.outer(theta, np.arange(128))
    inverse = np.concatenate([np.cos(full), np.sin(full)], 0) / 64
    lane_half = inverse / 2
    hi, lo = np_split(wide)
    lane_fwd = np.block([[hi, lo], [hi, lo]])
    hi, lo = np_split(forward.T)
    row_fwd = np.block([[hi, hi], [lo, lo]])
    hi, lo = np_split(lane_half)
    lane_inv = np.block([[hi, lo], [hi, lo]])
    hi, lo = np_split(inverse.T)
    row_inv = np.block([[hi, hi], [lo, lo]])
    return np.concatenate([lane_fwd, lane_inv, row_inv, row_fwd], 1)


def bands_kernel(taps_row, taps_col, tables_in, row_out, col_out, tables, sem):
    table_copy = pltpu.make_async_copy(tables_in, tables, sem)
    table_copy.start()
    gap = lax.broadcasted_iota(jnp.int32, (112, 128), 1) - lax.broadcasted_iota(jnp.int32, (112, 128), 0)
    band = jnp.zeros((112, 128), F32)
    for t in range(17):
        band = jnp.where(gap == t, taps_row[t], band)
    hi, lo = split(band)
    row_out[0:112, :] = hi
    row_out[112:224, :] = lo
    gap = lax.broadcasted_iota(jnp.int32, (128, 128), 0) - lax.broadcasted_iota(jnp.int32, (128, 128), 1) + 8
    band = jnp.zeros((128, 128), F32)
    for t in range(17):
        band = jnp.where(gap == t, taps_col[t], band)
    hi, lo = split(band)
    pair = jnp.concatenate([hi, lo], 1)
    col_out[...] = jnp.concatenate([pair, pair], 0)
    table_copy.wait()


def own_index(axis):
    return lax.axis_index(axis), lax.axis_size(axis)


def pack_rows_kernel(win_row, win_col, live_count, friction, probe, even_out, odd_out, rows, cols, count, sems):
    def fetch(down, up):
        return [
            pltpu.make_async_copy(friction.at[pl.ds(TILE_R - UP, UP)], down.at[pl.ds(0, UP)], sems.at[3]),
            pltpu.make_async_copy(friction.at[pl.ds(0, DOWN)], up.at[pl.ds(0, DOWN)], sems.at[4]),
            pltpu.make_async_copy(probe.at[pl.ds(0, 32)], up.at[pl.ds(DOWN, 32)], sems.at[5]),
        ]

    is_even = lax.rem(lax.axis_index("mx"), 2) == 0

    @pl.when(is_even)
    def _():
        for copy in fetch(even_out, odd_out):
            copy.start()

    @pl.when(jnp.logical_not(is_even))
    def _():
        for copy in fetch(odd_out, even_out):
            copy.start()

    copies = [
        pltpu.make_async_copy(win_row.at[0], rows, sems.at[0]),
        pltpu.make_async_copy(win_col.at[0], cols, sems.at[1]),
        pltpu.make_async_copy(live_count, count, sems.at[2]),
    ]
    for copy in copies:
        copy.start()
    for copy in copies:
        copy.wait()
    lane = lax.broadcasted_iota(jnp.int32, (1, SLOTS), 1)
    live = lane < count[...]
    row = jnp.where(live, rows[...].astype(F32), DEAD)
    col = cols[...].astype(F32)
    wide = jnp.concatenate([jnp.concatenate([x, jnp.zeros((1, LANES - SLOTS), F32)], 1) for x in (row, col)], 0)
    turned = pltpu.roll(wide, LANES - 2, 1)
    info = jnp.concatenate([wide[0:1], turned[0:1], wide[1:2], turned[1:2], jnp.zeros((4, LANES), F32)], 0)
    even_out[96:104, :] = info
    odd_out[96:104, :] = info
    for copy in fetch(even_out, odd_out):
        copy.wait()


def fetch_kernel(friction, probe, fa, pa, sems):
    copies = [
        pltpu.make_async_copy(friction, fa.at[pl.ds(UP, TILE_R)], sems.at[0]),
        pltpu.make_async_copy(probe, pa.at[pl.ds(0, TILE_R)], sems.at[1]),
    ]
    for copy in copies:
        copy.start()
    for copy in copies:
        copy.wait()


def pack_cols_kernel(fa_in, pa_in, mine, row_even, row_odd, fa, pa, infos, even_out, odd_out):
    at, count = own_index("mx")
    top, bottom = at == 0, at == count - 1
    is_even = lax.rem(at, 2) == 0
    above = jnp.where(is_even, row_odd[...], row_even[...])
    below = jnp.where(is_even, row_even[...], row_odd[...])
    fa[0:UP, :] = jnp.where(top, 0.0, above[0:UP])
    fa[UP + TILE_R : EXT_F, :] = jnp.where(bottom, 0.0, below[0:DOWN])
    pa[TILE_R:EXT_P, :] = jnp.where(bottom, 0.0, below[DOWN : DOWN + 32])
    infos[0:8, :] = mine[96:104, :]
    infos[8:16, :] = jnp.where(top, DEAD, above[96:104])
    infos[16:24, :] = jnp.where(bottom, DEAD, below[96:104])

    def packed(ref, rows, width, start):
        count = LANES // width
        part = rows // count
        lane = lax.broadcasted_iota(jnp.int32, (part, LANES), 1) // width
        total = jnp.zeros((part, LANES), F32)
        for i in range(count):
            piece = pltpu.roll(ref[i * part : (i + 1) * part, :], (width * i - start) % LANES, 1)
            total = jnp.where(lane == i, piece, total)
        return total

    def fill(right, left):
        right[0:88, :] = packed(fa, EXT_F, 32, 96)
        left[0:176, :] = packed(fa, EXT_F, 64, 0)
        left[176:248, :] = packed(pa, EXT_P, 32, 0)
        right[248:272, :] = infos[...]
        left[248:272, :] = infos[...]

    is_even = lax.rem(lax.axis_index("my"), 2) == 0

    @pl.when(is_even)
    def _():
        fill(even_out, odd_out)

    @pl.when(jnp.logical_not(is_even))
    def _():
        fill(odd_out, even_out)


def window(a, b, start):
    turn = lax.rem(256 - start, 128)
    lane = lax.broadcasted_iota(jnp.int32, a.shape, 1) + start
    return jnp.where((lane >= 0) & (lane < LANES), pltpu.roll(a, turn, 1), pltpu.roll(b, turn, 1))


def core_kernel(
    win_row_in, win_col_in, live_in, fa, pa, infos, even_in, odd_in, bands, col_band, tables,
    oa, ob, fb, pb, fw, y2, z, comb, spec, wide, win_row, win_col, live_count, from_left, from_right, sems,
):
    scalar_copies = [
        pltpu.make_async_copy(win_row_in, win_row, sems.at[1]),
        pltpu.make_async_copy(win_col_in, win_col, sems.at[2]),
        pltpu.make_async_copy(live_in, live_count, sems.at[3]),
    ]
    for copy in scalar_copies:
        copy.start()
    at_col, col_count = own_index("my")
    leftmost, rightmost = at_col == 0, at_col == col_count - 1
    is_even = lax.rem(at_col, 2) == 0
    from_left[...] = jnp.where(is_even, odd_in[...], even_in[...])
    from_right[...] = jnp.where(is_even, even_in[...], odd_in[...])
    lane = lax.broadcasted_iota(jnp.int32, (8, LANES), 1)
    for i in range(4):
        rows = slice(88 * i, 88 * i + 88)
        rim = pltpu.roll(from_left[0:88, :], 96 - 32 * i, 1)
        lane88 = lax.broadcasted_iota(jnp.int32, (88, LANES), 1)
        near = from_right[88 * (i % 2) : 88 * (i % 2) + 88, :]
        if i >= 2:
            near = pltpu.roll(near, 64, 1)
        keep_l = (lane88 >= 96) & jnp.logical_not(leftmost)
        keep_r = (lane88 < 64) & jnp.logical_not(rightmost)
        fb[rows, :] = jnp.where(keep_l, rim, jnp.where(keep_r, near, 0.0))
        lane72 = lax.broadcasted_iota(jnp.int32, (72, LANES), 1)
        near = pltpu.roll(from_right[176:248, :], (128 - 32 * i) % 128, 1)
        pb[72 * i : 72 * i + 72, :] = jnp.where((lane72 < 32) & jnp.logical_not(rightmost), near, 0.0)
    is_row = lax.broadcasted_iota(jnp.int32, (8, LANES), 0) < 2
    cand = jnp.full((8, LANES), DEAD, F32)
    tile = 0
    for dc in (0, -1, 1):
        for n, dr in enumerate((0, -1, 1)):
            if dc == 0:
                block = infos[8 * n : 8 * n + 8, :]
            elif dc == -1:
                block = jnp.where(leftmost, DEAD, from_left[248 + 8 * n : 256 + 8 * n, :])
            else:
                block = jnp.where(rightmost, DEAD, from_right[248 + 8 * n : 256 + 8 * n, :])
            block = block + jnp.where(is_row, float(TILE_R * dr), float(LANES * dc))
            here = (lane // 16 == tile // 2) & (lax.rem(lane, 4) // 2 == tile % 2)
            cand = jnp.where(here, pltpu.roll(block, 16 * (tile // 2) + 2 * (tile % 2), 1), cand)
            tile += 1
    sub_f = lax.broadcasted_iota(jnp.int32, (128, LANES), 0).astype(F32)
    lane_f = lax.broadcasted_iota(jnp.int32, (128, LANES), 1).astype(F32)
    lane1 = lax.broadcasted_iota(jnp.int32, (1, LANES), 1)
    upright = cand.T
    columns = [jnp.broadcast_to(upright[:, 2 + h : 3 + h], (128, LANES)) for h in range(2)]
    for k in range(SLOTS):
        half = (k % 4) // 2
        row0, col0 = infos[0:1, k : k + 1] - 64.0, infos[2:3, k : k + 1] - 64.0
        p = jnp.where(lax.rem(lane1, 2) == k % 2, cand[half : half + 1] - row0, -1.0)
        at_row = (sub_f == p).astype(F32).astype(BF)
        at_col = jnp.where(lane_f + col0 == columns[half], 64.0, 0.0).astype(BF)
        comb[k // 2, :, 128 * (k % 2) : 128 * (k % 2) + 128] = dot(at_row, at_col).astype(BF)
    for k in range(0, SLOTS, 2):
        t = halves(dot(bands[...], comb[k // 2]), 0)
        for m in range(2):
            hi, lo = split(t[:, 128 * m : 128 * m + 128])
            y2[pl.ds((k + m) * 112, 112), :] = jnp.concatenate([hi, lo], 1)
    for copy in scalar_copies:
        copy.wait()
    for k in range(SLOTS):
        rows = pl.ds(win_row[0, 0, k], 128)
        fw[k] = window(fa[rows, :], fb[rows, :], win_col[0, 0, k] - 32)
    first, n = 8, 112
    while True:
        o = halves(dot(y2[0 : SLOTS * n, :], col_band[...]), 1)
        o = o.reshape(SLOTS, n, 128) * fw[:, first : first + n, :]
        if n == PATCH:
            break
        hi, lo = split(o)
        both = jnp.concatenate([hi, lo], 1)
        m = n - 16
        band_hi, band_lo = bands[0:m, 0:n], bands[112 : 112 + m, 0:n]
        lhs = jnp.concatenate(
            [jnp.concatenate([band_hi, band_hi], 1), jnp.concatenate([band_lo, band_lo], 1)], 0
        )
        for k in range(0, SLOTS, 2):
            t = halves(dot(lhs, jnp.concatenate([both[k], both[k + 1]], 1)), 0)
            for i in range(2):
                hi, lo = split(t[:, 128 * i : 128 * i + 128])
                y2[pl.ds((k + i) * m, m), :] = jnp.concatenate([hi, lo], 1)
        first, n = first + 8, m

    def lane_transform(x):
        hi, lo = split(x)
        return split(halves(dot(jnp.concatenate([hi, lo], 1), tables[:, 0:256]), 1))

    ker_hi, ker_lo = lane_transform(o.reshape(SLOTS * PATCH, 128))
    for k in range(SLOTS):
        rows = pl.ds(win_row[0, 0, k], PATCH)
        z[pl.ds(k * PATCH, PATCH), :] = window(pa[rows, :], pb[rows, :], win_col[0, 0, k] - 32)
    win_hi, win_lo = lane_transform(z[...])
    left_half = lax.broadcasted_iota(jnp.int32, (PATCH, 128), 1) < 64
    sign = jnp.where(left_half, -1.0, 1.0)

    def pair(t):
        a, b = t[:64], pltpu.roll(t[64:], 64, 1) * sign
        return a + b, a - b

    def times(a, b):
        ar, br = pltpu.roll(a, 64, 1), pltpu.roll(b, 64, 1)
        return jnp.where(left_half, a, ar) * b + jnp.where(left_half, -ar, a) * br

    def spectrum(k):
        s = slice(PATCH * k, PATCH * k + PATCH)
        w = jnp.concatenate(
            [jnp.concatenate([ker_hi[s], win_hi[s]], 1), jnp.concatenate([ker_lo[s], win_lo[s]], 1)], 0
        )
        t = halves(dot(tables[:, 768:896], w), 0)
        k1, k2 = pair(t[:, :128])
        w1, w2 = pair(t[:, 128:])
        p1, p2 = times(k1, w1), times(k2, w2)
        return jnp.concatenate([p1 + p2, pltpu.roll((p1 - p2) * sign, 64, 1)], 0)

    for k in range(SLOTS):
        hi, lo = split(spectrum(k))
        spec[pl.ds(k * 128, 128), :] = jnp.concatenate([hi, lo], 1)
    for k in range(SLOTS):
        hi, lo = split(halves(dot(spec[k * 128 : k * 128 + 128, :], tables[:, 256:512]), 1))
        wide[k // 2, :, 128 * (k % 2) : 128 * (k % 2) + 128] = jnp.concatenate([hi, lo], 0)
    oa[...] = jnp.zeros_like(oa)
    ob[...] = jnp.zeros_like(ob)
    lane128 = lax.broadcasted_iota(jnp.int32, (128, LANES), 1)
    for k in range(0, SLOTS, 2):
        t = halves(dot(tables[:, 512:768], wide[k // 2]), 0)
        for m in range(2):
            kk = k + m
            col = win_col[0, 0, kk]
            live = jnp.where(kk < live_count[0, 0], 1.0, 0.0)
            patch = pltpu.roll(t[:, 128 * m : 128 * m + 128] * live, col, 1)
            rows = pl.ds(win_row[0, 0, kk], 128)
            oa[rows, :] += jnp.where(lane128 >= col, patch, 0.0)
            ob[rows, :] += jnp.where(lane128 < col, patch, 0.0)


def shape(rows, dtype=F32, cols=LANES):
    return jax.ShapeDtypeStruct((rows, cols), dtype)


def ring(x, axis, by):
    count = lax.axis_size(axis)
    return lax.ppermute(x, axis, [(i, (i + by) % count) for i in range(count)])


def swap(x, axis, odd):
    rows, cols = lax.axis_size("mx"), lax.axis_size("my")
    pairs = []
    for i in range(rows):
        for j in range(cols):
            if axis == "my":
                k = ((j + 1) ^ 1) - 1 if odd else j ^ 1
                to = (i, k) if 0 <= k < cols else (i ^ 1, j)
            else:
                k = ((i + 1) ^ 1) - 1 if odd else i ^ 1
                to = (k, j) if 0 <= k < rows else (i, j ^ 1)
            pairs.append((i * cols + j, to[0] * cols + to[1]))
    return lax.ppermute(x, ("mx", "my"), pairs)


def diagonal(x):
    rows, cols = lax.axis_size("mx"), lax.axis_size("my")
    pairs = [(i * cols + j, (i + 1) % rows * cols + (j + 1) % cols) for i in range(rows) for j in range(cols)]
    return lax.ppermute(x, ("mx", "my"), pairs)


def core_call(win_row, win_col, live_count, fa, pa, infos, even_in, odd_in, bands, col_band, tables):
    return pl.pallas_call(
        core_kernel,
        out_shape=[shape(OUT_R)] * 2,
        in_specs=[ANY] * 3 + [VMEM] * 8,
        out_specs=[VMEM] * 2,
        scratch_shapes=[
            pltpu.VMEM((EXT_F, LANES), F32),
            pltpu.VMEM((EXT_P, LANES), F32),
            pltpu.VMEM((SLOTS, 128, LANES), F32),
            pltpu.VMEM((SLOTS * 112, 256), BF),
            pltpu.VMEM((SLOTS * PATCH, LANES), F32),
            pltpu.VMEM((SLOTS // 2, 128, 256), BF),
            pltpu.VMEM((SLOTS * 128, 256), BF),
            pltpu.VMEM((SLOTS // 2, 256, 256), BF),
            pltpu.SMEM((1, 1, SLOTS), jnp.int32),
            pltpu.SMEM((1, 1, SLOTS), jnp.int32),
            pltpu.SMEM((1, 1), jnp.int32),
            pltpu.VMEM((272, LANES), F32),
            pltpu.VMEM((272, LANES), F32),
            pltpu.SemaphoreType.DMA((4,)),
        ],
        compiler_params=pltpu.CompilerParams(vmem_limit_bytes=40 * 2**20),
    )(
        win_row, win_col, live_count, fa, pa, infos, even_in, odd_in, bands, col_band, tables,
    )


def per_device(friction, taps_row, taps_col, probe, win_row, win_col, live_count):
    params = pltpu.CompilerParams(vmem_limit_bytes=40 * 2**20)
    row_even_out, row_odd_out = pl.pallas_call(
        pack_rows_kernel,
        out_shape=[shape(104), shape(104)],
        in_specs=[ANY] * 5,
        out_specs=[VMEM] * 2,
        scratch_shapes=[
            pltpu.VMEM((1, SLOTS), jnp.int32),
            pltpu.VMEM((1, SLOTS), jnp.int32),
            pltpu.VMEM((1, 1), jnp.int32),
            pltpu.SemaphoreType.DMA((6,)),
        ],
        compiler_params=pltpu.CompilerParams(vmem_limit_bytes=55040 * 2**10),
    )(win_row, win_col, live_count, friction, probe)
    row_odd = swap(row_odd_out, "mx", True)
    row_even = swap(row_even_out, "mx", False)
    fa, pa = pl.pallas_call(
        fetch_kernel,
        out_shape=[shape(EXT_F), shape(EXT_P)],
        in_specs=[ANY] * 2,
        out_specs=[VMEM] * 2,
        scratch_shapes=[pltpu.SemaphoreType.DMA((2,))],
        compiler_params=params,
    )(friction, probe)
    bands, col_band, tables = pl.pallas_call(
        bands_kernel,
        out_shape=[shape(224, BF), shape(256, BF, 256), shape(256, BF, 896)],
        in_specs=[SMEM] * 2 + [ANY],
        out_specs=[VMEM] * 3,
        scratch_shapes=[pltpu.SemaphoreType.DMA],
        compiler_params=params,
    )(taps_row, taps_col, jnp.asarray(transform_tables()))
    fa, pa, infos, even_out, odd_out = pl.pallas_call(
        pack_cols_kernel,
        out_shape=[shape(EXT_F), shape(EXT_P), shape(24), shape(272), shape(272)],
        in_specs=[VMEM] * 5,
        out_specs=[VMEM] * 5,
        input_output_aliases={0: 0, 1: 1},
        compiler_params=params,
    )(fa, pa, row_even_out, row_even, row_odd)
    odd_in = swap(odd_out, "my", True)
    even_in = swap(even_out, "my", False)
    oa, ob = core_call(
        win_row, win_col, live_count, fa, pa, infos, even_in, odd_in, bands, col_band, tables
    )
    side, side_low, own, own_low = ob[:TILE_R], ob[TILE_R:], oa[:TILE_R], oa[TILE_R:]
    spill = ring(side, "my", 1)
    corner = diagonal(side_low)
    lower = ring(own_low, "mx", 1)
    inner_row, inner_col = lax.axis_index("mx") > 0, lax.axis_index("my") > 0
    result = lax.optimization_barrier(own + jnp.where(inner_col, spill, 0.0))
    result = lax.optimization_barrier(result.at[:96].add(jnp.where(inner_row & inner_col, corner, 0.0)))
    low = jnp.where(inner_row, lower, 0.0)
    return result + jnp.pad(low, ((0, TILE_R - low.shape[0]), (0, 0)))


def solution(mesh):
    placed = (
        P("mx", "my"),
        P(),
        P(),
        P("mx", "my"),
        P("mx", "my", None),
        P("mx", "my", None),
        P("mx", "my"),
    )
    return jax.shard_map(
        per_device, mesh=mesh, in_specs=placed, out_specs=P("mx", "my"), check_vma=False
    )
```

```python
import ml_dtypes
import numpy as np

import jax
import jax.numpy as jnp
from jax import lax
from jax.experimental import pallas as pl
from jax.experimental.pallas import tpu as pltpu
from jax.sharding import PartitionSpec as P

SLOTS = 16
PATCH = 64
TILE_R = 256
LANES = 128
UP = 32
DOWN = 64
EXT_F = UP + TILE_R + DOWN
EXT_P = TILE_R + 32
OUT_R = TILE_R + 96
DEAD = -1.0e6
BF = jnp.bfloat16
F32 = jnp.float32
VMEM = pl.BlockSpec(memory_space=pltpu.VMEM)
SMEM = pl.BlockSpec(memory_space=pltpu.SMEM)
ANY = pl.BlockSpec(memory_space=pltpu.HBM)


def split(x):
    hi = x.astype(BF)
    return hi, (x - hi.astype(F32)).astype(BF)


def dot(a, b):
    return jnp.dot(a, b, preferred_element_type=F32)


def halves(x, axis):
    n = x.shape[axis] // 2
    return lax.slice_in_dim(x, 0, n, axis=axis) + lax.slice_in_dim(x, n, 2 * n, axis=axis)


def np_split(x):
    hi = x.astype(ml_dtypes.bfloat16)
    return hi, (x - hi.astype(np.float64)).astype(ml_dtypes.bfloat16)


def transform_tables():
    theta = np.pi * (2 * np.arange(64) + 1) / 128
    short = np.outer(np.arange(64), theta)
    forward = np.concatenate([np.cos(short), np.sin(short)], 1)
    wide = np.zeros((128, 128))
    wide[32:96] = forward
    full = np.outer(theta, np.arange(128))
    inverse = np.concatenate([np.cos(full), np.sin(full)], 0) / 64
    lane_half = inverse / 2
    hi, lo = np_split(wide)
    lane_fwd = np.block([[hi, lo], [hi, lo]])
    hi, lo = np_split(forward.T)
    row_fwd = np.block([[hi, hi], [lo, lo]])
    hi, lo = np_split(lane_half)
    lane_inv = np.block([[hi, lo], [hi, lo]])
    hi, lo = np_split(inverse.T)
    row_inv = np.block([[hi, hi], [lo, lo]])
    return np.concatenate([lane_fwd, lane_inv, row_inv, row_fwd], 1)


def bands_kernel(taps_row, taps_col, tables_in, row_out, col_out, tables, sem):
    table_copy = pltpu.make_async_copy(tables_in, tables, sem)
    table_copy.start()
    gap = lax.broadcasted_iota(jnp.int32, (112, 128), 1) - lax.broadcasted_iota(jnp.int32, (112, 128), 0)
    band = jnp.zeros((112, 128), F32)
    for t in range(17):
        band = jnp.where(gap == t, taps_row[t], band)
    hi, lo = split(band)
    row_out[0:112, :] = hi
    row_out[112:224, :] = lo
    gap = lax.broadcasted_iota(jnp.int32, (128, 128), 0) - lax.broadcasted_iota(jnp.int32, (128, 128), 1) + 8
    band = jnp.zeros((128, 128), F32)
    for t in range(17):
        band = jnp.where(gap == t, taps_col[t], band)
    hi, lo = split(band)
    pair = jnp.concatenate([hi, lo], 1)
    col_out[...] = jnp.concatenate([pair, pair], 0)
    table_copy.wait()


def own_index(axis):
    return lax.axis_index(axis), lax.axis_size(axis)


def pack_rows_kernel(win_row, win_col, live_count, friction, probe, even_out, odd_out, rows, cols, count, sems):
    def fetch(down, up):
        return [
            pltpu.make_async_copy(friction.at[pl.ds(TILE_R - UP, UP)], down.at[pl.ds(0, UP)], sems.at[3]),
            pltpu.make_async_copy(friction.at[pl.ds(0, DOWN)], up.at[pl.ds(0, DOWN)], sems.at[4]),
            pltpu.make_async_copy(probe.at[pl.ds(0, 32)], up.at[pl.ds(DOWN, 32)], sems.at[5]),
        ]

    is_even = lax.rem(lax.axis_index("mx"), 2) == 0

    @pl.when(is_even)
    def _():
        for copy in fetch(even_out, odd_out):
            copy.start()

    @pl.when(jnp.logical_not(is_even))
    def _():
        for copy in fetch(odd_out, even_out):
            copy.start()

    copies = [
        pltpu.make_async_copy(win_row.at[0], rows, sems.at[0]),
        pltpu.make_async_copy(win_col.at[0], cols, sems.at[1]),
        pltpu.make_async_copy(live_count, count, sems.at[2]),
    ]
    for copy in copies:
        copy.start()
    for copy in copies:
        copy.wait()
    lane = lax.broadcasted_iota(jnp.int32, (1, SLOTS), 1)
    live = lane < count[...]
    row = jnp.where(live, rows[...].astype(F32), DEAD)
    col = cols[...].astype(F32)
    wide = jnp.concatenate([jnp.concatenate([x, jnp.zeros((1, LANES - SLOTS), F32)], 1) for x in (row, col)], 0)
    turned = pltpu.roll(wide, LANES - 2, 1)
    info = jnp.concatenate([wide[0:1], turned[0:1], wide[1:2], turned[1:2], jnp.zeros((4, LANES), F32)], 0)
    even_out[96:104, :] = info
    odd_out[96:104, :] = info
    for copy in fetch(even_out, odd_out):
        copy.wait()


def fetch_kernel(friction, probe, fa, pa, sems):
    copies = [
        pltpu.make_async_copy(friction, fa.at[pl.ds(UP, TILE_R)], sems.at[0]),
        pltpu.make_async_copy(probe, pa.at[pl.ds(0, TILE_R)], sems.at[1]),
    ]
    for copy in copies:
        copy.start()
    for copy in copies:
        copy.wait()


def pack_cols_kernel(fa_in, pa_in, mine, row_even, row_odd, odd_slots, fa, pa, infos, even_out, odd_out):
    at, count = own_index("mx")
    top, bottom = at == 0, at == count - 1
    is_even = lax.rem(at, 2) == 0
    above = jnp.where(is_even, row_odd[...], row_even[...])
    below = jnp.where(is_even, row_even[...], row_odd[...])
    fa[0:UP, :] = jnp.where(top, 0.0, above[0:UP])
    fa[UP + TILE_R : EXT_F, :] = jnp.where(bottom, 0.0, below[0:DOWN])
    pa[TILE_R:EXT_P, :] = jnp.where(bottom, 0.0, below[DOWN : DOWN + 32])
    infos[0:8, :] = mine[96:104, :]
    infos[8:16, :] = jnp.where(top, DEAD, jnp.where(is_even, odd_slots[...], row_even[96:104, :]))
    infos[16:24, :] = jnp.where(bottom, DEAD, jnp.where(is_even, row_even[96:104, :], odd_slots[...]))

    def packed(ref, rows, width, start, first=0):
        count = LANES // width
        part = rows // count
        lane = lax.broadcasted_iota(jnp.int32, (part, LANES), 1) // width
        total = jnp.zeros((part, LANES), F32)
        for i in range(count):
            piece = pltpu.roll(ref[first + i * part : first + (i + 1) * part, :], (width * i - start) % LANES, 1)
            total = jnp.where(lane == i, piece, total)
        return total

    def fill(right, left):
        right[0:88, :] = packed(fa, EXT_F, 32, 96)
        left[0:168, :] = packed(fa, EXT_F - 16, 64, 0, 8)
        left[168:240, :] = packed(pa, EXT_P, 32, 0)
        third = lax.broadcasted_iota(jnp.int32, (8, LANES), 1) // 32
        both = jnp.where(third == 1, pltpu.roll(infos[8:16, :], 32, 1), pltpu.roll(infos[16:24, :], 64, 1))
        both = jnp.where(third == 0, infos[0:8, :], both)
        right[240:248, :] = both
        left[240:248, :] = both

    is_even = lax.rem(lax.axis_index("my"), 2) == 0

    @pl.when(is_even)
    def _():
        fill(even_out, odd_out)

    @pl.when(jnp.logical_not(is_even))
    def _():
        fill(odd_out, even_out)


def window(a, b, start):
    turn = lax.rem(256 - start, 128)
    lane = lax.broadcasted_iota(jnp.int32, a.shape, 1) + start
    return jnp.where((lane >= 0) & (lane < LANES), pltpu.roll(a, turn, 1), pltpu.roll(b, turn, 1))


def core_kernel(
    win_row_in, win_col_in, live_in, fa, pa, infos, even_in, odd_in, odd_slots, bands, col_band, tables,
    own, own_low, side, side_low, oa, ob, fb, pb, fw, y2, z, comb, spec, wide, win_row, win_col, live_count, from_left, from_right, sems,
):
    scalar_copies = [
        pltpu.make_async_copy(win_row_in, win_row, sems.at[1]),
        pltpu.make_async_copy(win_col_in, win_col, sems.at[2]),
        pltpu.make_async_copy(live_in, live_count, sems.at[3]),
    ]
    for copy in scalar_copies:
        copy.start()
    at_col, col_count = own_index("my")
    leftmost, rightmost = at_col == 0, at_col == col_count - 1
    is_even = lax.rem(at_col, 2) == 0
    from_left[0:240, :] = jnp.where(is_even, odd_in[0:240, :], even_in[0:240, :])
    from_right[0:240, :] = jnp.where(is_even, even_in[0:240, :], odd_in[0:240, :])
    from_left[240:248, :] = jnp.where(is_even, odd_slots[...], even_in[240:248, :])
    from_right[240:248, :] = jnp.where(is_even, even_in[240:248, :], odd_slots[...])
    lane = lax.broadcasted_iota(jnp.int32, (8, LANES), 1)
    lane88 = lax.broadcasted_iota(jnp.int32, (88, LANES), 1)
    lane72 = lax.broadcasted_iota(jnp.int32, (72, LANES), 1)
    lane168 = lax.broadcasted_iota(jnp.int32, (168, LANES), 1)
    for i in range(4):
        rim = pltpu.roll(from_left[0:88, :], 96 - 32 * i, 1)
        fb[88 * i : 88 * i + 88, :] = jnp.where((lane88 >= 96) & jnp.logical_not(leftmost), rim, 0.0)
        near = pltpu.roll(from_right[168:240, :], (128 - 32 * i) % 128, 1)
        pb[72 * i : 72 * i + 72, :] = jnp.where((lane72 < 32) & jnp.logical_not(rightmost), near, 0.0)
    for i in range(2):
        rows = slice(8 + 168 * i, 176 + 168 * i)
        near = from_right[0:168, :] if i == 0 else pltpu.roll(from_right[0:168, :], 64, 1)
        fb[rows, :] = jnp.where((lane168 < 64) & jnp.logical_not(rightmost), near, fb[rows, :])
    is_row = lax.broadcasted_iota(jnp.int32, (8, LANES), 0) < 2
    cand = jnp.full((8, LANES), DEAD, F32)
    tile = 0
    for dc in (0, -1, 1):
        for n, dr in enumerate((0, -1, 1)):
            if dc == 0:
                block = infos[8 * n : 8 * n + 8, :]
            elif dc == -1:
                block = jnp.where(leftmost, DEAD, pltpu.roll(from_left[240:248, :], (128 - 32 * n) % 128, 1))
            else:
                block = jnp.where(rightmost, DEAD, pltpu.roll(from_right[240:248, :], (128 - 32 * n) % 128, 1))
            block = block + jnp.where(is_row, float(TILE_R * dr), float(LANES * dc))
            here = (lane // 16 == tile // 2) & (lax.rem(lane, 4) // 2 == tile % 2)
            cand = jnp.where(here, pltpu.roll(block, 16 * (tile // 2) + 2 * (tile % 2), 1), cand)
            tile += 1
    sub_f = lax.broadcasted_iota(jnp.int32, (128, LANES), 0).astype(F32)
    lane_f = lax.broadcasted_iota(jnp.int32, (128, LANES), 1).astype(F32)
    lane1 = lax.broadcasted_iota(jnp.int32, (1, LANES), 1)
    upright = cand.T
    columns = [jnp.broadcast_to(upright[:, 2 + h : 3 + h], (128, LANES)) for h in range(2)]
    for k in range(SLOTS):
        half = (k % 4) // 2
        row0, col0 = infos[0:1, k : k + 1] - 64.0, infos[2:3, k : k + 1] - 64.0
        p = jnp.where(lax.rem(lane1, 2) == k % 2, cand[half : half + 1] - row0, -1.0)
        at_row = (sub_f == p).astype(F32).astype(BF)
        at_col = jnp.where(lane_f + col0 == columns[half], 64.0, 0.0).astype(BF)
        comb[k // 2, :, 128 * (k % 2) : 128 * (k % 2) + 128] = dot(at_row, at_col).astype(BF)
    for k in range(0, SLOTS, 2):
        t = halves(dot(bands[...], comb[k // 2]), 0)
        for m in range(2):
            hi, lo = split(t[:, 128 * m : 128 * m + 128])
            y2[pl.ds((k + m) * 112, 112), :] = jnp.concatenate([hi, lo], 1)
    for copy in scalar_copies:
        copy.wait()
    for k in range(SLOTS):
        rows = pl.ds(win_row[0, 0, k], 128)
        fw[k] = window(fa[rows, :], fb[rows, :], win_col[0, 0, k] - 32)
    first, n = 8, 112
    while True:
        o = halves(dot(y2[0 : SLOTS * n, :], col_band[...]), 1)
        o = o.reshape(SLOTS, n, 128) * fw[:, first : first + n, :]
        if n == PATCH:
            break
        hi, lo = split(o)
        both = jnp.concatenate([hi, lo], 1)
        m = n - 16
        band_hi, band_lo = bands[0:m, 0:n], bands[112 : 112 + m, 0:n]
        lhs = jnp.concatenate(
            [jnp.concatenate([band_hi, band_hi], 1), jnp.concatenate([band_lo, band_lo], 1)], 0
        )
        for k in range(0, SLOTS, 2):
            t = halves(dot(lhs, jnp.concatenate([both[k], both[k + 1]], 1)), 0)
            for i in range(2):
                hi, lo = split(t[:, 128 * i : 128 * i + 128])
                y2[pl.ds((k + i) * m, m), :] = jnp.concatenate([hi, lo], 1)
        first, n = first + 8, m

    def lane_transform(x):
        hi, lo = split(x)
        return split(halves(dot(jnp.concatenate([hi, lo], 1), tables[:, 0:256]), 1))

    ker_hi, ker_lo = lane_transform(o.reshape(SLOTS * PATCH, 128))
    for k in range(SLOTS):
        rows = pl.ds(win_row[0, 0, k], PATCH)
        z[pl.ds(k * PATCH, PATCH), :] = window(pa[rows, :], pb[rows, :], win_col[0, 0, k] - 32)
    win_hi, win_lo = lane_transform(z[...])
    left_half = lax.broadcasted_iota(jnp.int32, (PATCH, 128), 1) < 64
    sign = jnp.where(left_half, -1.0, 1.0)

    def pair(t):
        a, b = t[:64], pltpu.roll(t[64:], 64, 1) * sign
        return a + b, a - b

    def times(a, b):
        ar, br = pltpu.roll(a, 64, 1), pltpu.roll(b, 64, 1)
        return jnp.where(left_half, a, ar) * b + jnp.where(left_half, -ar, a) * br

    def spectrum(k):
        s = slice(PATCH * k, PATCH * k + PATCH)
        w = jnp.concatenate(
            [jnp.concatenate([ker_hi[s], win_hi[s]], 1), jnp.concatenate([ker_lo[s], win_lo[s]], 1)], 0
        )
        t = halves(dot(tables[:, 768:896], w), 0)
        k1, k2 = pair(t[:, :128])
        w1, w2 = pair(t[:, 128:])
        p1, p2 = times(k1, w1), times(k2, w2)
        return jnp.concatenate([p1 + p2, pltpu.roll((p1 - p2) * sign, 64, 1)], 0)

    for k in range(SLOTS):
        hi, lo = split(spectrum(k))
        spec[pl.ds(k * 128, 128), :] = jnp.concatenate([hi, lo], 1)
    for k in range(SLOTS):
        hi, lo = split(halves(dot(spec[k * 128 : k * 128 + 128, :], tables[:, 256:512]), 1))
        wide[k // 2, :, 128 * (k % 2) : 128 * (k % 2) + 128] = jnp.concatenate([hi, lo], 0)
    oa[...] = jnp.zeros_like(oa)
    ob[...] = jnp.zeros_like(ob)
    lane128 = lax.broadcasted_iota(jnp.int32, (128, LANES), 1)
    for k in range(0, SLOTS, 2):
        t = halves(dot(tables[:, 512:768], wide[k // 2]), 0)
        for m in range(2):
            kk = k + m
            col = win_col[0, 0, kk]
            live = jnp.where(kk < live_count[0, 0], 1.0, 0.0)
            patch = pltpu.roll(t[:, 128 * m : 128 * m + 128] * live, col, 1)
            rows = pl.ds(win_row[0, 0, kk], 128)
            oa[rows, :] += jnp.where(lane128 >= col, patch, 0.0)
            ob[rows, :] += jnp.where(lane128 < col, patch, 0.0)
    at_row, row_count = own_index("mx")
    inner = at_row < row_count - 1
    own[...] = oa[0:TILE_R, :]
    own_low[...] = jnp.where(inner, oa[TILE_R:OUT_R, :], 0.0)
    side_low[...] = jnp.where(inner & jnp.logical_not(rightmost), ob[TILE_R:OUT_R, :], 0.0)
    free = lax.broadcasted_iota(jnp.int32, (64, LANES), 1) >= 96
    for i in range(3):
        rows = slice(64 * i, 64 * i + 64)
        piece = jnp.where(free, pltpu.roll(ob[192:256, :], 96 - 32 * i, 1), ob[rows, :])
        side[rows, :] = jnp.where(rightmost, 0.0, piece)


def peek_kernel(payload, slots):
    slots[...] = payload[payload.shape[0] - 8 :, :]


def add_side_kernel(own, spill, total):
    lane = lax.broadcasted_iota(jnp.int32, (64, LANES), 1)
    last = jnp.zeros((64, LANES), F32)
    for i in range(3):
        rows = slice(64 * i, 64 * i + 64)
        total[rows, :] = own[rows, :] + jnp.where(lane < 96, spill[rows, :], 0.0)
        last = jnp.where(lane // 32 == i, pltpu.roll(spill[rows, :], (32 + 32 * i) % 128, 1), last)
    total[192:256, :] = own[192:256, :] + last


def shape(rows, dtype=F32, cols=LANES):
    return jax.ShapeDtypeStruct((rows, cols), dtype)


def ring(x, axis, by):
    count = lax.axis_size(axis)
    return lax.ppermute(x, axis, [(i, (i + by) % count) for i in range(count)])


def swap(x, axis, odd):
    rows, cols = lax.axis_size("mx"), lax.axis_size("my")
    pairs = []
    for i in range(rows):
        for j in range(cols):
            if axis == "my":
                k = ((j + 1) ^ 1) - 1 if odd else j ^ 1
                to = (i, k) if 0 <= k < cols else (i ^ 1, j)
            else:
                k = ((i + 1) ^ 1) - 1 if odd else i ^ 1
                to = (k, j) if 0 <= k < rows else (i, j ^ 1)
            pairs.append((i * cols + j, to[0] * cols + to[1]))
    return lax.ppermute(x, ("mx", "my"), pairs)


def diagonal(x):
    rows, cols = lax.axis_size("mx"), lax.axis_size("my")
    pairs = [(i * cols + j, (i + 1) % rows * cols + (j + 1) % cols) for i in range(rows) for j in range(cols)]
    return lax.ppermute(x, ("mx", "my"), pairs)


def core_call(win_row, win_col, live_count, fa, pa, infos, even_in, odd_in, odd_slots, bands, col_band, tables):
    return pl.pallas_call(
        core_kernel,
        out_shape=[shape(TILE_R), shape(OUT_R - TILE_R), shape(192), shape(OUT_R - TILE_R)],
        in_specs=[ANY] * 3 + [VMEM] * 9,
        out_specs=[VMEM] * 4,
        scratch_shapes=[
            pltpu.VMEM((OUT_R, LANES), F32),
            pltpu.VMEM((OUT_R, LANES), F32),
            pltpu.VMEM((EXT_F, LANES), F32),
            pltpu.VMEM((EXT_P, LANES), F32),
            pltpu.VMEM((SLOTS, 128, LANES), F32),
            pltpu.VMEM((SLOTS * 112, 256), BF),
            pltpu.VMEM((SLOTS * PATCH, LANES), F32),
            pltpu.VMEM((SLOTS // 2, 128, 256), BF),
            pltpu.VMEM((SLOTS * 128, 256), BF),
            pltpu.VMEM((SLOTS // 2, 256, 256), BF),
            pltpu.SMEM((1, 1, SLOTS), jnp.int32),
            pltpu.SMEM((1, 1, SLOTS), jnp.int32),
            pltpu.SMEM((1, 1), jnp.int32),
            pltpu.VMEM((248, LANES), F32),
            pltpu.VMEM((248, LANES), F32),
            pltpu.SemaphoreType.DMA((4,)),
        ],
        compiler_params=pltpu.CompilerParams(vmem_limit_bytes=40 * 2**20),
    )(
        win_row, win_col, live_count, fa, pa, infos, even_in, odd_in, odd_slots, bands, col_band, tables,
    )


def peek(payload, params):
    return pl.pallas_call(
        peek_kernel,
        out_shape=shape(8),
        in_specs=[VMEM],
        out_specs=VMEM,
        compiler_params=params,
    )(payload)


def per_device(friction, taps_row, taps_col, probe, win_row, win_col, live_count):
    params = pltpu.CompilerParams(vmem_limit_bytes=40 * 2**20)
    row_even_out, row_odd_out = pl.pallas_call(
        pack_rows_kernel,
        out_shape=[shape(104), shape(104)],
        in_specs=[ANY] * 5,
        out_specs=[VMEM] * 2,
        scratch_shapes=[
            pltpu.VMEM((1, SLOTS), jnp.int32),
            pltpu.VMEM((1, SLOTS), jnp.int32),
            pltpu.VMEM((1, 1), jnp.int32),
            pltpu.SemaphoreType.DMA((6,)),
        ],
        compiler_params=pltpu.CompilerParams(vmem_limit_bytes=55040 * 2**10),
    )(win_row, win_col, live_count, friction, probe)
    row_odd = swap(row_odd_out, "mx", True)
    row_even = swap(row_even_out, "mx", False)
    fa, pa = pl.pallas_call(
        fetch_kernel,
        out_shape=[shape(EXT_F), shape(EXT_P)],
        in_specs=[ANY] * 2,
        out_specs=[VMEM] * 2,
        scratch_shapes=[pltpu.SemaphoreType.DMA((2,))],
        compiler_params=params,
    )(friction, probe)
    bands, col_band, tables = pl.pallas_call(
        bands_kernel,
        out_shape=[shape(224, BF), shape(256, BF, 256), shape(256, BF, 896)],
        in_specs=[SMEM] * 2 + [ANY],
        out_specs=[VMEM] * 3,
        scratch_shapes=[pltpu.SemaphoreType.DMA],
        compiler_params=params,
    )(taps_row, taps_col, jnp.asarray(transform_tables()))
    fa, pa, infos, even_out, odd_out = pl.pallas_call(
        pack_cols_kernel,
        out_shape=[shape(EXT_F), shape(EXT_P), shape(24), shape(248), shape(248)],
        in_specs=[VMEM] * 6,
        out_specs=[VMEM] * 5,
        input_output_aliases={0: 0, 1: 1},
        compiler_params=params,
    )(fa, pa, row_even_out, row_even, row_odd, peek(row_odd, params))
    odd_in = swap(odd_out, "my", True)
    even_in = swap(even_out, "my", False)
    own, own_low, side, side_low = core_call(
        win_row, win_col, live_count, fa, pa, infos, even_in, odd_in, peek(odd_in, params), bands, col_band, tables
    )
    spill = ring(side, "my", 1)
    corner = diagonal(side_low)
    lower = ring(own_low, "mx", 1)
    total = pl.pallas_call(
        add_side_kernel,
        out_shape=shape(TILE_R),
        in_specs=[VMEM] * 2,
        out_specs=VMEM,
        compiler_params=params,
    )(own, spill)
    below = ((0, TILE_R - corner.shape[0]), (0, 0))
    total = lax.optimization_barrier(total + jnp.pad(corner, below))
    return total + jnp.pad(lower, below)


def solution(mesh):
    placed = (
        P("mx", "my"),
        P(),
        P(),
        P("mx", "my"),
        P("mx", "my", None),
        P("mx", "my", None),
        P("mx", "my"),
    )
    return jax.shard_map(
        per_device, mesh=mesh, in_specs=placed, out_specs=P("mx", "my"), check_vma=False
    )
```

```python
import ml_dtypes
import numpy as np

import jax
import jax.numpy as jnp
from jax import lax
from jax.experimental import pallas as pl
from jax.experimental.pallas import tpu as pltpu
from jax.sharding import PartitionSpec as P

SLOTS = 16
PATCH = 64
TILE_R = 256
LANES = 128
UP = 32
DOWN = 64
EXT_F = UP + TILE_R + DOWN
EXT_P = TILE_R + 32
OUT_R = TILE_R + 96
DEAD = -1.0e6
BF = jnp.bfloat16
F32 = jnp.float32
VMEM = pl.BlockSpec(memory_space=pltpu.VMEM)
SMEM = pl.BlockSpec(memory_space=pltpu.SMEM)
ANY = pl.BlockSpec(memory_space=pltpu.HBM)


def split(x):
    hi = x.astype(BF)
    return hi, (x - hi.astype(F32)).astype(BF)


def dot(a, b):
    return jnp.dot(a, b, preferred_element_type=F32)


def halves(x, axis):
    n = x.shape[axis] // 2
    return lax.slice_in_dim(x, 0, n, axis=axis) + lax.slice_in_dim(x, n, 2 * n, axis=axis)


def np_split(x):
    hi = x.astype(ml_dtypes.bfloat16)
    return hi, (x - hi.astype(np.float64)).astype(ml_dtypes.bfloat16)


def transform_tables():
    theta = np.pi * (2 * np.arange(64) + 1) / 128
    short = np.outer(np.arange(64), theta)
    forward = np.concatenate([np.cos(short), np.sin(short)], 1)
    wide = np.zeros((128, 128))
    wide[32:96] = forward
    full = np.outer(theta, np.arange(128))
    inverse = np.concatenate([np.cos(full), np.sin(full)], 0) / 64
    lane_half = inverse / 2
    hi, lo = np_split(wide)
    lane_fwd = np.block([[hi, lo], [hi, lo]])
    hi, lo = np_split(forward.T)
    row_fwd = np.block([[hi, hi], [lo, lo]])
    hi, lo = np_split(lane_half)
    lane_inv = np.block([[hi, lo], [hi, lo]])
    hi, lo = np_split(inverse.T)
    row_inv = np.block([[hi, hi], [lo, lo]])
    return np.concatenate([lane_fwd, lane_inv, row_inv, row_fwd], 1)


def bands_kernel(taps_row, taps_col, tables_in, row_out, col_out, tables, sem):
    table_copy = pltpu.make_async_copy(tables_in, tables, sem)
    table_copy.start()
    gap = lax.broadcasted_iota(jnp.int32, (112, 128), 1) - lax.broadcasted_iota(jnp.int32, (112, 128), 0)
    band = jnp.zeros((112, 128), F32)
    for t in range(17):
        band = jnp.where(gap == t, taps_row[t], band)
    hi, lo = split(band)
    row_out[0:112, :] = hi
    row_out[112:224, :] = lo
    gap = lax.broadcasted_iota(jnp.int32, (128, 128), 0) - lax.broadcasted_iota(jnp.int32, (128, 128), 1) + 8
    band = jnp.zeros((128, 128), F32)
    for t in range(17):
        band = jnp.where(gap == t, taps_col[t], band)
    hi, lo = split(band)
    pair = jnp.concatenate([hi, lo], 1)
    col_out[...] = jnp.concatenate([pair, pair], 0)
    table_copy.wait()


def own_index(axis):
    return lax.axis_index(axis), lax.axis_size(axis)


def pack_rows_kernel(win_row, win_col, live_count, friction, probe, even_out, odd_out, rows, cols, count, sems):
    def fetch(down, up):
        return [
            pltpu.make_async_copy(friction.at[pl.ds(TILE_R - UP, UP)], down.at[pl.ds(0, UP)], sems.at[3]),
            pltpu.make_async_copy(friction.at[pl.ds(0, DOWN)], up.at[pl.ds(0, DOWN)], sems.at[4]),
            pltpu.make_async_copy(probe.at[pl.ds(0, 32)], up.at[pl.ds(DOWN, 32)], sems.at[5]),
        ]

    is_even = lax.rem(lax.axis_index("mx"), 2) == 0

    @pl.when(is_even)
    def _():
        for copy in fetch(even_out, odd_out):
            copy.start()

    @pl.when(jnp.logical_not(is_even))
    def _():
        for copy in fetch(odd_out, even_out):
            copy.start()

    copies = [
        pltpu.make_async_copy(win_row.at[0], rows, sems.at[0]),
        pltpu.make_async_copy(win_col.at[0], cols, sems.at[1]),
        pltpu.make_async_copy(live_count, count, sems.at[2]),
    ]
    for copy in copies:
        copy.start()
    for copy in copies:
        copy.wait()
    lane = lax.broadcasted_iota(jnp.int32, (1, SLOTS), 1)
    live = lane < count[...]
    row = jnp.where(live, rows[...].astype(F32), DEAD)
    col = cols[...].astype(F32)
    wide = jnp.concatenate([jnp.concatenate([x, jnp.zeros((1, LANES - SLOTS), F32)], 1) for x in (row, col)], 0)
    turned = pltpu.roll(wide, LANES - 2, 1)
    info = jnp.concatenate([wide[0:1], turned[0:1], wide[1:2], turned[1:2], jnp.zeros((4, LANES), F32)], 0)
    even_out[96:104, :] = info
    odd_out[96:104, :] = info
    for copy in fetch(even_out, odd_out):
        copy.wait()


def fetch_kernel(friction, probe, fa, pa, sems):
    copies = [
        pltpu.make_async_copy(friction, fa.at[pl.ds(UP, TILE_R)], sems.at[0]),
        pltpu.make_async_copy(probe, pa.at[pl.ds(0, TILE_R)], sems.at[1]),
    ]
    for copy in copies:
        copy.start()
    for copy in copies:
        copy.wait()


def pack_cols_kernel(fa_in, pa_in, mine, row_even, row_odd, odd_slots, fa, pa, infos, even_out, odd_out):
    at, count = own_index("mx")
    top, bottom = at == 0, at == count - 1
    is_even = lax.rem(at, 2) == 0
    above = jnp.where(is_even, row_odd[...], row_even[...])
    below = jnp.where(is_even, row_even[...], row_odd[...])
    fa[0:UP, :] = jnp.where(top, 0.0, above[0:UP])
    fa[UP + TILE_R : EXT_F, :] = jnp.where(bottom, 0.0, below[0:DOWN])
    pa[TILE_R:EXT_P, :] = jnp.where(bottom, 0.0, below[DOWN : DOWN + 32])
    infos[0:8, :] = mine[96:104, :]
    infos[8:16, :] = jnp.where(top, DEAD, jnp.where(is_even, odd_slots[...], row_even[96:104, :]))
    infos[16:24, :] = jnp.where(bottom, DEAD, jnp.where(is_even, row_even[96:104, :], odd_slots[...]))

    def packed(ref, rows, width, start, first=0):
        count = LANES // width
        part = rows // count
        lane = lax.broadcasted_iota(jnp.int32, (part, LANES), 1) // width
        total = jnp.zeros((part, LANES), F32)
        for i in range(count):
            piece = pltpu.roll(ref[first + i * part : first + (i + 1) * part, :], (width * i - start) % LANES, 1)
            total = jnp.where(lane == i, piece, total)
        return total

    def fill(right, left):
        right[0:88, :] = packed(fa, EXT_F, 32, 96)
        left[0:168, :] = packed(fa, EXT_F - 16, 64, 0, 8)
        left[168:240, :] = packed(pa, EXT_P, 32, 0)
        third = lax.broadcasted_iota(jnp.int32, (8, LANES), 1) // 32
        both = jnp.where(third == 1, pltpu.roll(infos[8:16, :], 32, 1), pltpu.roll(infos[16:24, :], 64, 1))
        both = jnp.where(third == 0, infos[0:8, :], both)
        right[240:248, :] = both
        left[240:248, :] = both

    is_even = lax.rem(lax.axis_index("my"), 2) == 0

    @pl.when(is_even)
    def _():
        fill(even_out, odd_out)

    @pl.when(jnp.logical_not(is_even))
    def _():
        fill(odd_out, even_out)


def window(a, b, start):
    turn = lax.rem(256 - start, 128)
    lane = lax.broadcasted_iota(jnp.int32, a.shape, 1) + start
    return jnp.where((lane >= 0) & (lane < LANES), pltpu.roll(a, turn, 1), pltpu.roll(b, turn, 1))


def core_kernel(
    win_row_in, win_col_in, live_in, fa, pa, infos, even_in, odd_in, odd_slots, bands, col_band, tables,
    own, own_low, side, side_low, oa, ob, fb, pb, fw, y2, z, comb, spec, wide, win_row, win_col, live_count, from_left, from_right, sems,
):
    scalar_copies = [
        pltpu.make_async_copy(win_row_in, win_row, sems.at[1]),
        pltpu.make_async_copy(win_col_in, win_col, sems.at[2]),
        pltpu.make_async_copy(live_in, live_count, sems.at[3]),
    ]
    for copy in scalar_copies:
        copy.start()
    at_col, col_count = own_index("my")
    leftmost, rightmost = at_col == 0, at_col == col_count - 1
    is_even = lax.rem(at_col, 2) == 0
    from_left[0:240, :] = jnp.where(is_even, odd_in[0:240, :], even_in[0:240, :])
    from_right[0:240, :] = jnp.where(is_even, even_in[0:240, :], odd_in[0:240, :])
    from_left[240:248, :] = jnp.where(is_even, odd_slots[...], even_in[240:248, :])
    from_right[240:248, :] = jnp.where(is_even, even_in[240:248, :], odd_slots[...])
    lane = lax.broadcasted_iota(jnp.int32, (8, LANES), 1)
    lane88 = lax.broadcasted_iota(jnp.int32, (88, LANES), 1)
    lane72 = lax.broadcasted_iota(jnp.int32, (72, LANES), 1)
    lane168 = lax.broadcasted_iota(jnp.int32, (168, LANES), 1)
    for i in range(4):
        rim = pltpu.roll(from_left[0:88, :], 96 - 32 * i, 1)
        fb[88 * i : 88 * i + 88, :] = jnp.where((lane88 >= 96) & jnp.logical_not(leftmost), rim, 0.0)
        near = pltpu.roll(from_right[168:240, :], (128 - 32 * i) % 128, 1)
        pb[72 * i : 72 * i + 72, :] = jnp.where((lane72 < 32) & jnp.logical_not(rightmost), near, 0.0)
    for i in range(2):
        rows = slice(8 + 168 * i, 176 + 168 * i)
        near = from_right[0:168, :] if i == 0 else pltpu.roll(from_right[0:168, :], 64, 1)
        fb[rows, :] = jnp.where((lane168 < 64) & jnp.logical_not(rightmost), near, fb[rows, :])
    is_row = lax.broadcasted_iota(jnp.int32, (8, LANES), 0) < 2
    cand = jnp.full((8, LANES), DEAD, F32)
    tile = 0
    for dc in (0, -1, 1):
        for n, dr in enumerate((0, -1, 1)):
            if dc == 0:
                block = infos[8 * n : 8 * n + 8, :]
            elif dc == -1:
                block = jnp.where(leftmost, DEAD, pltpu.roll(from_left[240:248, :], (128 - 32 * n) % 128, 1))
            else:
                block = jnp.where(rightmost, DEAD, pltpu.roll(from_right[240:248, :], (128 - 32 * n) % 128, 1))
            block = block + jnp.where(is_row, float(TILE_R * dr), float(LANES * dc))
            here = (lane // 16 == tile // 2) & (lax.rem(lane, 4) // 2 == tile % 2)
            cand = jnp.where(here, pltpu.roll(block, 16 * (tile // 2) + 2 * (tile % 2), 1), cand)
            tile += 1
    sub_f = lax.broadcasted_iota(jnp.int32, (128, LANES), 0).astype(F32)
    lane_f = lax.broadcasted_iota(jnp.int32, (128, LANES), 1).astype(F32)
    lane1 = lax.broadcasted_iota(jnp.int32, (1, LANES), 1)
    upright = cand.T
    columns = [jnp.broadcast_to(upright[:, 2 + h : 3 + h], (128, LANES)) for h in range(2)]
    for k in range(SLOTS):
        half = (k % 4) // 2
        row0, col0 = infos[0:1, k : k + 1] - 64.0, infos[2:3, k : k + 1] - 64.0
        p = jnp.where(lax.rem(lane1, 2) == k % 2, cand[half : half + 1] - row0, -1.0)
        at_row = (sub_f == p).astype(F32).astype(BF)
        at_col = jnp.where(lane_f + col0 == columns[half], 64.0, 0.0).astype(BF)
        comb[k // 2, :, 128 * (k % 2) : 128 * (k % 2) + 128] = dot(at_row, at_col).astype(BF)
    for k in range(0, SLOTS, 2):
        t = halves(dot(bands[...], comb[k // 2]), 0)
        for m in range(2):
            hi, lo = split(t[:, 128 * m : 128 * m + 128])
            y2[pl.ds((k + m) * 112, 112), :] = jnp.concatenate([hi, lo], 1)
    for copy in scalar_copies:
        copy.wait()
    for k in range(SLOTS):
        rows = pl.ds(win_row[0, 0, k], 128)
        fw[k] = window(fa[rows, :], fb[rows, :], win_col[0, 0, k] - 32)
    first, n = 8, 112
    while True:
        o = halves(dot(y2[0 : SLOTS * n, :], col_band[...]), 1)
        o = o.reshape(SLOTS, n, 128) * fw[:, first : first + n, :]
        if n == PATCH:
            break
        hi, lo = split(o)
        both = jnp.concatenate([hi, lo], 1)
        m = n - 16
        band_hi, band_lo = bands[0:m, 0:n], bands[112 : 112 + m, 0:n]
        lhs = jnp.concatenate(
            [jnp.concatenate([band_hi, band_hi], 1), jnp.concatenate([band_lo, band_lo], 1)], 0
        )
        for k in range(0, SLOTS, 2):
            t = halves(dot(lhs, jnp.concatenate([both[k], both[k + 1]], 1)), 0)
            for i in range(2):
                hi, lo = split(t[:, 128 * i : 128 * i + 128])
                y2[pl.ds((k + i) * m, m), :] = jnp.concatenate([hi, lo], 1)
        first, n = first + 8, m

    def lane_transform(x):
        hi, lo = split(x)
        return split(halves(dot(jnp.concatenate([hi, lo], 1), tables[:, 0:256]), 1))

    ker_hi, ker_lo = lane_transform(o.reshape(SLOTS * PATCH, 128))
    for k in range(SLOTS):
        rows = pl.ds(win_row[0, 0, k], PATCH)
        z[pl.ds(k * PATCH, PATCH), :] = window(pa[rows, :], pb[rows, :], win_col[0, 0, k] - 32)
    win_hi, win_lo = lane_transform(z[...])
    left_half = lax.broadcasted_iota(jnp.int32, (PATCH, 128), 1) < 64
    sign = jnp.where(left_half, -1.0, 1.0)

    def pair(t):
        a, b = t[:64], pltpu.roll(t[64:], 64, 1) * sign
        return a + b, a - b

    def times(a, b):
        ar, br = pltpu.roll(a, 64, 1), pltpu.roll(b, 64, 1)
        return jnp.where(left_half, a, ar) * b + jnp.where(left_half, -ar, a) * br

    def spectrum(k):
        s = slice(PATCH * k, PATCH * k + PATCH)
        w = jnp.concatenate(
            [jnp.concatenate([ker_hi[s], win_hi[s]], 1), jnp.concatenate([ker_lo[s], win_lo[s]], 1)], 0
        )
        t = halves(dot(tables[:, 768:896], w), 0)
        k1, k2 = pair(t[:, :128])
        w1, w2 = pair(t[:, 128:])
        p1, p2 = times(k1, w1), times(k2, w2)
        return jnp.concatenate([p1 + p2, pltpu.roll((p1 - p2) * sign, 64, 1)], 0)

    for k in range(SLOTS):
        hi, lo = split(spectrum(k))
        spec[pl.ds(k * 128, 128), :] = jnp.concatenate([hi, lo], 1)
    for k in range(SLOTS):
        hi, lo = split(halves(dot(spec[k * 128 : k * 128 + 128, :], tables[:, 256:512]), 1))
        wide[k // 2, :, 128 * (k % 2) : 128 * (k % 2) + 128] = jnp.concatenate([hi, lo], 0)
    oa[...] = jnp.zeros_like(oa)
    ob[...] = jnp.zeros_like(ob)
    lane128 = lax.broadcasted_iota(jnp.int32, (128, LANES), 1)
    for k in range(0, SLOTS, 2):
        t = halves(dot(tables[:, 512:768], wide[k // 2]), 0)
        for m in range(2):
            kk = k + m
            col = win_col[0, 0, kk]
            live = jnp.where(kk < live_count[0, 0], 1.0, 0.0)
            patch = pltpu.roll(t[:, 128 * m : 128 * m + 128] * live, col, 1)
            rows = pl.ds(win_row[0, 0, kk], 128)
            oa[rows, :] += jnp.where(lane128 >= col, patch, 0.0)
            ob[rows, :] += jnp.where(lane128 < col, patch, 0.0)
    at_row, row_count = own_index("mx")
    inner = at_row < row_count - 1
    own[...] = oa[0:TILE_R, :]
    own_low[...] = jnp.where(inner, oa[TILE_R:OUT_R, :], 0.0)
    side_low[...] = jnp.where(inner & jnp.logical_not(rightmost), ob[TILE_R:OUT_R, :], 0.0)
    free = lax.broadcasted_iota(jnp.int32, (64, LANES), 1) >= 96
    for i in range(3):
        rows = slice(64 * i, 64 * i + 64)
        piece = jnp.where(free, pltpu.roll(ob[192:256, :], 96 - 32 * i, 1), ob[rows, :])
        side[rows, :] = jnp.where(rightmost, 0.0, piece)


def peek_kernel(payload, slots):
    slots[...] = payload[payload.shape[0] - 8 :, :]


def add_side_kernel(own, spill, total):
    lane = lax.broadcasted_iota(jnp.int32, (64, LANES), 1)
    last = jnp.zeros((64, LANES), F32)
    for i in range(3):
        rows = slice(64 * i, 64 * i + 64)
        total[rows, :] = own[rows, :] + jnp.where(lane < 96, spill[rows, :], 0.0)
        last = jnp.where(lane // 32 == i, pltpu.roll(spill[rows, :], (32 + 32 * i) % 128, 1), last)
    total[192:256, :] = own[192:256, :] + last


def shape(rows, dtype=F32, cols=LANES):
    return jax.ShapeDtypeStruct((rows, cols), dtype)


def ring(x, axis, by):
    count = lax.axis_size(axis)
    return lax.ppermute(x, axis, [(i, (i + by) % count) for i in range(count)])


def swap(x, axis, odd):
    rows, cols = lax.axis_size("mx"), lax.axis_size("my")
    pairs = []
    for i in range(rows):
        for j in range(cols):
            if axis == "my":
                k = ((j + 1) ^ 1) - 1 if odd else j ^ 1
                to = (i, k) if 0 <= k < cols else (i ^ 1, j)
            else:
                k = ((i + 1) ^ 1) - 1 if odd else i ^ 1
                to = (k, j) if 0 <= k < rows else (i, j ^ 1)
            pairs.append((i * cols + j, to[0] * cols + to[1]))
    return lax.ppermute(x, ("mx", "my"), pairs)


def diagonal(x):
    rows, cols = lax.axis_size("mx"), lax.axis_size("my")
    pairs = []
    for i in range(rows):
        for j in range(cols):
            to = (i + 1, (j + 1) % cols) if i + 1 < rows else (0, j)
            pairs.append((i * cols + j, to[0] * cols + to[1]))
    return lax.ppermute(x, ("mx", "my"), pairs)


def core_call(win_row, win_col, live_count, fa, pa, infos, even_in, odd_in, odd_slots, bands, col_band, tables):
    return pl.pallas_call(
        core_kernel,
        out_shape=[shape(TILE_R), shape(OUT_R - TILE_R), shape(192), shape(OUT_R - TILE_R)],
        in_specs=[ANY] * 3 + [VMEM] * 9,
        out_specs=[VMEM] * 4,
        scratch_shapes=[
            pltpu.VMEM((OUT_R, LANES), F32),
            pltpu.VMEM((OUT_R, LANES), F32),
            pltpu.VMEM((EXT_F, LANES), F32),
            pltpu.VMEM((EXT_P, LANES), F32),
            pltpu.VMEM((SLOTS, 128, LANES), F32),
            pltpu.VMEM((SLOTS * 112, 256), BF),
            pltpu.VMEM((SLOTS * PATCH, LANES), F32),
            pltpu.VMEM((SLOTS // 2, 128, 256), BF),
            pltpu.VMEM((SLOTS * 128, 256), BF),
            pltpu.VMEM((SLOTS // 2, 256, 256), BF),
            pltpu.SMEM((1, 1, SLOTS), jnp.int32),
            pltpu.SMEM((1, 1, SLOTS), jnp.int32),
            pltpu.SMEM((1, 1), jnp.int32),
            pltpu.VMEM((248, LANES), F32),
            pltpu.VMEM((248, LANES), F32),
            pltpu.SemaphoreType.DMA((4,)),
        ],
        compiler_params=pltpu.CompilerParams(vmem_limit_bytes=40 * 2**20),
    )(
        win_row, win_col, live_count, fa, pa, infos, even_in, odd_in, odd_slots, bands, col_band, tables,
    )


def peek(payload, params):
    return pl.pallas_call(
        peek_kernel,
        out_shape=shape(8),
        in_specs=[VMEM],
        out_specs=VMEM,
        compiler_params=params,
    )(payload)


def per_device(friction, taps_row, taps_col, probe, win_row, win_col, live_count):
    params = pltpu.CompilerParams(vmem_limit_bytes=40 * 2**20)
    row_even_out, row_odd_out = pl.pallas_call(
        pack_rows_kernel,
        out_shape=[shape(104), shape(104)],
        in_specs=[ANY] * 5,
        out_specs=[VMEM] * 2,
        scratch_shapes=[
            pltpu.VMEM((1, SLOTS), jnp.int32),
            pltpu.VMEM((1, SLOTS), jnp.int32),
            pltpu.VMEM((1, 1), jnp.int32),
            pltpu.SemaphoreType.DMA((6,)),
        ],
        compiler_params=pltpu.CompilerParams(vmem_limit_bytes=55040 * 2**10),
    )(win_row, win_col, live_count, friction, probe)
    row_odd = swap(row_odd_out, "mx", True)
    row_even = swap(row_even_out, "mx", False)
    fa, pa = pl.pallas_call(
        fetch_kernel,
        out_shape=[shape(EXT_F), shape(EXT_P)],
        in_specs=[ANY] * 2,
        out_specs=[VMEM] * 2,
        scratch_shapes=[pltpu.SemaphoreType.DMA((2,))],
        compiler_params=params,
    )(friction, probe)
    bands, col_band, tables = pl.pallas_call(
        bands_kernel,
        out_shape=[shape(224, BF), shape(256, BF, 256), shape(256, BF, 896)],
        in_specs=[SMEM] * 2 + [ANY],
        out_specs=[VMEM] * 3,
        scratch_shapes=[pltpu.SemaphoreType.DMA],
        compiler_params=params,
    )(taps_row, taps_col, jnp.asarray(transform_tables()))
    fa, pa, infos, even_out, odd_out = pl.pallas_call(
        pack_cols_kernel,
        out_shape=[shape(EXT_F), shape(EXT_P), shape(24), shape(248), shape(248)],
        in_specs=[VMEM] * 6,
        out_specs=[VMEM] * 5,
        input_output_aliases={0: 0, 1: 1},
        compiler_params=params,
    )(fa, pa, row_even_out, row_even, row_odd, peek(row_odd, params))
    odd_in = swap(odd_out, "my", True)
    even_in = swap(even_out, "my", False)
    own, own_low, side, side_low = core_call(
        win_row, win_col, live_count, fa, pa, infos, even_in, odd_in, peek(odd_in, params), bands, col_band, tables
    )
    spill = ring(side, "my", 1)
    corner = diagonal(side_low)
    lower = ring(own_low, "mx", 1)
    total = pl.pallas_call(
        add_side_kernel,
        out_shape=shape(TILE_R),
        in_specs=[VMEM] * 2,
        out_specs=VMEM,
        compiler_params=params,
    )(own, spill)
    below = ((0, TILE_R - corner.shape[0]), (0, 0))
    total = lax.optimization_barrier(total + jnp.pad(corner, below))
    return total + jnp.pad(lower, below)


def solution(mesh):
    placed = (
        P("mx", "my"),
        P(),
        P(),
        P("mx", "my"),
        P("mx", "my", None),
        P("mx", "my", None),
        P("mx", "my"),
    )
    return jax.shard_map(
        per_device, mesh=mesh, in_specs=placed, out_specs=P("mx", "my"), check_vma=False
    )
```

```python
import ml_dtypes
import numpy as np

import jax
import jax.numpy as jnp
from jax import lax
from jax.experimental import pallas as pl
from jax.experimental.pallas import tpu as pltpu
from jax.sharding import PartitionSpec as P

SLOTS = 16
PATCH = 64
TILE_R = 256
LANES = 128
UP = 32
DOWN = 64
EXT_F = UP + TILE_R + DOWN
EXT_P = TILE_R + 32
OUT_R = TILE_R + 96
DEAD = -1.0e6
BF = jnp.bfloat16
F32 = jnp.float32
VMEM = pl.BlockSpec(memory_space=pltpu.VMEM)
SMEM = pl.BlockSpec(memory_space=pltpu.SMEM)
ANY = pl.BlockSpec(memory_space=pltpu.HBM)


def split(x):
    hi = x.astype(BF)
    return hi, (x - hi.astype(F32)).astype(BF)


def dot(a, b):
    return jnp.dot(a, b, preferred_element_type=F32)


def halves(x, axis):
    n = x.shape[axis] // 2
    return lax.slice_in_dim(x, 0, n, axis=axis) + lax.slice_in_dim(x, n, 2 * n, axis=axis)


def np_split(x):
    hi = x.astype(ml_dtypes.bfloat16)
    return hi, (x - hi.astype(np.float64)).astype(ml_dtypes.bfloat16)


def transform_tables():
    theta = np.pi * (2 * np.arange(64) + 1) / 128
    short = np.outer(np.arange(64), theta)
    forward = np.concatenate([np.cos(short), np.sin(short)], 1)
    wide = np.zeros((128, 128))
    wide[32:96] = forward
    full = np.outer(theta, np.arange(128))
    inverse = np.concatenate([np.cos(full), np.sin(full)], 0) / 64
    lane_half = inverse / 2
    hi, lo = np_split(wide)
    lane_fwd = np.block([[hi, lo], [hi, lo]])
    hi, lo = np_split(forward.T)
    row_fwd = np.block([[hi, hi], [lo, lo]])
    hi, lo = np_split(lane_half)
    lane_inv = np.block([[hi, lo], [hi, lo]])
    hi, lo = np_split(inverse.T)
    row_inv = np.block([[hi, hi], [lo, lo]])
    return np.concatenate([lane_fwd, lane_inv, row_inv, row_fwd], 1)


def bands_kernel(taps_row, taps_col, tables_in, row_out, col_out, tables, sem):
    table_copy = pltpu.make_async_copy(tables_in, tables, sem)
    table_copy.start()
    gap = lax.broadcasted_iota(jnp.int32, (112, 128), 1) - lax.broadcasted_iota(jnp.int32, (112, 128), 0)
    band = jnp.zeros((112, 128), F32)
    for t in range(17):
        band = jnp.where(gap == t, taps_row[t], band)
    hi, lo = split(band)
    row_out[0:112, :] = hi
    row_out[112:224, :] = lo
    gap = lax.broadcasted_iota(jnp.int32, (128, 128), 0) - lax.broadcasted_iota(jnp.int32, (128, 128), 1) + 8
    band = jnp.zeros((128, 128), F32)
    for t in range(17):
        band = jnp.where(gap == t, taps_col[t], band)
    hi, lo = split(band)
    pair = jnp.concatenate([hi, lo], 1)
    col_out[...] = jnp.concatenate([pair, pair], 0)
    table_copy.wait()


def own_index(axis):
    return lax.axis_index(axis), lax.axis_size(axis)


def pack_rows_kernel(
    win_row, win_col, live_count, friction, probe, even_out, odd_out, scalars, rows, cols, count, sems
):
    def fetch(down, up):
        return [
            pltpu.make_async_copy(friction.at[pl.ds(TILE_R - UP, UP)], down.at[pl.ds(0, UP)], sems.at[3]),
            pltpu.make_async_copy(friction.at[pl.ds(0, DOWN)], up.at[pl.ds(0, DOWN)], sems.at[4]),
            pltpu.make_async_copy(probe.at[pl.ds(0, 32)], up.at[pl.ds(DOWN, 32)], sems.at[5]),
        ]

    is_even = lax.rem(lax.axis_index("mx"), 2) == 0

    @pl.when(is_even)
    def _():
        for copy in fetch(even_out, odd_out):
            copy.start()

    @pl.when(jnp.logical_not(is_even))
    def _():
        for copy in fetch(odd_out, even_out):
            copy.start()

    copies = [
        pltpu.make_async_copy(win_row.at[0], rows, sems.at[0]),
        pltpu.make_async_copy(win_col.at[0], cols, sems.at[1]),
        pltpu.make_async_copy(live_count, count, sems.at[2]),
    ]
    for copy in copies:
        copy.start()
    for copy in copies:
        copy.wait()
    lane = lax.broadcasted_iota(jnp.int32, (1, SLOTS), 1)
    live = lane < count[...]
    row = jnp.where(live, rows[...].astype(F32), DEAD)
    col = cols[...].astype(F32)
    wide = jnp.concatenate([jnp.concatenate([x, jnp.zeros((1, LANES - SLOTS), F32)], 1) for x in (row, col)], 0)
    turned = pltpu.roll(wide, LANES - 2, 1)
    info = jnp.concatenate([wide[0:1], turned[0:1], wide[1:2], turned[1:2], jnp.zeros((4, LANES), F32)], 0)
    none = jnp.zeros((1, LANES - SLOTS), jnp.int32)
    many = jnp.broadcast_to(count[...], (1, SLOTS))
    whole = [jnp.concatenate([x, none], 1) for x in (rows[...], cols[...], many)]
    scalars[...] = jnp.concatenate(whole + [jnp.zeros((5, LANES), jnp.int32)], 0)
    even_out[96:104, :] = info
    odd_out[96:104, :] = info
    for copy in fetch(even_out, odd_out):
        copy.wait()


def fetch_kernel(friction, probe, fa, pa, sems):
    copies = [
        pltpu.make_async_copy(friction, fa.at[pl.ds(UP, TILE_R)], sems.at[0]),
        pltpu.make_async_copy(probe, pa.at[pl.ds(0, TILE_R)], sems.at[1]),
    ]
    for copy in copies:
        copy.start()
    for copy in copies:
        copy.wait()


def pack_cols_kernel(fa_in, pa_in, mine, row_even, row_odd, odd_slots, fa, pa, infos, even_out, odd_out):
    at, count = own_index("mx")
    top, bottom = at == 0, at == count - 1
    is_even = lax.rem(at, 2) == 0
    above = jnp.where(is_even, row_odd[...], row_even[...])
    below = jnp.where(is_even, row_even[...], row_odd[...])
    fa[0:UP, :] = jnp.where(top, 0.0, above[0:UP])
    fa[UP + TILE_R : EXT_F, :] = jnp.where(bottom, 0.0, below[0:DOWN])
    pa[TILE_R:EXT_P, :] = jnp.where(bottom, 0.0, below[DOWN : DOWN + 32])
    infos[0:8, :] = mine[96:104, :]
    infos[8:16, :] = jnp.where(top, DEAD, jnp.where(is_even, odd_slots[...], row_even[96:104, :]))
    infos[16:24, :] = jnp.where(bottom, DEAD, jnp.where(is_even, row_even[96:104, :], odd_slots[...]))

    def packed(ref, rows, width, start, first=0):
        count = LANES // width
        part = rows // count
        lane = lax.broadcasted_iota(jnp.int32, (part, LANES), 1) // width
        total = jnp.zeros((part, LANES), F32)
        for i in range(count):
            piece = pltpu.roll(ref[first + i * part : first + (i + 1) * part, :], (width * i - start) % LANES, 1)
            total = jnp.where(lane == i, piece, total)
        return total

    def fill(right, left):
        right[0:88, :] = packed(fa, EXT_F, 32, 96)
        left[0:168, :] = packed(fa, EXT_F - 16, 64, 0, 8)
        left[168:240, :] = packed(pa, EXT_P, 32, 0)
        third = lax.broadcasted_iota(jnp.int32, (8, LANES), 1) // 32
        both = jnp.where(third == 1, pltpu.roll(infos[8:16, :], 32, 1), pltpu.roll(infos[16:24, :], 64, 1))
        both = jnp.where(third == 0, infos[0:8, :], both)
        right[240:248, :] = both
        left[240:248, :] = both

    is_even = lax.rem(lax.axis_index("my"), 2) == 0

    @pl.when(is_even)
    def _():
        fill(even_out, odd_out)

    @pl.when(jnp.logical_not(is_even))
    def _():
        fill(odd_out, even_out)


def window(a, b, start):
    turn = lax.rem(256 - start, 128)
    lane = lax.broadcasted_iota(jnp.int32, a.shape, 1) + start
    return jnp.where((lane >= 0) & (lane < LANES), pltpu.roll(a, turn, 1), pltpu.roll(b, turn, 1))


def core_kernel(
    scalars_in, fa, pa, infos, even_in, odd_in, odd_slots, bands, col_band, tables,
    own, own_low, side, side_low, oa, ob, fb, pb, fw, y2, z, comb, spec, wide, scalars, from_left, from_right, sem,
):
    scalar_copy = pltpu.make_async_copy(scalars_in, scalars, sem)
    scalar_copy.start()
    at_col, col_count = own_index("my")
    leftmost, rightmost = at_col == 0, at_col == col_count - 1
    is_even = lax.rem(at_col, 2) == 0
    from_left[0:240, :] = jnp.where(is_even, odd_in[0:240, :], even_in[0:240, :])
    from_right[0:240, :] = jnp.where(is_even, even_in[0:240, :], odd_in[0:240, :])
    from_left[240:248, :] = jnp.where(is_even, odd_slots[...], even_in[240:248, :])
    from_right[240:248, :] = jnp.where(is_even, even_in[240:248, :], odd_slots[...])
    lane = lax.broadcasted_iota(jnp.int32, (8, LANES), 1)
    lane88 = lax.broadcasted_iota(jnp.int32, (88, LANES), 1)
    lane72 = lax.broadcasted_iota(jnp.int32, (72, LANES), 1)
    lane168 = lax.broadcasted_iota(jnp.int32, (168, LANES), 1)
    for i in range(4):
        rim = pltpu.roll(from_left[0:88, :], 96 - 32 * i, 1)
        fb[88 * i : 88 * i + 88, :] = jnp.where((lane88 >= 96) & jnp.logical_not(leftmost), rim, 0.0)
        near = pltpu.roll(from_right[168:240, :], (128 - 32 * i) % 128, 1)
        pb[72 * i : 72 * i + 72, :] = jnp.where((lane72 < 32) & jnp.logical_not(rightmost), near, 0.0)
    for i in range(2):
        rows = slice(8 + 168 * i, 176 + 168 * i)
        near = from_right[0:168, :] if i == 0 else pltpu.roll(from_right[0:168, :], 64, 1)
        fb[rows, :] = jnp.where((lane168 < 64) & jnp.logical_not(rightmost), near, fb[rows, :])
    is_row = lax.broadcasted_iota(jnp.int32, (8, LANES), 0) < 2
    cand = jnp.full((8, LANES), DEAD, F32)
    tile = 0
    for dc in (0, -1, 1):
        for n, dr in enumerate((0, -1, 1)):
            if dc == 0:
                block = infos[8 * n : 8 * n + 8, :]
            elif dc == -1:
                block = jnp.where(leftmost, DEAD, pltpu.roll(from_left[240:248, :], (128 - 32 * n) % 128, 1))
            else:
                block = jnp.where(rightmost, DEAD, pltpu.roll(from_right[240:248, :], (128 - 32 * n) % 128, 1))
            block = block + jnp.where(is_row, float(TILE_R * dr), float(LANES * dc))
            here = (lane // 16 == tile // 2) & (lax.rem(lane, 4) // 2 == tile % 2)
            cand = jnp.where(here, pltpu.roll(block, 16 * (tile // 2) + 2 * (tile % 2), 1), cand)
            tile += 1
    sub_f = lax.broadcasted_iota(jnp.int32, (128, LANES), 0).astype(F32)
    lane_f = lax.broadcasted_iota(jnp.int32, (128, LANES), 1).astype(F32)
    lane1 = lax.broadcasted_iota(jnp.int32, (1, LANES), 1)
    upright = cand.T
    columns = [jnp.broadcast_to(upright[:, 2 + h : 3 + h], (128, LANES)) for h in range(2)]
    for k in range(SLOTS):
        half = (k % 4) // 2
        row0, col0 = infos[0:1, k : k + 1] - 64.0, infos[2:3, k : k + 1] - 64.0
        p = jnp.where(lax.rem(lane1, 2) == k % 2, cand[half : half + 1] - row0, -1.0)
        at_row = (sub_f == p).astype(F32).astype(BF)
        at_col = jnp.where(lane_f + col0 == columns[half], 64.0, 0.0).astype(BF)
        comb[k // 2, :, 128 * (k % 2) : 128 * (k % 2) + 128] = dot(at_row, at_col).astype(BF)
    for k in range(0, SLOTS, 2):
        t = halves(dot(bands[...], comb[k // 2]), 0)
        for m in range(2):
            hi, lo = split(t[:, 128 * m : 128 * m + 128])
            y2[pl.ds((k + m) * 112, 112), :] = jnp.concatenate([hi, lo], 1)
    scalar_copy.wait()
    for k in range(SLOTS):
        rows = pl.ds(scalars[0, k], 128)
        fw[k] = window(fa[rows, :], fb[rows, :], scalars[1, k] - 32)
    first, n = 8, 112
    while True:
        o = halves(dot(y2[0 : SLOTS * n, :], col_band[...]), 1)
        o = o.reshape(SLOTS, n, 128) * fw[:, first : first + n, :]
        if n == PATCH:
            break
        hi, lo = split(o)
        both = jnp.concatenate([hi, lo], 1)
        m = n - 16
        band_hi, band_lo = bands[0:m, 0:n], bands[112 : 112 + m, 0:n]
        lhs = jnp.concatenate(
            [jnp.concatenate([band_hi, band_hi], 1), jnp.concatenate([band_lo, band_lo], 1)], 0
        )
        for k in range(0, SLOTS, 2):
            t = halves(dot(lhs, jnp.concatenate([both[k], both[k + 1]], 1)), 0)
            for i in range(2):
                hi, lo = split(t[:, 128 * i : 128 * i + 128])
                y2[pl.ds((k + i) * m, m), :] = jnp.concatenate([hi, lo], 1)
        first, n = first + 8, m

    def lane_transform(x):
        hi, lo = split(x)
        return split(halves(dot(jnp.concatenate([hi, lo], 1), tables[:, 0:256]), 1))

    ker_hi, ker_lo = lane_transform(o.reshape(SLOTS * PATCH, 128))
    for k in range(SLOTS):
        rows = pl.ds(scalars[0, k], PATCH)
        z[pl.ds(k * PATCH, PATCH), :] = window(pa[rows, :], pb[rows, :], scalars[1, k] - 32)
    win_hi, win_lo = lane_transform(z[...])
    left_half = lax.broadcasted_iota(jnp.int32, (PATCH, 128), 1) < 64
    sign = jnp.where(left_half, -1.0, 1.0)

    def pair(t):
        a, b = t[:64], pltpu.roll(t[64:], 64, 1) * sign
        return a + b, a - b

    def times(a, b):
        ar, br = pltpu.roll(a, 64, 1), pltpu.roll(b, 64, 1)
        return jnp.where(left_half, a, ar) * b + jnp.where(left_half, -ar, a) * br

    def spectrum(k):
        s = slice(PATCH * k, PATCH * k + PATCH)
        w = jnp.concatenate(
            [jnp.concatenate([ker_hi[s], win_hi[s]], 1), jnp.concatenate([ker_lo[s], win_lo[s]], 1)], 0
        )
        t = halves(dot(tables[:, 768:896], w), 0)
        k1, k2 = pair(t[:, :128])
        w1, w2 = pair(t[:, 128:])
        p1, p2 = times(k1, w1), times(k2, w2)
        return jnp.concatenate([p1 + p2, pltpu.roll((p1 - p2) * sign, 64, 1)], 0)

    for k in range(SLOTS):
        hi, lo = split(spectrum(k))
        spec[pl.ds(k * 128, 128), :] = jnp.concatenate([hi, lo], 1)
    for k in range(SLOTS):
        hi, lo = split(halves(dot(spec[k * 128 : k * 128 + 128, :], tables[:, 256:512]), 1))
        wide[k // 2, :, 128 * (k % 2) : 128 * (k % 2) + 128] = jnp.concatenate([hi, lo], 0)
    oa[...] = jnp.zeros_like(oa)
    ob[...] = jnp.zeros_like(ob)
    lane128 = lax.broadcasted_iota(jnp.int32, (128, LANES), 1)
    for k in range(0, SLOTS, 2):
        t = halves(dot(tables[:, 512:768], wide[k // 2]), 0)
        for m in range(2):
            kk = k + m
            col = scalars[1, kk]
            live = jnp.where(kk < scalars[2, 0], 1.0, 0.0)
            patch = pltpu.roll(t[:, 128 * m : 128 * m + 128] * live, col, 1)
            rows = pl.ds(scalars[0, kk], 128)
            oa[rows, :] += jnp.where(lane128 >= col, patch, 0.0)
            ob[rows, :] += jnp.where(lane128 < col, patch, 0.0)
    at_row, row_count = own_index("mx")
    inner = at_row < row_count - 1
    own[...] = oa[0:TILE_R, :]
    own_low[...] = jnp.where(inner, oa[TILE_R:OUT_R, :], 0.0)
    side_low[...] = jnp.where(inner & jnp.logical_not(rightmost), ob[TILE_R:OUT_R, :], 0.0)
    free = lax.broadcasted_iota(jnp.int32, (64, LANES), 1) >= 96
    for i in range(3):
        rows = slice(64 * i, 64 * i + 64)
        piece = jnp.where(free, pltpu.roll(ob[192:256, :], 96 - 32 * i, 1), ob[rows, :])
        side[rows, :] = jnp.where(rightmost, 0.0, piece)


def peek_kernel(payload, slots):
    slots[...] = payload[payload.shape[0] - 8 :, :]


def add_side_kernel(own, spill, total):
    lane = lax.broadcasted_iota(jnp.int32, (64, LANES), 1)
    last = jnp.zeros((64, LANES), F32)
    for i in range(3):
        rows = slice(64 * i, 64 * i + 64)
        total[rows, :] = own[rows, :] + jnp.where(lane < 96, spill[rows, :], 0.0)
        last = jnp.where(lane // 32 == i, pltpu.roll(spill[rows, :], (32 + 32 * i) % 128, 1), last)
    total[192:256, :] = own[192:256, :] + last


def shape(rows, dtype=F32, cols=LANES):
    return jax.ShapeDtypeStruct((rows, cols), dtype)


def ring(x, axis, by):
    count = lax.axis_size(axis)
    return lax.ppermute(x, axis, [(i, (i + by) % count) for i in range(count)])


def swap(x, axis, odd):
    rows, cols = lax.axis_size("mx"), lax.axis_size("my")
    pairs = []
    for i in range(rows):
        for j in range(cols):
            if axis == "my":
                k = ((j + 1) ^ 1) - 1 if odd else j ^ 1
                to = (i, k) if 0 <= k < cols else (i ^ 1, j)
            else:
                k = ((i + 1) ^ 1) - 1 if odd else i ^ 1
                to = (k, j) if 0 <= k < rows else (i, j ^ 1)
            pairs.append((i * cols + j, to[0] * cols + to[1]))
    return lax.ppermute(x, ("mx", "my"), pairs)


def diagonal(x):
    rows, cols = lax.axis_size("mx"), lax.axis_size("my")
    pairs = []
    for i in range(rows):
        for j in range(cols):
            to = (i + 1, (j + 1) % cols) if i + 1 < rows else (0, j)
            pairs.append((i * cols + j, to[0] * cols + to[1]))
    return lax.ppermute(x, ("mx", "my"), pairs)


def core_call(scalars, fa, pa, infos, even_in, odd_in, odd_slots, bands, col_band, tables):
    return pl.pallas_call(
        core_kernel,
        out_shape=[shape(TILE_R), shape(OUT_R - TILE_R), shape(192), shape(OUT_R - TILE_R)],
        in_specs=[VMEM] * 10,
        out_specs=[VMEM] * 4,
        scratch_shapes=[
            pltpu.VMEM((OUT_R, LANES), F32),
            pltpu.VMEM((OUT_R, LANES), F32),
            pltpu.VMEM((EXT_F, LANES), F32),
            pltpu.VMEM((EXT_P, LANES), F32),
            pltpu.VMEM((SLOTS, 128, LANES), F32),
            pltpu.VMEM((SLOTS * 112, 256), BF),
            pltpu.VMEM((SLOTS * PATCH, LANES), F32),
            pltpu.VMEM((SLOTS // 2, 128, 256), BF),
            pltpu.VMEM((SLOTS * 128, 256), BF),
            pltpu.VMEM((SLOTS // 2, 256, 256), BF),
            pltpu.SMEM((8, LANES), jnp.int32),
            pltpu.VMEM((248, LANES), F32),
            pltpu.VMEM((248, LANES), F32),
            pltpu.SemaphoreType.DMA,
        ],
        compiler_params=pltpu.CompilerParams(vmem_limit_bytes=40 * 2**20),
    )(
        scalars, fa, pa, infos, even_in, odd_in, odd_slots, bands, col_band, tables,
    )


def peek(payload, params):
    return pl.pallas_call(
        peek_kernel,
        out_shape=shape(8),
        in_specs=[VMEM],
        out_specs=VMEM,
        compiler_params=params,
    )(payload)


def per_device(friction, taps_row, taps_col, probe, win_row, win_col, live_count):
    params = pltpu.CompilerParams(vmem_limit_bytes=40 * 2**20)
    row_even_out, row_odd_out, scalars = pl.pallas_call(
        pack_rows_kernel,
        out_shape=[shape(104), shape(104), shape(8, jnp.int32)],
        in_specs=[ANY] * 5,
        out_specs=[VMEM] * 3,
        scratch_shapes=[
            pltpu.VMEM((1, SLOTS), jnp.int32),
            pltpu.VMEM((1, SLOTS), jnp.int32),
            pltpu.VMEM((1, 1), jnp.int32),
            pltpu.SemaphoreType.DMA((6,)),
        ],
        compiler_params=pltpu.CompilerParams(vmem_limit_bytes=55040 * 2**10),
    )(win_row, win_col, live_count, friction, probe)
    row_odd = swap(row_odd_out, "mx", True)
    row_even = swap(row_even_out, "mx", False)
    fa, pa = pl.pallas_call(
        fetch_kernel,
        out_shape=[shape(EXT_F), shape(EXT_P)],
        in_specs=[ANY] * 2,
        out_specs=[VMEM] * 2,
        scratch_shapes=[pltpu.SemaphoreType.DMA((2,))],
        compiler_params=params,
    )(friction, probe)
    bands, col_band, tables = pl.pallas_call(
        bands_kernel,
        out_shape=[shape(224, BF), shape(256, BF, 256), shape(256, BF, 896)],
        in_specs=[SMEM] * 2 + [ANY],
        out_specs=[VMEM] * 3,
        scratch_shapes=[pltpu.SemaphoreType.DMA],
        compiler_params=params,
    )(taps_row, taps_col, jnp.asarray(transform_tables()))
    fa, pa, infos, even_out, odd_out = pl.pallas_call(
        pack_cols_kernel,
        out_shape=[shape(EXT_F), shape(EXT_P), shape(24), shape(248), shape(248)],
        in_specs=[VMEM] * 6,
        out_specs=[VMEM] * 5,
        input_output_aliases={0: 0, 1: 1},
        compiler_params=params,
    )(fa, pa, row_even_out, row_even, row_odd, peek(row_odd, params))
    odd_in = swap(odd_out, "my", True)
    even_in = swap(even_out, "my", False)
    own, own_low, side, side_low = core_call(
        scalars, fa, pa, infos, even_in, odd_in, peek(odd_in, params), bands, col_band, tables
    )
    spill = ring(side, "my", 1)
    corner = diagonal(side_low)
    lower = ring(own_low, "mx", 1)
    total = pl.pallas_call(
        add_side_kernel,
        out_shape=shape(TILE_R),
        in_specs=[VMEM] * 2,
        out_specs=VMEM,
        compiler_params=params,
    )(own, spill)
    below = ((0, TILE_R - corner.shape[0]), (0, 0))
    total = lax.optimization_barrier(total + jnp.pad(corner, below))
    return total + jnp.pad(lower, below)


def solution(mesh):
    placed = (
        P("mx", "my"),
        P(),
        P(),
        P("mx", "my"),
        P("mx", "my", None),
        P("mx", "my", None),
        P("mx", "my"),
    )
    return jax.shard_map(
        per_device, mesh=mesh, in_specs=placed, out_specs=P("mx", "my"), check_vma=False
    )
```

```python
import ml_dtypes
import numpy as np

import jax
import jax.numpy as jnp
from jax import lax
from jax.experimental import pallas as pl
from jax.experimental.pallas import tpu as pltpu
from jax.sharding import PartitionSpec as P

SLOTS = 16
PATCH = 64
TILE_R = 256
LANES = 128
UP = 32
DOWN = 64
EXT_F = UP + TILE_R + DOWN
EXT_P = TILE_R + 32
OUT_R = TILE_R + 96
DEAD = -1.0e6
BF = jnp.bfloat16
F32 = jnp.float32
VMEM = pl.BlockSpec(memory_space=pltpu.VMEM)
SMEM = pl.BlockSpec(memory_space=pltpu.SMEM)
ANY = pl.BlockSpec(memory_space=pltpu.HBM)


def split(x):
    hi = x.astype(BF)
    return hi, (x - hi.astype(F32)).astype(BF)


def dot(a, b):
    return jnp.dot(a, b, preferred_element_type=F32)


def halves(x, axis):
    n = x.shape[axis] // 2
    return lax.slice_in_dim(x, 0, n, axis=axis) + lax.slice_in_dim(x, n, 2 * n, axis=axis)


def np_split(x):
    hi = x.astype(ml_dtypes.bfloat16)
    return hi, (x - hi.astype(np.float64)).astype(ml_dtypes.bfloat16)


def transform_tables():
    theta = np.pi * (2 * np.arange(64) + 1) / 128
    short = np.outer(np.arange(64), theta)
    forward = np.concatenate([np.cos(short), np.sin(short)], 1)
    wide = np.zeros((128, 128))
    wide[32:96] = forward
    full = np.outer(theta, np.arange(128))
    inverse = np.concatenate([np.cos(full), np.sin(full)], 0) / 64
    lane_half = inverse / 2
    hi, lo = np_split(wide)
    lane_fwd = np.block([[hi, lo], [hi, lo]])
    hi, lo = np_split(forward.T)
    row_fwd = np.block([[hi, hi], [lo, lo]])
    hi, lo = np_split(lane_half)
    lane_inv = np.block([[hi, lo], [hi, lo]])
    hi, lo = np_split(inverse.T)
    row_inv = np.block([[hi, hi], [lo, lo]])
    return np.concatenate([lane_fwd, lane_inv, row_inv, row_fwd], 1)


def bands_kernel(taps_row, taps_col, tables_in, row_out, col_out, tables, sem):
    table_copy = pltpu.make_async_copy(tables_in, tables, sem)
    table_copy.start()
    gap = lax.broadcasted_iota(jnp.int32, (112, 128), 1) - lax.broadcasted_iota(jnp.int32, (112, 128), 0)
    band = jnp.zeros((112, 128), F32)
    for t in range(17):
        band = jnp.where(gap == t, taps_row[t], band)
    hi, lo = split(band)
    row_out[0:112, :] = hi
    row_out[112:224, :] = lo
    gap = lax.broadcasted_iota(jnp.int32, (128, 128), 0) - lax.broadcasted_iota(jnp.int32, (128, 128), 1) + 8
    band = jnp.zeros((128, 128), F32)
    for t in range(17):
        band = jnp.where(gap == t, taps_col[t], band)
    hi, lo = split(band)
    pair = jnp.concatenate([hi, lo], 1)
    col_out[...] = jnp.concatenate([pair, pair], 0)
    table_copy.wait()


def own_index(axis):
    return lax.axis_index(axis), lax.axis_size(axis)


def pack_rows_kernel(
    win_row, win_col, live_count, friction, probe, even_out, odd_out, scalars, rows, cols, count, sems
):
    def fetch(down, up):
        return [
            pltpu.make_async_copy(friction.at[pl.ds(TILE_R - UP, UP)], down.at[pl.ds(0, UP)], sems.at[3]),
            pltpu.make_async_copy(friction.at[pl.ds(0, DOWN)], up.at[pl.ds(0, DOWN)], sems.at[4]),
            pltpu.make_async_copy(probe.at[pl.ds(0, 32)], up.at[pl.ds(DOWN, 32)], sems.at[5]),
        ]

    is_even = lax.rem(lax.axis_index("mx"), 2) == 0

    @pl.when(is_even)
    def _():
        for copy in fetch(even_out, odd_out):
            copy.start()

    @pl.when(jnp.logical_not(is_even))
    def _():
        for copy in fetch(odd_out, even_out):
            copy.start()

    copies = [
        pltpu.make_async_copy(win_row.at[0], rows, sems.at[0]),
        pltpu.make_async_copy(win_col.at[0], cols, sems.at[1]),
        pltpu.make_async_copy(live_count, count, sems.at[2]),
    ]
    for copy in copies:
        copy.start()
    for copy in copies:
        copy.wait()
    lane = lax.broadcasted_iota(jnp.int32, (1, SLOTS), 1)
    live = lane < count[...]
    row = jnp.where(live, rows[...].astype(F32), DEAD)
    col = cols[...].astype(F32)
    wide = jnp.concatenate([jnp.concatenate([x, jnp.zeros((1, LANES - SLOTS), F32)], 1) for x in (row, col)], 0)
    turned = pltpu.roll(wide, LANES - 2, 1)
    info = jnp.concatenate([wide[0:1], turned[0:1], wide[1:2], turned[1:2], jnp.zeros((4, LANES), F32)], 0)
    none = jnp.zeros((1, LANES - SLOTS), jnp.int32)
    many = jnp.broadcast_to(count[...], (1, SLOTS))
    whole = [jnp.concatenate([x, none], 1) for x in (rows[...], cols[...], many)]
    scalars[...] = jnp.concatenate(whole + [jnp.zeros((5, LANES), jnp.int32)], 0)
    even_out[96:104, :] = info
    odd_out[96:104, :] = info
    for copy in fetch(even_out, odd_out):
        copy.wait()


def fetch_kernel(friction, probe, fa, pa, sems):
    copies = [
        pltpu.make_async_copy(friction, fa.at[pl.ds(UP, TILE_R)], sems.at[0]),
        pltpu.make_async_copy(probe, pa.at[pl.ds(0, TILE_R)], sems.at[1]),
    ]
    for copy in copies:
        copy.start()
    for copy in copies:
        copy.wait()


def pack_cols_kernel(fa_in, pa_in, mine, row_even, row_odd, odd_slots, fa, pa, infos, even_out, odd_out):
    at, count = own_index("mx")
    top, bottom = at == 0, at == count - 1
    is_even = lax.rem(at, 2) == 0
    above = jnp.where(is_even, row_odd[...], row_even[...])
    below = jnp.where(is_even, row_even[...], row_odd[...])
    fa[0:UP, :] = jnp.where(top, 0.0, above[0:UP])
    fa[UP + TILE_R : EXT_F, :] = jnp.where(bottom, 0.0, below[0:DOWN])
    pa[TILE_R:EXT_P, :] = jnp.where(bottom, 0.0, below[DOWN : DOWN + 32])
    infos[0:8, :] = mine[96:104, :]
    infos[8:16, :] = jnp.where(top, DEAD, jnp.where(is_even, odd_slots[...], row_even[96:104, :]))
    infos[16:24, :] = jnp.where(bottom, DEAD, jnp.where(is_even, row_even[96:104, :], odd_slots[...]))

    def packed(ref, rows, width, start, first=0):
        count = LANES // width
        part = rows // count
        lane = lax.broadcasted_iota(jnp.int32, (part, LANES), 1) // width
        total = jnp.zeros((part, LANES), F32)
        for i in range(count):
            piece = pltpu.roll(ref[first + i * part : first + (i + 1) * part, :], (width * i - start) % LANES, 1)
            total = jnp.where(lane == i, piece, total)
        return total

    def fill(right, left):
        right[0:88, :] = packed(fa, EXT_F, 32, 96)
        left[0:168, :] = packed(fa, EXT_F - 16, 64, 0, 8)
        left[168:240, :] = packed(pa, EXT_P, 32, 0)
        third = lax.broadcasted_iota(jnp.int32, (8, LANES), 1) // 32
        both = jnp.where(third == 1, pltpu.roll(infos[8:16, :], 32, 1), pltpu.roll(infos[16:24, :], 64, 1))
        both = jnp.where(third == 0, infos[0:8, :], both)
        right[240:248, :] = both
        left[240:248, :] = both

    is_even = lax.rem(lax.axis_index("my"), 2) == 0

    @pl.when(is_even)
    def _():
        fill(even_out, odd_out)

    @pl.when(jnp.logical_not(is_even))
    def _():
        fill(odd_out, even_out)


def window(a, b, start):
    turn = lax.rem(256 - start, 128)
    lane = lax.broadcasted_iota(jnp.int32, a.shape, 1) + start
    return jnp.where((lane >= 0) & (lane < LANES), pltpu.roll(a, turn, 1), pltpu.roll(b, turn, 1))


def core_kernel(
    scalars_in, fa, pa, infos, even_in, odd_in, odd_slots, bands, col_band, tables,
    own, own_low, side, side_low, oa, ob, fb, pb, fw, y2, z, comb, spec, wide, scalars, from_left, from_right, sem,
):
    scalar_copy = pltpu.make_async_copy(scalars_in, scalars, sem)
    scalar_copy.start()
    at_col, col_count = own_index("my")
    leftmost, rightmost = at_col == 0, at_col == col_count - 1
    is_even = lax.rem(at_col, 2) == 0
    from_left[0:240, :] = jnp.where(is_even, odd_in[0:240, :], even_in[0:240, :])
    from_right[0:240, :] = jnp.where(is_even, even_in[0:240, :], odd_in[0:240, :])
    from_left[240:248, :] = jnp.where(is_even, odd_slots[...], even_in[240:248, :])
    from_right[240:248, :] = jnp.where(is_even, even_in[240:248, :], odd_slots[...])
    lane = lax.broadcasted_iota(jnp.int32, (8, LANES), 1)
    lane88 = lax.broadcasted_iota(jnp.int32, (88, LANES), 1)
    lane72 = lax.broadcasted_iota(jnp.int32, (72, LANES), 1)
    lane168 = lax.broadcasted_iota(jnp.int32, (168, LANES), 1)
    for i in range(4):
        rim = pltpu.roll(from_left[0:88, :], 96 - 32 * i, 1)
        fb[88 * i : 88 * i + 88, :] = jnp.where((lane88 >= 96) & jnp.logical_not(leftmost), rim, 0.0)
        near = pltpu.roll(from_right[168:240, :], (128 - 32 * i) % 128, 1)
        pb[72 * i : 72 * i + 72, :] = jnp.where((lane72 < 32) & jnp.logical_not(rightmost), near, 0.0)
    for i in range(2):
        rows = slice(8 + 168 * i, 176 + 168 * i)
        near = from_right[0:168, :] if i == 0 else pltpu.roll(from_right[0:168, :], 64, 1)
        fb[rows, :] = jnp.where((lane168 < 64) & jnp.logical_not(rightmost), near, fb[rows, :])
    is_row = lax.broadcasted_iota(jnp.int32, (8, LANES), 0) < 2
    cand = jnp.full((8, LANES), DEAD, F32)
    tile = 0
    for dc in (0, -1, 1):
        for n, dr in enumerate((0, -1, 1)):
            if dc == 0:
                block = infos[8 * n : 8 * n + 8, :]
            elif dc == -1:
                block = jnp.where(leftmost, DEAD, pltpu.roll(from_left[240:248, :], (128 - 32 * n) % 128, 1))
            else:
                block = jnp.where(rightmost, DEAD, pltpu.roll(from_right[240:248, :], (128 - 32 * n) % 128, 1))
            block = block + jnp.where(is_row, float(TILE_R * dr), float(LANES * dc))
            here = (lane // 16 == tile // 2) & (lax.rem(lane, 4) // 2 == tile % 2)
            cand = jnp.where(here, pltpu.roll(block, 16 * (tile // 2) + 2 * (tile % 2), 1), cand)
            tile += 1
    sub_f = lax.broadcasted_iota(jnp.int32, (128, LANES), 0).astype(F32)
    lane_f = lax.broadcasted_iota(jnp.int32, (128, LANES), 1).astype(F32)
    lane1 = lax.broadcasted_iota(jnp.int32, (1, LANES), 1)
    upright = cand.T
    columns = [jnp.broadcast_to(upright[:, 2 + h : 3 + h], (128, LANES)) for h in range(2)]
    for k in range(SLOTS):
        half = (k % 4) // 2
        row0, col0 = infos[0:1, k : k + 1] - 64.0, infos[2:3, k : k + 1] - 64.0
        p = jnp.where(lax.rem(lane1, 2) == k % 2, cand[half : half + 1] - row0, -1.0)
        at_row = (sub_f == p).astype(F32).astype(BF)
        at_col = jnp.where(lane_f + col0 == columns[half], 64.0, 0.0).astype(BF)
        comb[k // 2, :, 128 * (k % 2) : 128 * (k % 2) + 128] = dot(at_row, at_col).astype(BF)
    for k in range(0, SLOTS, 2):
        t = halves(dot(bands[...], comb[k // 2]), 0)
        for m in range(2):
            hi, lo = split(t[:, 128 * m : 128 * m + 128])
            y2[pl.ds((k + m) * 112, 112), :] = jnp.concatenate([hi, lo], 1)
    scalar_copy.wait()
    for k in range(SLOTS):
        rows = pl.ds(scalars[0, k], 128)
        fw[k] = window(fa[rows, :], fb[rows, :], scalars[1, k] - 32)
    first, n = 8, 112
    while True:
        o = halves(dot(y2[0 : SLOTS * n, :], col_band[...]), 1)
        o = o.reshape(SLOTS, n, 128) * fw[:, first : first + n, :]
        if n == PATCH:
            break
        hi, lo = split(o)
        both = jnp.concatenate([hi, lo], 1)
        m = n - 16
        band_hi, band_lo = bands[0:m, 0:n], bands[112 : 112 + m, 0:n]
        lhs = jnp.concatenate(
            [jnp.concatenate([band_hi, band_hi], 1), jnp.concatenate([band_lo, band_lo], 1)], 0
        )
        for k in range(0, SLOTS, 2):
            t = halves(dot(lhs, jnp.concatenate([both[k], both[k + 1]], 1)), 0)
            for i in range(2):
                hi, lo = split(t[:, 128 * i : 128 * i + 128])
                y2[pl.ds((k + i) * m, m), :] = jnp.concatenate([hi, lo], 1)
        first, n = first + 8, m

    def lane_transform(x):
        hi, lo = split(x)
        return split(halves(dot(jnp.concatenate([hi, lo], 1), tables[:, 0:256]), 1))

    ker_hi, ker_lo = lane_transform(o.reshape(SLOTS * PATCH, 128))
    for k in range(SLOTS):
        rows = pl.ds(scalars[0, k], PATCH)
        z[pl.ds(k * PATCH, PATCH), :] = window(pa[rows, :], pb[rows, :], scalars[1, k] - 32)
    win_hi, win_lo = lane_transform(z[...])
    left_half = lax.broadcasted_iota(jnp.int32, (PATCH, 128), 1) < 64
    sign = jnp.where(left_half, -1.0, 1.0)

    def pair(t):
        a, b = t[:64], pltpu.roll(t[64:], 64, 1) * sign
        return a + b, a - b

    def times(a, b):
        ar, br = pltpu.roll(a, 64, 1), pltpu.roll(b, 64, 1)
        return jnp.where(left_half, a, ar) * b + jnp.where(left_half, -ar, a) * br

    def spectrum(k):
        s = slice(PATCH * k, PATCH * k + PATCH)
        w = jnp.concatenate(
            [jnp.concatenate([ker_hi[s], win_hi[s]], 1), jnp.concatenate([ker_lo[s], win_lo[s]], 1)], 0
        )
        t = halves(dot(tables[:, 768:896], w), 0)
        k1, k2 = pair(t[:, :128])
        w1, w2 = pair(t[:, 128:])
        p1, p2 = times(k1, w1), times(k2, w2)
        return jnp.concatenate([p1 + p2, pltpu.roll((p1 - p2) * sign, 64, 1)], 0)

    for k in range(SLOTS):
        hi, lo = split(spectrum(k))
        spec[pl.ds(k * 128, 128), :] = jnp.concatenate([hi, lo], 1)
    for k in range(SLOTS):
        hi, lo = split(halves(dot(spec[k * 128 : k * 128 + 128, :], tables[:, 256:512]), 1))
        wide[k // 2, :, 128 * (k % 2) : 128 * (k % 2) + 128] = jnp.concatenate([hi, lo], 0)
    oa[...] = jnp.zeros_like(oa)
    ob[...] = jnp.zeros_like(ob)
    lane128 = lax.broadcasted_iota(jnp.int32, (128, LANES), 1)
    for k in range(0, SLOTS, 2):
        t = halves(dot(tables[:, 512:768], wide[k // 2]), 0)
        for m in range(2):
            kk = k + m
            col = scalars[1, kk]
            live = jnp.where(kk < scalars[2, 0], 1.0, 0.0)
            patch = pltpu.roll(t[:, 128 * m : 128 * m + 128] * live, col, 1)
            rows = pl.ds(scalars[0, kk], 128)
            oa[rows, :] += jnp.where(lane128 >= col, patch, 0.0)
            ob[rows, :] += jnp.where(lane128 < col, patch, 0.0)
    at_row, row_count = own_index("mx")
    inner = at_row < row_count - 1
    own[...] = oa[0:TILE_R, :]
    own_low[...] = jnp.where(inner, oa[TILE_R:OUT_R, :], 0.0)
    free = lax.broadcasted_iota(jnp.int32, (24, LANES), 1) >= 96
    for i in range(3):
        rest = pltpu.roll(ob[TILE_R + 72 : OUT_R, :], 96 - 32 * i, 1)
        piece = jnp.where(free, rest, ob[TILE_R + 24 * i : TILE_R + 24 * i + 24, :])
        side_low[24 * i : 24 * i + 24, :] = jnp.where(inner & jnp.logical_not(rightmost), piece, 0.0)
    free = lax.broadcasted_iota(jnp.int32, (64, LANES), 1) >= 96
    for i in range(3):
        rows = slice(64 * i, 64 * i + 64)
        piece = jnp.where(free, pltpu.roll(ob[192:256, :], 96 - 32 * i, 1), ob[rows, :])
        side[rows, :] = jnp.where(rightmost, 0.0, piece)


def peek_kernel(payload, slots):
    slots[...] = payload[payload.shape[0] - 8 :, :]


def add_low_kernel(own, corner, total):
    lane = lax.broadcasted_iota(jnp.int32, (24, LANES), 1)
    last = jnp.zeros((24, LANES), F32)
    for i in range(3):
        rows = slice(24 * i, 24 * i + 24)
        total[rows, :] = own[rows, :] + jnp.where(lane < 96, corner[rows, :], 0.0)
        last = jnp.where(lane // 32 == i, pltpu.roll(corner[rows, :], (32 + 32 * i) % 128, 1), last)
    total[72:96, :] = own[72:96, :] + last
    total[96:TILE_R, :] = own[96:TILE_R, :]


def add_side_kernel(own, spill, total):
    lane = lax.broadcasted_iota(jnp.int32, (64, LANES), 1)
    last = jnp.zeros((64, LANES), F32)
    for i in range(3):
        rows = slice(64 * i, 64 * i + 64)
        total[rows, :] = own[rows, :] + jnp.where(lane < 96, spill[rows, :], 0.0)
        last = jnp.where(lane // 32 == i, pltpu.roll(spill[rows, :], (32 + 32 * i) % 128, 1), last)
    total[192:256, :] = own[192:256, :] + last


def shape(rows, dtype=F32, cols=LANES):
    return jax.ShapeDtypeStruct((rows, cols), dtype)


def ring(x, axis, by):
    count = lax.axis_size(axis)
    return lax.ppermute(x, axis, [(i, (i + by) % count) for i in range(count)])


def swap(x, axis, odd):
    rows, cols = lax.axis_size("mx"), lax.axis_size("my")
    pairs = []
    for i in range(rows):
        for j in range(cols):
            if axis == "my":
                k = ((j + 1) ^ 1) - 1 if odd else j ^ 1
                to = (i, k) if 0 <= k < cols else (i ^ 1, j)
            else:
                k = ((i + 1) ^ 1) - 1 if odd else i ^ 1
                to = (k, j) if 0 <= k < rows else (i, j ^ 1)
            pairs.append((i * cols + j, to[0] * cols + to[1]))
    return lax.ppermute(x, ("mx", "my"), pairs)


def diagonal(x):
    rows, cols = lax.axis_size("mx"), lax.axis_size("my")
    pairs = []
    for i in range(rows):
        for j in range(cols):
            to = (i + 1, (j + 1) % cols) if i + 1 < rows else (0, j)
            pairs.append((i * cols + j, to[0] * cols + to[1]))
    return lax.ppermute(x, ("mx", "my"), pairs)


def core_call(scalars, fa, pa, infos, even_in, odd_in, odd_slots, bands, col_band, tables):
    return pl.pallas_call(
        core_kernel,
        out_shape=[shape(TILE_R), shape(OUT_R - TILE_R), shape(192), shape(72)],
        in_specs=[VMEM] * 10,
        out_specs=[VMEM] * 4,
        scratch_shapes=[
            pltpu.VMEM((OUT_R, LANES), F32),
            pltpu.VMEM((OUT_R, LANES), F32),
            pltpu.VMEM((EXT_F, LANES), F32),
            pltpu.VMEM((EXT_P, LANES), F32),
            pltpu.VMEM((SLOTS, 128, LANES), F32),
            pltpu.VMEM((SLOTS * 112, 256), BF),
            pltpu.VMEM((SLOTS * PATCH, LANES), F32),
            pltpu.VMEM((SLOTS // 2, 128, 256), BF),
            pltpu.VMEM((SLOTS * 128, 256), BF),
            pltpu.VMEM((SLOTS // 2, 256, 256), BF),
            pltpu.SMEM((8, LANES), jnp.int32),
            pltpu.VMEM((248, LANES), F32),
            pltpu.VMEM((248, LANES), F32),
            pltpu.SemaphoreType.DMA,
        ],
        compiler_params=pltpu.CompilerParams(vmem_limit_bytes=40 * 2**20),
    )(
        scalars, fa, pa, infos, even_in, odd_in, odd_slots, bands, col_band, tables,
    )


def peek(payload, params):
    return pl.pallas_call(
        peek_kernel,
        out_shape=shape(8),
        in_specs=[VMEM],
        out_specs=VMEM,
        compiler_params=params,
    )(payload)


def per_device(friction, taps_row, taps_col, probe, win_row, win_col, live_count):
    params = pltpu.CompilerParams(vmem_limit_bytes=40 * 2**20)
    row_even_out, row_odd_out, scalars = pl.pallas_call(
        pack_rows_kernel,
        out_shape=[shape(104), shape(104), shape(8, jnp.int32)],
        in_specs=[ANY] * 5,
        out_specs=[VMEM] * 3,
        scratch_shapes=[
            pltpu.VMEM((1, SLOTS), jnp.int32),
            pltpu.VMEM((1, SLOTS), jnp.int32),
            pltpu.VMEM((1, 1), jnp.int32),
            pltpu.SemaphoreType.DMA((6,)),
        ],
        compiler_params=pltpu.CompilerParams(vmem_limit_bytes=55040 * 2**10),
    )(win_row, win_col, live_count, friction, probe)
    row_odd = swap(row_odd_out, "mx", True)
    row_even = swap(row_even_out, "mx", False)
    fa, pa = pl.pallas_call(
        fetch_kernel,
        out_shape=[shape(EXT_F), shape(EXT_P)],
        in_specs=[ANY] * 2,
        out_specs=[VMEM] * 2,
        scratch_shapes=[pltpu.SemaphoreType.DMA((2,))],
        compiler_params=params,
    )(friction, probe)
    bands, col_band, tables = pl.pallas_call(
        bands_kernel,
        out_shape=[shape(224, BF), shape(256, BF, 256), shape(256, BF, 896)],
        in_specs=[SMEM] * 2 + [ANY],
        out_specs=[VMEM] * 3,
        scratch_shapes=[pltpu.SemaphoreType.DMA],
        compiler_params=params,
    )(taps_row, taps_col, jnp.asarray(transform_tables()))
    fa, pa, infos, even_out, odd_out = pl.pallas_call(
        pack_cols_kernel,
        out_shape=[shape(EXT_F), shape(EXT_P), shape(24), shape(248), shape(248)],
        in_specs=[VMEM] * 6,
        out_specs=[VMEM] * 5,
        input_output_aliases={0: 0, 1: 1},
        compiler_params=params,
    )(fa, pa, row_even_out, row_even, row_odd, peek(row_odd, params))
    odd_in = swap(odd_out, "my", True)
    even_in = swap(even_out, "my", False)
    own, own_low, side, side_low = core_call(
        scalars, fa, pa, infos, even_in, odd_in, peek(odd_in, params), bands, col_band, tables
    )
    spill = ring(side, "my", 1)
    corner = diagonal(side_low)
    lower = ring(own_low, "mx", 1)
    below = ((0, TILE_R - lower.shape[0]), (0, 0))
    total = pl.pallas_call(
        add_side_kernel,
        out_shape=shape(TILE_R),
        in_specs=[VMEM] * 2,
        out_specs=VMEM,
        compiler_params=params,
    )(own, spill)
    total = pl.pallas_call(
        add_low_kernel,
        out_shape=shape(TILE_R),
        in_specs=[VMEM] * 2,
        out_specs=VMEM,
        compiler_params=params,
    )(total, corner)
    return total + jnp.pad(lower, below)


def solution(mesh):
    placed = (
        P("mx", "my"),
        P(),
        P(),
        P("mx", "my"),
        P("mx", "my", None),
        P("mx", "my", None),
        P("mx", "my"),
    )
    return jax.shard_map(
        per_device, mesh=mesh, in_specs=placed, out_specs=P("mx", "my"), check_vma=False
    )
```

```python
import ml_dtypes
import numpy as np

import jax
import jax.numpy as jnp
from jax import lax
from jax.experimental import pallas as pl
from jax.experimental.pallas import tpu as pltpu
from jax.sharding import PartitionSpec as P

SLOTS = 16
PATCH = 64
TILE_R = 256
LANES = 128
UP = 32
DOWN = 64
EXT_F = UP + TILE_R + DOWN
EXT_P = TILE_R + 32
OUT_R = TILE_R + 96
DEAD = -1.0e6
BF = jnp.bfloat16
F32 = jnp.float32
VMEM = pl.BlockSpec(memory_space=pltpu.VMEM)
SMEM = pl.BlockSpec(memory_space=pltpu.SMEM)
ANY = pl.BlockSpec(memory_space=pltpu.HBM)


def split(x):
    hi = x.astype(BF)
    return hi, (x - hi.astype(F32)).astype(BF)


def dot(a, b):
    return jnp.dot(a, b, preferred_element_type=F32)


def halves(x, axis):
    n = x.shape[axis] // 2
    return lax.slice_in_dim(x, 0, n, axis=axis) + lax.slice_in_dim(x, n, 2 * n, axis=axis)


def np_split(x):
    hi = x.astype(ml_dtypes.bfloat16)
    return hi, (x - hi.astype(np.float64)).astype(ml_dtypes.bfloat16)


def transform_tables():
    theta = np.pi * (2 * np.arange(64) + 1) / 128
    short = np.outer(np.arange(64), theta)
    forward = np.concatenate([np.cos(short), np.sin(short)], 1)
    wide = np.zeros((128, 128))
    wide[32:96] = forward
    full = np.outer(theta, np.arange(128))
    inverse = np.concatenate([np.cos(full), np.sin(full)], 0) / 64
    lane_half = inverse / 2
    hi, lo = np_split(wide)
    lane_fwd = np.block([[hi, lo], [hi, lo]])
    hi, lo = np_split(forward.T)
    row_fwd = np.block([[hi, hi], [lo, lo]])
    hi, lo = np_split(lane_half)
    lane_inv = np.block([[hi, lo], [hi, lo]])
    hi, lo = np_split(inverse.T)
    row_inv = np.block([[hi, hi], [lo, lo]])
    return np.concatenate([lane_fwd, lane_inv, row_inv, row_fwd], 1)


def bands_kernel(taps_row, taps_col, tables_in, row_out, col_out, tables, sem):
    table_copy = pltpu.make_async_copy(tables_in, tables, sem)
    table_copy.start()
    gap = lax.broadcasted_iota(jnp.int32, (112, 128), 1) - lax.broadcasted_iota(jnp.int32, (112, 128), 0)
    band = jnp.zeros((112, 128), F32)
    for t in range(17):
        band = jnp.where(gap == t, taps_row[t], band)
    hi, lo = split(band)
    row_out[0:112, :] = hi
    row_out[112:224, :] = lo
    gap = lax.broadcasted_iota(jnp.int32, (128, 128), 0) - lax.broadcasted_iota(jnp.int32, (128, 128), 1) + 8
    band = jnp.zeros((128, 128), F32)
    for t in range(17):
        band = jnp.where(gap == t, taps_col[t], band)
    hi, lo = split(band)
    pair = jnp.concatenate([hi, lo], 1)
    col_out[...] = jnp.concatenate([pair, pair], 0)
    table_copy.wait()


def own_index(axis):
    return lax.axis_index(axis), lax.axis_size(axis)


def pack_rows_kernel(
    win_row, win_col, live_count, friction, probe, even_out, odd_out, scalars, rows, cols, count, sems
):
    def fetch(down, up):
        return [
            pltpu.make_async_copy(friction.at[pl.ds(TILE_R - UP, UP)], down.at[pl.ds(0, UP)], sems.at[3]),
            pltpu.make_async_copy(friction.at[pl.ds(0, DOWN)], up.at[pl.ds(0, DOWN)], sems.at[4]),
            pltpu.make_async_copy(probe.at[pl.ds(0, 32)], up.at[pl.ds(DOWN, 32)], sems.at[5]),
        ]

    is_even = lax.rem(lax.axis_index("mx"), 2) == 0

    @pl.when(is_even)
    def _():
        for copy in fetch(even_out, odd_out):
            copy.start()

    @pl.when(jnp.logical_not(is_even))
    def _():
        for copy in fetch(odd_out, even_out):
            copy.start()

    copies = [
        pltpu.make_async_copy(win_row.at[0], rows, sems.at[0]),
        pltpu.make_async_copy(win_col.at[0], cols, sems.at[1]),
        pltpu.make_async_copy(live_count, count, sems.at[2]),
    ]
    for copy in copies:
        copy.start()
    for copy in copies:
        copy.wait()
    lane = lax.broadcasted_iota(jnp.int32, (1, SLOTS), 1)
    live = lane < count[...]
    row = jnp.where(live, rows[...].astype(F32), DEAD)
    col = cols[...].astype(F32)
    wide = jnp.concatenate([jnp.concatenate([x, jnp.zeros((1, LANES - SLOTS), F32)], 1) for x in (row, col)], 0)
    turned = pltpu.roll(wide, LANES - 2, 1)
    info = jnp.concatenate([wide[0:1], turned[0:1], wide[1:2], turned[1:2], jnp.zeros((4, LANES), F32)], 0)
    none = jnp.zeros((1, LANES - SLOTS), jnp.int32)
    many = jnp.broadcast_to(count[...], (1, SLOTS))
    whole = [jnp.concatenate([x, none], 1) for x in (rows[...], cols[...], many)]
    scalars[...] = jnp.concatenate(whole + [jnp.zeros((5, LANES), jnp.int32)], 0)
    even_out[96:104, :] = info
    odd_out[96:104, :] = info
    for copy in fetch(even_out, odd_out):
        copy.wait()


def fetch_kernel(friction, probe, fa, pa, sems):
    copies = [
        pltpu.make_async_copy(friction, fa.at[pl.ds(UP, TILE_R)], sems.at[0]),
        pltpu.make_async_copy(probe, pa.at[pl.ds(0, TILE_R)], sems.at[1]),
    ]
    for copy in copies:
        copy.start()
    for copy in copies:
        copy.wait()


def pack_cols_kernel(fa_in, pa_in, mine, row_even, row_odd, odd_slots, fa, pa, infos, even_out, odd_out):
    at, count = own_index("mx")
    top, bottom = at == 0, at == count - 1
    is_even = lax.rem(at, 2) == 0
    above = jnp.where(is_even, row_odd[...], row_even[...])
    below = jnp.where(is_even, row_even[...], row_odd[...])
    fa[0:UP, :] = jnp.where(top, 0.0, above[0:UP])
    fa[UP + TILE_R : EXT_F, :] = jnp.where(bottom, 0.0, below[0:DOWN])
    pa[TILE_R:EXT_P, :] = jnp.where(bottom, 0.0, below[DOWN : DOWN + 32])
    infos[0:8, :] = mine[96:104, :]
    infos[8:16, :] = jnp.where(top, DEAD, jnp.where(is_even, odd_slots[...], row_even[96:104, :]))
    infos[16:24, :] = jnp.where(bottom, DEAD, jnp.where(is_even, row_even[96:104, :], odd_slots[...]))

    def packed(ref, rows, width, start, first=0):
        count = LANES // width
        part = rows // count
        lane = lax.broadcasted_iota(jnp.int32, (part, LANES), 1) // width
        total = jnp.zeros((part, LANES), F32)
        for i in range(count):
            piece = pltpu.roll(ref[first + i * part : first + (i + 1) * part, :], (width * i - start) % LANES, 1)
            total = jnp.where(lane == i, piece, total)
        return total

    def fill(right, left):
        right[0:88, :] = packed(fa, EXT_F, 32, 96)
        left[0:168, :] = packed(fa, EXT_F - 16, 64, 0, 8)
        left[168:240, :] = packed(pa, EXT_P, 32, 0)
        third = lax.broadcasted_iota(jnp.int32, (8, LANES), 1) // 32
        both = jnp.where(third == 1, pltpu.roll(infos[8:16, :], 32, 1), pltpu.roll(infos[16:24, :], 64, 1))
        both = jnp.where(third == 0, infos[0:8, :], both)
        right[240:248, :] = both
        left[240:248, :] = both

    is_even = lax.rem(lax.axis_index("my"), 2) == 0

    @pl.when(is_even)
    def _():
        fill(even_out, odd_out)

    @pl.when(jnp.logical_not(is_even))
    def _():
        fill(odd_out, even_out)


def window(a, b, start):
    turn = lax.rem(256 - start, 128)
    lane = lax.broadcasted_iota(jnp.int32, a.shape, 1) + start
    return jnp.where((lane >= 0) & (lane < LANES), pltpu.roll(a, turn, 1), pltpu.roll(b, turn, 1))


def core_kernel(
    scalars_in, fa, pa, infos, even_in, odd_in, odd_slots, bands, col_band, tables,
    own, own_low, side, side_low, oa, ob, fb, pb, fw, y2, z, comb, spec, wide, scalars, from_left, from_right, sem,
):
    scalar_copy = pltpu.make_async_copy(scalars_in, scalars, sem)
    scalar_copy.start()
    at_col, col_count = own_index("my")
    leftmost, rightmost = at_col == 0, at_col == col_count - 1
    is_even = lax.rem(at_col, 2) == 0
    from_left[0:88, :] = jnp.where(is_even, odd_in[0:88, :], even_in[0:88, :])
    from_right[0:240, :] = jnp.where(is_even, even_in[0:240, :], odd_in[0:240, :])
    from_left[240:248, :] = jnp.where(is_even, odd_slots[...], even_in[240:248, :])
    from_right[240:248, :] = jnp.where(is_even, even_in[240:248, :], odd_slots[...])
    lane = lax.broadcasted_iota(jnp.int32, (8, LANES), 1)
    lane88 = lax.broadcasted_iota(jnp.int32, (88, LANES), 1)
    lane72 = lax.broadcasted_iota(jnp.int32, (72, LANES), 1)
    lane168 = lax.broadcasted_iota(jnp.int32, (168, LANES), 1)
    for i in range(4):
        rim = pltpu.roll(from_left[0:88, :], 96 - 32 * i, 1)
        fb[88 * i : 88 * i + 88, :] = jnp.where((lane88 >= 96) & jnp.logical_not(leftmost), rim, 0.0)
        near = pltpu.roll(from_right[168:240, :], (128 - 32 * i) % 128, 1)
        pb[72 * i : 72 * i + 72, :] = jnp.where((lane72 < 32) & jnp.logical_not(rightmost), near, 0.0)
    for i in range(2):
        rows = slice(8 + 168 * i, 176 + 168 * i)
        near = from_right[0:168, :] if i == 0 else pltpu.roll(from_right[0:168, :], 64, 1)
        fb[rows, :] = jnp.where((lane168 < 64) & jnp.logical_not(rightmost), near, fb[rows, :])
    is_row = lax.broadcasted_iota(jnp.int32, (8, LANES), 0) < 2
    cand = jnp.full((8, LANES), DEAD, F32)
    tile = 0
    for dc in (0, -1, 1):
        for n, dr in enumerate((0, -1, 1)):
            if dc == 0:
                block = infos[8 * n : 8 * n + 8, :]
            elif dc == -1:
                block = jnp.where(leftmost, DEAD, pltpu.roll(from_left[240:248, :], (128 - 32 * n) % 128, 1))
            else:
                block = jnp.where(rightmost, DEAD, pltpu.roll(from_right[240:248, :], (128 - 32 * n) % 128, 1))
            block = block + jnp.where(is_row, float(TILE_R * dr), float(LANES * dc))
            here = (lane // 16 == tile // 2) & (lax.rem(lane, 4) // 2 == tile % 2)
            cand = jnp.where(here, pltpu.roll(block, 16 * (tile // 2) + 2 * (tile % 2), 1), cand)
            tile += 1
    sub_f = lax.broadcasted_iota(jnp.int32, (128, LANES), 0).astype(F32)
    lane_f = lax.broadcasted_iota(jnp.int32, (128, LANES), 1).astype(F32)
    lane1 = lax.broadcasted_iota(jnp.int32, (1, LANES), 1)
    upright = cand.T
    columns = [jnp.broadcast_to(upright[:, 2 + h : 3 + h], (128, LANES)) for h in range(2)]
    for k in range(SLOTS):
        half = (k % 4) // 2
        row0, col0 = infos[0:1, k : k + 1] - 64.0, infos[2:3, k : k + 1] - 64.0
        p = jnp.where(lax.rem(lane1, 2) == k % 2, cand[half : half + 1] - row0, -1.0)
        at_row = (sub_f == p).astype(F32).astype(BF)
        at_col = jnp.where(lane_f + col0 == columns[half], 64.0, 0.0).astype(BF)
        comb[k // 2, :, 128 * (k % 2) : 128 * (k % 2) + 128] = dot(at_row, at_col).astype(BF)
    for k in range(0, SLOTS, 2):
        t = halves(dot(bands[...], comb[k // 2]), 0)
        for m in range(2):
            hi, lo = split(t[:, 128 * m : 128 * m + 128])
            y2[pl.ds((k + m) * 112, 112), :] = jnp.concatenate([hi, lo], 1)
    scalar_copy.wait()
    for k in range(SLOTS):
        rows = pl.ds(scalars[0, k], 128)
        fw[k] = window(fa[rows, :], fb[rows, :], scalars[1, k] - 32)
    def lane_transform(x):
        hi, lo = split(x)
        return split(halves(dot(jnp.concatenate([hi, lo], 1), tables[:, 0:256]), 1))

    for k in range(SLOTS):
        rows = pl.ds(scalars[0, k], PATCH)
        z[pl.ds(k * PATCH, PATCH), :] = window(pa[rows, :], pb[rows, :], scalars[1, k] - 32)
    win_hi, win_lo = lane_transform(z[...])
    first, n = 8, 112
    while True:
        o = halves(dot(y2[0 : SLOTS * n, :], col_band[...]), 1)
        o = o.reshape(SLOTS, n, 128) * fw[:, first : first + n, :]
        if n == PATCH:
            break
        hi, lo = split(o)
        both = jnp.concatenate([hi, lo], 1)
        m = n - 16
        band_hi, band_lo = bands[0:m, 0:n], bands[112 : 112 + m, 0:n]
        lhs = jnp.concatenate(
            [jnp.concatenate([band_hi, band_hi], 1), jnp.concatenate([band_lo, band_lo], 1)], 0
        )
        for k in range(0, SLOTS, 2):
            t = halves(dot(lhs, jnp.concatenate([both[k], both[k + 1]], 1)), 0)
            for i in range(2):
                hi, lo = split(t[:, 128 * i : 128 * i + 128])
                y2[pl.ds((k + i) * m, m), :] = jnp.concatenate([hi, lo], 1)
        first, n = first + 8, m

    ker_hi, ker_lo = lane_transform(o.reshape(SLOTS * PATCH, 128))
    left_half = lax.broadcasted_iota(jnp.int32, (PATCH, 128), 1) < 64
    sign = jnp.where(left_half, -1.0, 1.0)

    def pair(t):
        a, b = t[:64], pltpu.roll(t[64:], 64, 1) * sign
        return a + b, a - b

    def times(a, b):
        ar, br = pltpu.roll(a, 64, 1), pltpu.roll(b, 64, 1)
        return jnp.where(left_half, a, ar) * b + jnp.where(left_half, -ar, a) * br

    def spectrum(k):
        s = slice(PATCH * k, PATCH * k + PATCH)
        w = jnp.concatenate(
            [jnp.concatenate([ker_hi[s], win_hi[s]], 1), jnp.concatenate([ker_lo[s], win_lo[s]], 1)], 0
        )
        t = halves(dot(tables[:, 768:896], w), 0)
        k1, k2 = pair(t[:, :128])
        w1, w2 = pair(t[:, 128:])
        p1, p2 = times(k1, w1), times(k2, w2)
        return jnp.concatenate([p1 + p2, pltpu.roll((p1 - p2) * sign, 64, 1)], 0)

    for k in range(SLOTS):
        hi, lo = split(spectrum(k))
        spec[pl.ds(k * 128, 128), :] = jnp.concatenate([hi, lo], 1)
    for k in range(SLOTS):
        hi, lo = split(halves(dot(spec[k * 128 : k * 128 + 128, :], tables[:, 256:512]), 1))
        wide[k // 2, :, 128 * (k % 2) : 128 * (k % 2) + 128] = jnp.concatenate([hi, lo], 0)
    oa[...] = jnp.zeros_like(oa)
    ob[...] = jnp.zeros_like(ob)
    lane128 = lax.broadcasted_iota(jnp.int32, (128, LANES), 1)
    for k in range(0, SLOTS, 2):
        t = halves(dot(tables[:, 512:768], wide[k // 2]), 0)
        for m in range(2):
            kk = k + m
            col = scalars[1, kk]
            live = jnp.where(kk < scalars[2, 0], 1.0, 0.0)
            patch = pltpu.roll(t[:, 128 * m : 128 * m + 128] * live, col, 1)
            rows = pl.ds(scalars[0, kk], 128)
            oa[rows, :] += jnp.where(lane128 >= col, patch, 0.0)
            ob[rows, :] += jnp.where(lane128 < col, patch, 0.0)
    at_row, row_count = own_index("mx")
    inner = at_row < row_count - 1
    own[...] = oa[0:TILE_R, :]
    own_low[...] = jnp.where(inner, oa[TILE_R:OUT_R, :], 0.0)
    side_low[...] = jnp.where(inner & jnp.logical_not(rightmost), ob[TILE_R:OUT_R, :], 0.0)
    free = lax.broadcasted_iota(jnp.int32, (64, LANES), 1) >= 96
    for i in range(3):
        rows = slice(64 * i, 64 * i + 64)
        piece = jnp.where(free, pltpu.roll(ob[192:256, :], 96 - 32 * i, 1), ob[rows, :])
        side[rows, :] = jnp.where(rightmost, 0.0, piece)


def peek_kernel(payload, slots):
    slots[...] = payload[payload.shape[0] - 8 :, :]


def add_side_kernel(own, spill, total):
    lane = lax.broadcasted_iota(jnp.int32, (64, LANES), 1)
    last = jnp.zeros((64, LANES), F32)
    for i in range(3):
        rows = slice(64 * i, 64 * i + 64)
        total[rows, :] = own[rows, :] + jnp.where(lane < 96, spill[rows, :], 0.0)
        last = jnp.where(lane // 32 == i, pltpu.roll(spill[rows, :], (32 + 32 * i) % 128, 1), last)
    total[192:256, :] = own[192:256, :] + last


def shape(rows, dtype=F32, cols=LANES):
    return jax.ShapeDtypeStruct((rows, cols), dtype)


def ring(x, axis, by):
    count = lax.axis_size(axis)
    return lax.ppermute(x, axis, [(i, (i + by) % count) for i in range(count)])


def swap(x, axis, odd):
    rows, cols = lax.axis_size("mx"), lax.axis_size("my")
    pairs = []
    for i in range(rows):
        for j in range(cols):
            if axis == "my":
                k = ((j + 1) ^ 1) - 1 if odd else j ^ 1
                to = (i, k) if 0 <= k < cols else (i ^ 1, j)
            else:
                k = ((i + 1) ^ 1) - 1 if odd else i ^ 1
                to = (k, j) if 0 <= k < rows else (i, j ^ 1)
            pairs.append((i * cols + j, to[0] * cols + to[1]))
    return lax.ppermute(x, ("mx", "my"), pairs)


def diagonal(x):
    rows, cols = lax.axis_size("mx"), lax.axis_size("my")
    pairs = []
    for i in range(rows):
        for j in range(cols):
            to = (i + 1, (j + 1) % cols) if i + 1 < rows else (0, j)
            pairs.append((i * cols + j, to[0] * cols + to[1]))
    return lax.ppermute(x, ("mx", "my"), pairs)


def core_call(scalars, fa, pa, infos, even_in, odd_in, odd_slots, bands, col_band, tables):
    return pl.pallas_call(
        core_kernel,
        out_shape=[shape(TILE_R), shape(OUT_R - TILE_R), shape(192), shape(OUT_R - TILE_R)],
        in_specs=[VMEM] * 10,
        out_specs=[VMEM] * 4,
        scratch_shapes=[
            pltpu.VMEM((OUT_R, LANES), F32),
            pltpu.VMEM((OUT_R, LANES), F32),
            pltpu.VMEM((EXT_F, LANES), F32),
            pltpu.VMEM((EXT_P, LANES), F32),
            pltpu.VMEM((SLOTS, 128, LANES), F32),
            pltpu.VMEM((SLOTS * 112, 256), BF),
            pltpu.VMEM((SLOTS * PATCH, LANES), F32),
            pltpu.VMEM((SLOTS // 2, 128, 256), BF),
            pltpu.VMEM((SLOTS * 128, 256), BF),
            pltpu.VMEM((SLOTS // 2, 256, 256), BF),
            pltpu.SMEM((8, LANES), jnp.int32),
            pltpu.VMEM((248, LANES), F32),
            pltpu.VMEM((248, LANES), F32),
            pltpu.SemaphoreType.DMA,
        ],
        compiler_params=pltpu.CompilerParams(vmem_limit_bytes=40 * 2**20),
    )(
        scalars, fa, pa, infos, even_in, odd_in, odd_slots, bands, col_band, tables,
    )


def peek(payload, params):
    return pl.pallas_call(
        peek_kernel,
        out_shape=shape(8),
        in_specs=[VMEM],
        out_specs=VMEM,
        compiler_params=params,
    )(payload)


def per_device(friction, taps_row, taps_col, probe, win_row, win_col, live_count):
    params = pltpu.CompilerParams(vmem_limit_bytes=40 * 2**20)
    row_even_out, row_odd_out, scalars = pl.pallas_call(
        pack_rows_kernel,
        out_shape=[shape(104), shape(104), shape(8, jnp.int32)],
        in_specs=[ANY] * 5,
        out_specs=[VMEM] * 3,
        scratch_shapes=[
            pltpu.VMEM((1, SLOTS), jnp.int32),
            pltpu.VMEM((1, SLOTS), jnp.int32),
            pltpu.VMEM((1, 1), jnp.int32),
            pltpu.SemaphoreType.DMA((6,)),
        ],
        compiler_params=pltpu.CompilerParams(vmem_limit_bytes=55040 * 2**10),
    )(win_row, win_col, live_count, friction, probe)
    row_odd = swap(row_odd_out, "mx", True)
    row_even = swap(row_even_out, "mx", False)
    fa, pa = pl.pallas_call(
        fetch_kernel,
        out_shape=[shape(EXT_F), shape(EXT_P)],
        in_specs=[ANY] * 2,
        out_specs=[VMEM] * 2,
        scratch_shapes=[pltpu.SemaphoreType.DMA((2,))],
        compiler_params=params,
    )(friction, probe)
    bands, col_band, tables = pl.pallas_call(
        bands_kernel,
        out_shape=[shape(224, BF), shape(256, BF, 256), shape(256, BF, 896)],
        in_specs=[SMEM] * 2 + [ANY],
        out_specs=[VMEM] * 3,
        scratch_shapes=[pltpu.SemaphoreType.DMA],
        compiler_params=params,
    )(taps_row, taps_col, jnp.asarray(transform_tables()))
    fa, pa, infos, even_out, odd_out = pl.pallas_call(
        pack_cols_kernel,
        out_shape=[shape(EXT_F), shape(EXT_P), shape(24), shape(248), shape(248)],
        in_specs=[VMEM] * 6,
        out_specs=[VMEM] * 5,
        input_output_aliases={0: 0, 1: 1},
        compiler_params=params,
    )(fa, pa, row_even_out, row_even, row_odd, peek(row_odd, params))
    odd_in = swap(odd_out, "my", True)
    even_in = swap(even_out, "my", False)
    own, own_low, side, side_low = core_call(
        scalars, fa, pa, infos, even_in, odd_in, peek(odd_in, params), bands, col_band, tables
    )
    spill = ring(side, "my", 1)
    corner = diagonal(side_low)
    lower = ring(own_low, "mx", 1)
    total = pl.pallas_call(
        add_side_kernel,
        out_shape=shape(TILE_R),
        in_specs=[VMEM] * 2,
        out_specs=VMEM,
        compiler_params=params,
    )(own, spill)
    below = ((0, TILE_R - corner.shape[0]), (0, 0))
    total = lax.optimization_barrier(total + jnp.pad(corner, below))
    return total + jnp.pad(lower, below)


def solution(mesh):
    placed = (
        P("mx", "my"),
        P(),
        P(),
        P("mx", "my"),
        P("mx", "my", None),
        P("mx", "my", None),
        P("mx", "my"),
    )
    return jax.shard_map(
        per_device, mesh=mesh, in_specs=placed, out_specs=P("mx", "my"), check_vma=False
    )
```
